512 devices in a mesh: lat: 16 (over y_hi, x, core), lon: 16 (over z), batch: 2 (over y_lo).
Axes of the slice: x: 4, y: 4 (y_hi: 2, y_lo: 2; y = y_hi * 2 + y_lo), z: 16, core: 2. Of those that a mesh axis runs over, the one named last changes fastest.
Arguments:
- grid: bfloat16 [512, 720, 1440], P('batch', 'lat', 'lon'), parts along dimension 0, may hold values from -6 to 6
- norm_gain: float32 [256], replicated, may hold values from 0.5 to 1.5
- mlp_in: bfloat16 [256, 512], replicated, may hold values from -0.375 to 0.375
- mlp_out: bfloat16 [512, 256], replicated, may hold values from -0.25 to 0.25
- filter_weight: bfloat16 [512, 256, 256], P(('lat', 'lon')), may hold values from -0.375 to 0.375
Outputs:
- updated: bfloat16 [512, 720, 1440], P(('batch', 'lon'), 'lat'), parts along dimension 0
The draws below stay inside these ranges and needn't reach their ends.
There are 2 independent parts, one for each index of `batch`. The reference program is written for one: setup_inputs(seed, part) draws one part's arguments, and reference() takes and returns one part's arrays. A program takes and returns all parts, laid end to end along the dimension named above; an argument that names none is the same for every part. Nothing has to cross between parts.
All inputs are finite; a program needn't handle non-finite values.
Results may differ from the reference program's by a relative error of at most 0.0095.
Values may be sent and summed in bfloat16 or wider, within the bound.
A program may use at most 128 MiB of HBM per device.

```python
import jax
import jax.numpy as jnp
from jax import lax

C = 256
HID = 512
LAT_DEV = 45
NLAT = 720
NLON = 1440
MODES = 512
N_LAT = 16


def level_of(key, dims, cuts, smallest, high):
    def one(position, shards_of):
        steps = jax.random.uniform(jax.random.fold_in(jax.random.fold_in(key, 6), position), (shards_of,), jnp.float32, smallest / len(cuts), high / len(cuts))
        return jnp.repeat(jnp.exp(steps), dims[position] // shards_of).reshape((-1,) + (1,) * (len(dims) - position - 1))

    level = one(*cuts[0])
    for cut in cuts[1:]:
        level = level * one(*cut)
    return level


def gaussian(stream_key, dims, scale, reach, split=(), held_as=jnp.bfloat16):
    array = scale * jax.random.normal(stream_key, dims, jnp.float32)
    if split:
        array = array * level_of(stream_key, dims, split, -0.22, 0.18)
    return jnp.clip(array, -reach, reach).astype(held_as)


def setup_inputs(seed: int = 0, part: int = 0) -> dict:
    key_list = jax.random.split(jax.random.key(seed), 6)
    part_splits = jax.random.split(jax.random.fold_in(key_list[5], part), 6)
    grid = gaussian(part_splits[0], (C, NLAT, NLON), 1.0, 6.0, ((1, 16), (2, 16)))
    norm_gain = jnp.clip(1.0 + 0.1 * jax.random.normal(key_list[1], (C,), jnp.float32), 0.5, 1.5)
    mlp_in = gaussian(key_list[2], (C, HID), C ** -0.5, 0.375)
    mlp_out = gaussian(key_list[3], (HID, C), HID ** -0.5, 0.25)
    filter_weight = gaussian(key_list[4], (MODES, C, C), C ** -0.5, 0.375, ((0, 256),))
    return {"grid": grid, "norm_gain": norm_gain, "mlp_in": mlp_in, "mlp_out": mlp_out, "filter_weight": filter_weight}


def quadrature(nlat):
    rows = jnp.arange(nlat, dtype=jnp.float32)
    theta = jnp.pi * (rows + 0.5) / nlat
    return (theta, jnp.pi / nlat * jnp.sin(theta))

def legendre(orders, nlat, degrees):
    theta = quadrature(nlat)[0]
    cosine = jnp.cos(theta)
    sine = jnp.sin(theta)
    order = orders.astype(jnp.float32)[:, None]
    degree = jnp.arange(degrees, dtype=jnp.float32)[None, :]
    active = degree > order
    second = degree > order + 1.0
    growth = jnp.sqrt(jnp.where(active, 4.0 * degree * degree - 1.0, 1.0) / jnp.where(active, degree * degree - order * order, 1.0))
    before = degree - 1.0
    damping = jnp.sqrt(jnp.where(second, before * before - order * order, 0.0) / jnp.where(second, 4.0 * before * before - 1.0, 1.0))
    counts = jnp.arange(1, degrees + 1, dtype=jnp.float32)
    ratios = jnp.log((2.0 * counts - 1.0) / (2.0 * counts))
    partial_log = lax.optimization_barrier(jnp.sum(jnp.where(counts[None, :] <= order, ratios[None, :], 0.0), axis=1))
    start_log = order * jnp.log(sine)[None, :] + 0.5 * jnp.log(order + 0.5) + 0.5 * partial_log[:, None]

    def advance(carry, inputs):
        upper, lower, scale_log = carry
        grow, damp, live = inputs
        fresh = grow[:, None] * cosine[None, :] * upper - (grow * damp)[:, None] * lower
        largest = jnp.maximum(jnp.abs(fresh), jnp.abs(upper))
        largest = jnp.where(largest > 0.0, largest, 1.0)
        alive = live[:, None]
        new_upper = jnp.where(alive, fresh / largest, upper)
        new_lower = jnp.where(alive, upper / largest, lower)
        new_log = jnp.where(alive, scale_log + jnp.log(largest), scale_log)
        return ((new_upper, new_lower, new_log), new_upper * jnp.exp(new_log + start_log))
    shape = (orders.shape[0], nlat)
    start = (jnp.ones(shape, jnp.float32), jnp.zeros(shape, jnp.float32), jnp.zeros(shape, jnp.float32))
    values = lax.scan(advance, start, (growth.T, damping.T, active.T))[1]
    values = values.transpose(1, 0, 2)
    return jnp.where((degree >= order)[:, :, None], values, 0.0)

def forward_table(orders, nlon):
    points = jnp.arange(nlon, dtype=jnp.int32)
    phase = points[:, None] * orders[None, :] % nlon
    angle = 2.0 * jnp.pi / nlon * phase.astype(jnp.float32)
    return jnp.stack([jnp.cos(angle), -jnp.sin(angle)], axis=2).astype(jnp.bfloat16)

def inverse_half(orders, nlon):
    points = jnp.arange(nlon // 2, dtype=jnp.int32)
    phase = orders[:, None] * points[None, :] % nlon
    angle = 2.0 * jnp.pi / nlon * phase.astype(jnp.float32)
    amplitude = jnp.where(orders == 0, 1.0, 2.0).astype(jnp.float32)[:, None]
    return jnp.stack([amplitude * jnp.cos(angle), -amplitude * jnp.sin(angle)], axis=1).astype(jnp.bfloat16)

def mlp_rows(fields, norm_gain, mlp_in, mlp_out):
    values = fields.astype(jnp.float32)
    mean = lax.optimization_barrier(jnp.mean(values, axis=0))
    centered = values - mean
    spread = lax.optimization_barrier(jnp.mean(centered * centered, axis=0))
    normed = (centered * lax.rsqrt(spread + 1e-05) * norm_gain[:, None, None]).astype(jnp.bfloat16)
    flat = normed.reshape(normed.shape[0], -1)
    hidden = jax.nn.gelu(jnp.dot(mlp_in.T, flat, preferred_element_type=jnp.float32)).astype(jnp.bfloat16)
    update = jnp.dot(mlp_out.T, hidden, preferred_element_type=jnp.float32)
    return (values + update.reshape(values.shape)).astype(jnp.bfloat16)

def reference(grid, norm_gain, mlp_in, mlp_out, filter_weight):
    bands = grid.reshape(C, N_LAT, LAT_DEV, NLON).transpose(1, 0, 2, 3)
    mixed_bands = lax.map(lambda lat_band: mlp_rows(lat_band, norm_gain, mlp_in, mlp_out), bands)
    mixed = mixed_bands.transpose(1, 0, 2, 3).reshape(C, NLAT, NLON)
    orders = jnp.arange(MODES, dtype=jnp.int32)
    dft_table = forward_table(orders, NLON).reshape(NLON, 2 * MODES)
    spectrum = (jnp.dot(mixed.reshape(C * NLAT, NLON), dft_table, preferred_element_type=jnp.float32) / NLON).astype(jnp.bfloat16)
    fields = spectrum.reshape(C, NLAT, MODES, 2).transpose(2, 3, 0, 1).reshape(MODES, 2 * C, NLAT)
    weights = quadrature(NLAT)[1]

    def mode_block(start):
        orders_here = start + jnp.arange(16, dtype=jnp.int32)
        table = legendre(orders_here, NLAT, MODES)
        analysis_table = (table * weights).astype(jnp.bfloat16)
        synthesis_table = table.astype(jnp.bfloat16)
        block_fields = lax.dynamic_slice_in_dim(fields, start, 16, 0)
        coefficients = jnp.einsum('mlj,mkj->mlk', analysis_table.astype(jnp.float32), block_fields.astype(jnp.float32)).astype(jnp.bfloat16)
        split_parts = coefficients.reshape(16, MODES, 2, C)
        filtered = jnp.einsum('mlrc,lco->mlro', split_parts.astype(jnp.float32), filter_weight.astype(jnp.float32)).astype(jnp.bfloat16)
        merged = filtered.reshape(16, MODES, 2 * C)
        return jnp.einsum('mlj,mlk->mkj', synthesis_table.astype(jnp.float32), merged.astype(jnp.float32)).astype(jnp.bfloat16)
    synthesis = lax.map(mode_block, jnp.arange(0, MODES, 16, dtype=jnp.int32)).reshape(2 * MODES, C * NLAT)
    half_table = inverse_half(orders, NLON)
    parity = jnp.where(orders % 2 == 0, 1.0, -1.0).astype(jnp.bfloat16)[:, None, None]
    inverse_table = jnp.concatenate([half_table, half_table * parity], axis=2).reshape(2 * MODES, NLON)
    spatial = jnp.dot(synthesis.T, inverse_table, preferred_element_type=jnp.float32)
    return (mixed.astype(jnp.float32) + spatial.reshape(C, NLAT, NLON)).astype(jnp.bfloat16)
```

```python
import functools

import jax
import jax.numpy as jnp
from jax import lax
from jax.experimental import pallas as pl
from jax.experimental.pallas import tpu as pltpu
from jax.sharding import PartitionSpec as P

F32 = jnp.float32
BF16 = jnp.bfloat16

CH = 256
HID = 512
JD = 45
JP = 48
ND = 90
NP = 96
NLAT = 720
NLON = 1440
MODES = 512
NA = 16
NZ = 16
JALL = NA * JP
ROWS = 144
LIMIT = 56 * 1024 * 1024


def call(kernel, out_shape, grid, in_specs, out_specs, scratch, flops, moved):
    return pl.pallas_call(
        kernel,
        out_shape=out_shape,
        grid=grid,
        in_specs=in_specs,
        out_specs=out_specs,
        scratch_shapes=scratch,
        cost_estimate=pl.CostEstimate(flops=flops, bytes_accessed=moved, transcendentals=0),
        compiler_params=pltpu.CompilerParams(
            dimension_semantics=("arbitrary",) * len(grid), vmem_limit_bytes=LIMIT
        ),
    )


def swap_blocks(xs):
    block = lax.broadcasted_iota(jnp.int32, xs[0].shape, 1) // 16
    for bit in (1, 2, 4):
        upper = (block & bit) != 0
        new = list(xs)
        for i in range(8):
            if i & bit == 0:
                low, high = xs[i], xs[i | bit]
                new[i] = jnp.where(upper, pltpu.roll(high, 16 * bit, 1), low)
                new[i | bit] = jnp.where(upper, high, pltpu.roll(low, 128 - 16 * bit, 1))
        xs = new
    return xs


def mlp_kernel(x_ref, gain_ref, in_ref, out_w_ref, o_ref, pad_ref, mix_ref):
    g = pl.program_id(0)
    pad_ref[...] = jnp.zeros_like(pad_ref)
    for j in range(8):
        pad_ref[j * NP : j * NP + ND, :] = x_ref[j].astype(F32)
    half = 2 * NP
    for part in range(4):
        rows = slice(part * half, (part + 1) * half)
        x = pad_ref[rows, :]
        mean = jnp.mean(x, axis=1, keepdims=True)
        centered = x - mean
        spread = jnp.mean(centered * centered, axis=1, keepdims=True)
        normed = (centered * lax.rsqrt(spread + 1e-05) * gain_ref[...]).astype(BF16)
        hidden = jnp.dot(normed, in_ref[...], preferred_element_type=F32)
        hidden = jax.nn.gelu(hidden).astype(BF16)
        mixed = x + jnp.dot(hidden, out_w_ref[...], preferred_element_type=F32)
        mix_ref[0, rows, :] = mixed[:, :128]
        mix_ref[1, rows, :] = mixed[:, 128:]
    lane = lax.broadcasted_iota(jnp.int32, (16, 128), 1)
    row = lax.broadcasted_iota(jnp.int32, (16, 128), 0)
    live = lane // 16 < JD - 8 * g

    def place(step, _):
        start = pl.multiple_of(step * 16, 16)
        keep = jnp.logical_and(live, row < ND - start)
        for h in range(2):
            xs = [mix_ref[h, pl.ds(pl.multiple_of(j * NP + start, 16), 16), :] for j in range(8)]
            for z, y in enumerate(swap_blocks(xs)):
                o_ref[h * 8 + z, 0, pl.ds(start, 16), :] = jnp.where(keep, y, 0.0).astype(BF16)
        return 0

    lax.fori_loop(0, NP // 16, place, 0)


def mlp(points, gain, mlp_in, mlp_out):
    return call(
        mlp_kernel,
        jax.ShapeDtypeStruct((NZ, 6, NP, 128), BF16),
        (6,),
        [
            pl.BlockSpec((8, ND, CH), lambda g: (g, 0, 0)),
            pl.BlockSpec((1, CH), lambda g: (0, 0)),
            pl.BlockSpec((CH, HID), lambda g: (0, 0)),
            pl.BlockSpec((HID, CH), lambda g: (0, 0)),
        ],
        pl.BlockSpec((NZ, 1, NP, 128), lambda g: (0, g, 0, 0)),
        [pltpu.VMEM((8 * NP, CH), F32), pltpu.VMEM((2, 8 * NP, 128), F32)],
        4 * 4050 * CH * HID,
        5_000_000,
    )(points, gain, mlp_in, mlp_out)


def dft_kernel(x_ref, table_ref, weight_ref, o_ref, acc_ref, swap_ref):
    both = jnp.concatenate(
        [x_ref[:, gg].reshape(NZ * NP, 128) for gg in range(2)], axis=1
    )
    for part in range(4):
        rows = slice(part * 256, (part + 1) * 256)
        acc = jnp.dot(table_ref[rows, :], both, preferred_element_type=F32)
        acc = acc * weight_ref[0]
        acc_ref[0, rows, :] = acc[:, :128]
        acc_ref[1, rows, :] = acc[:, 128:]

    def place(a, _):
        for gg in range(2):
            xs = [
                acc_ref[gg, pl.ds(pl.multiple_of(a * 64 + mr * 8, 8), 8), :] for mr in range(8)
            ]
            for j, y in enumerate(swap_blocks(xs)):
                swap_ref[pl.ds(gg * 8 + j, 8, stride=16), :] = y
        o_ref[a] = swap_ref[...].astype(BF16).reshape(8, 16, 128)
        return 0

    lax.fori_loop(0, NA, place, 0)


def dft(fields, table, weights):
    return call(
        dft_kernel,
        jax.ShapeDtypeStruct((NA, 8, JP, 128), BF16),
        (3,),
        [
            pl.BlockSpec((NZ, 2, NP, 128), lambda g: (0, g, 0, 0)),
            pl.BlockSpec((2 * MODES, NZ * NP), lambda g: (0, 0)),
            pl.BlockSpec((1, 1, 256), lambda g: (g, 0, 0)),
        ],
        pl.BlockSpec((NA, 8, 16, 128), lambda g: (0, 0, g, 0)),
        [pltpu.VMEM((2, 2 * MODES, 128), F32), pltpu.VMEM((128, 128), F32)],
        2 * 2 * MODES * NZ * NP * JALL,
        7_000_000,
    )(fields, table, weights)


def legendre_kernel(order_ref, cos_ref, log_ref, o_ref, up_ref, low_ref, scale_ref, swap_ref):
    q = pl.program_id(0)
    lb = pl.program_id(1)

    @pl.when(lb == 0)
    def _():
        up_ref[...] = jnp.zeros_like(up_ref)
        low_ref[...] = jnp.zeros_like(low_ref)
        scale_ref[...] = log_ref[0]

    @pl.when(lb >= q)
    def _():
        order = order_ref[0]
        degree = lax.broadcasted_iota(jnp.int32, (8, 128), 1).astype(F32) + (lb * 128).astype(F32)
        active = degree > order
        second = degree > order + 1.0
        grow = jnp.sqrt(
            jnp.where(active, 4.0 * degree * degree - 1.0, 0.0)
            / jnp.where(active, degree * degree - order * order, 1.0)
        )
        before = degree - 1.0
        damp = jnp.sqrt(
            jnp.where(second, before * before - order * order, 0.0)
            / jnp.where(second, 4.0 * before * before - 1.0, 1.0)
        )
        damp = grow * damp
        first = jnp.where(degree == order, 1.0, 0.0)

        def group(i, _):
            shift = lax.rem(128 - 16 * i, 128)
            grow_i = pltpu.roll(grow, shift, 1)
            damp_i = pltpu.roll(damp, shift, 1)
            first_i = pltpu.roll(first, shift, 1)
            for k in range(6):
                cols = slice(k * 128, (k + 1) * 128)
                up = up_ref[:, cols]
                low = low_ref[:, cols]
                scale_log = scale_ref[:, cols]
                root = jnp.exp(0.5 * scale_log)
                cosine = cos_ref[:, cols]
                for s in range(16):
                    a = jnp.broadcast_to(grow_i[:, s : s + 1], (8, 128))
                    b = jnp.broadcast_to(damp_i[:, s : s + 1], (8, 128))
                    e = jnp.broadcast_to(first_i[:, s : s + 1], (8, 128))
                    fresh = a * (cosine * up) - b * low + e
                    low = up
                    up = fresh
                    swap_ref[k, s * 8 : s * 8 + 8, :] = fresh * root * root
                largest = jnp.maximum(jnp.abs(up), jnp.abs(low))
                largest = jnp.where(largest > 0.0, largest, 1.0)
                up_ref[:, cols] = up / largest
                low_ref[:, cols] = low / largest
                scale_ref[:, cols] = scale_log + jnp.log(largest)
            start = pl.multiple_of(i * 16, 16)
            for m in range(8):
                for k in range(6):
                    o_ref[0, 0, m, pl.ds(start, 16), k * 128 : (k + 1) * 128] = swap_ref[
                        k, pl.ds(m, 16, stride=8), :
                    ].astype(BF16)
            return 0

        lax.fori_loop(0, 8, group, 0)


def legendre(orders, cosine, start_log):
    return call(
        legendre_kernel,
        jax.ShapeDtypeStruct((4, 4, 8, 128, JALL), BF16),
        (4, 4),
        [
            pl.BlockSpec((1, 8, 128), lambda q, b: (q, 0, 0)),
            pl.BlockSpec((8, JALL), lambda q, b: (0, 0)),
            pl.BlockSpec((1, 8, JALL), lambda q, b: (q, 0, 0)),
        ],
        pl.BlockSpec((1, 1, 8, 128, JALL), lambda q, b: (q, jnp.maximum(b, q), 0, 0, 0)),
        [
            pltpu.VMEM((8, JALL), F32),
            pltpu.VMEM((8, JALL), F32),
            pltpu.VMEM((8, JALL), F32),
            pltpu.VMEM((6, 128, 128), F32),
        ],
        200_000_000,
        16_000_000,
    )(orders, cosine, start_log)


def analysis_kernel(table_ref, x_ref, o_ref, all_ref):
    q = pl.program_id(0)
    lb = pl.program_id(1)
    block = lax.broadcasted_iota(jnp.int32, (128, 128), 1) // 32

    @pl.when(lb >= q)
    def _():
        for i in range(2):
            x = x_ref[:, i].reshape(JALL, 128)
            total = jnp.zeros((128, 128), F32)
            for m in range(4):
                part = jnp.dot(table_ref[0, 0, i * 4 + m], x, preferred_element_type=F32)
                total = jnp.where(block == m, part, total)
            all_ref[2 * q + i, pl.ds(pl.multiple_of(lb * 128, 128), 128), :] = total

    @pl.when(jnp.logical_and(q == 3, lb == 3))
    def _():
        row = lax.broadcasted_iota(jnp.int32, (16, 128), 0)

        def place(z, _):
            for t in range(2):
                parts = [all_ref[g, pl.ds(2 * z + t, 16, stride=32), :] for g in range(8)]
                o_ref[z, t * 16 : t * 16 + 16, :] = parts[0].astype(BF16)
                for s in range(1, 4):
                    both = jnp.where(row < 2 * s, pltpu.roll(parts[8 - s], 2 * s, 0), parts[s])
                    o_ref[z, s * 32 + t * 16 : s * 32 + t * 16 + 16, :] = both.astype(BF16)
                if t == 0:
                    kept = parts[4][8:]
                else:
                    o_ref[z, 128:144, :] = jnp.concatenate([kept, parts[4][8:]], axis=0).astype(
                        BF16
                    )
            return 0

        lax.fori_loop(0, NZ, place, 0)


def analysis(table, fields):
    return call(
        analysis_kernel,
        jax.ShapeDtypeStruct((NZ, ROWS, 128), BF16),
        (4, 4),
        [
            pl.BlockSpec((1, 1, 8, 128, JALL), lambda q, b: (q, jnp.maximum(b, q), 0, 0, 0)),
            pl.BlockSpec((NA, 2, JP, 128), lambda q, b: (0, q, 0, 0)),
        ],
        pl.BlockSpec((NZ, ROWS, 128), lambda q, b: (0, 0, 0)),
        [pltpu.VMEM((8, MODES, 128), F32)],
        2 * 80 * 128 * JALL * 128,
        18_000_000,
    )(table, fields)


def filter_row(mg, a, t):
    if mg < 4:
        return 32 * mg + 16 * t + a
    if mg == 4:
        return 128 + 8 * t + a - 8
    return 32 * (8 - mg) + 16 * t + a - 2 * mg


def filter_kernel(x_ref, w_ref, o_ref, in_ref, out_ref):
    def gather(step, _):
        start = pl.multiple_of(step * 16, 16)
        for h in range(2):
            xs = [x_ref[h * 8 + z, pl.ds(start, 16), :].astype(F32) for z in range(8)]
            for mr, y in enumerate(swap_blocks(xs)):
                in_ref[h, pl.ds(start * 8 + mr, 16, stride=8), :] = y
        return 0

    lax.fori_loop(0, ROWS // 16, gather, 0)
    for a in range(16):
        for t in range(2):
            rows = [8 * filter_row(mg, a, t) for mg in range(a // 2 + 1)]
            x = jnp.concatenate(
                [
                    jnp.concatenate([in_ref[h, r : r + 8, :] for r in rows], axis=0)
                    for h in range(2)
                ],
                axis=1,
            ).astype(BF16)
            y = jnp.dot(x, w_ref[a, t], preferred_element_type=F32)
            for i, r in enumerate(rows):
                for h in range(2):
                    out_ref[h, r : r + 8, :] = y[i * 8 : i * 8 + 8, h * 128 : h * 128 + 128]

    def scatter(step, _):
        start = pl.multiple_of(step * 16, 16)
        for h in range(2):
            xs = [out_ref[h, pl.ds(start * 8 + mr, 16, stride=8), :] for mr in range(8)]
            for z, y in enumerate(swap_blocks(xs)):
                o_ref[h * 8 + z, pl.ds(start, 16), :] = y.astype(BF16)
        return 0

    lax.fori_loop(0, ROWS // 16, scatter, 0)


def channel_filter(coefficients, weight):
    whole = pl.BlockSpec((NZ, ROWS, 128), lambda i: (0, 0, 0))
    return call(
        filter_kernel,
        jax.ShapeDtypeStruct((NZ, ROWS, 128), BF16),
        (1,),
        [whole, pl.BlockSpec((NA, 2, CH, CH), lambda i: (0, 0, 0, 0))],
        whole,
        [pltpu.VMEM((2, ROWS * 8, 128), F32), pltpu.VMEM((2, ROWS * 8, 128), F32)],
        2 * ROWS * 8 * CH * CH,
        6_000_000,
    )(coefficients, weight)


def synthesis_kernel(table_ref, x_ref, o_ref, all_ref, acc_ref):
    q = pl.program_id(0)
    lb = pl.program_id(1)

    @pl.when(jnp.logical_and(q == 0, lb == 0))
    def _():
        row = lax.broadcasted_iota(jnp.int32, (16, 128), 0)

        def place(z, _):
            last = x_ref[z, 128:144, :].astype(F32)
            for t in range(2):
                where = pl.ds(2 * z + t, 16, stride=32)
                all_ref[0, where, :] = x_ref[z, t * 16 : t * 16 + 16, :].astype(F32)
                for s in range(1, 4):
                    x = x_ref[z, s * 32 + t * 16 : s * 32 + t * 16 + 16, :].astype(F32)
                    all_ref[s, where, :] = jnp.where(row >= 2 * s, x, 0.0)
                    all_ref[8 - s, where, :] = jnp.where(
                        row >= 16 - 2 * s, pltpu.roll(x, 16 - 2 * s, 0), 0.0
                    )
                all_ref[4, where, :] = jnp.concatenate(
                    [jnp.zeros((8, 128), F32), last[t * 8 : t * 8 + 8]], axis=0
                )
            return 0

        lax.fori_loop(0, NZ, place, 0)

    @pl.when(lb == 0)
    def _():
        acc_ref[...] = jnp.zeros_like(acc_ref)

    @pl.when(lb >= q)
    def _():
        for i in range(2):
            x = all_ref[2 * q + i, pl.ds(pl.multiple_of(lb * 128, 128), 128), :]
            x = x.T.astype(BF16)
            for m in range(4):
                rows = slice(m * 32, m * 32 + 32)
                acc_ref[i, rows, :] += jnp.dot(
                    x[rows], table_ref[0, 0, i * 4 + m], preferred_element_type=F32
                )

    @pl.when(lb == 3)
    def _():
        for i in range(2):
            o_ref[:, i] = acc_ref[i].T.astype(BF16).reshape(NA, JP, 128)


def synthesis(table, filtered):
    return call(
        synthesis_kernel,
        jax.ShapeDtypeStruct((NA, 8, JP, 128), BF16),
        (4, 4),
        [
            pl.BlockSpec((1, 1, 8, 128, JALL), lambda q, b: (q, jnp.maximum(b, q), 0, 0, 0)),
            pl.BlockSpec((NZ, ROWS, 128), lambda q, b: (0, 0, 0)),
        ],
        pl.BlockSpec((NA, 2, JP, 128), lambda q, b: (0, q, 0, 0)),
        [pltpu.VMEM((8, MODES, 128), F32), pltpu.VMEM((2, 128, JALL), F32)],
        2 * 80 * 128 * JALL * 32,
        18_000_000,
    )(table, filtered)


def inverse_kernel(u_ref, x_ref, table_ref, o_ref, wide_ref, rows_ref, lhs_ref, acc_ref):
    def place(a, _):
        wide_ref[...] = u_ref[a].reshape(128, 128).astype(F32)
        for gg in range(2):
            xs = [wide_ref[pl.ds(gg * 8 + j, 8, stride=16), :] for j in range(8)]
            for mr, y in enumerate(swap_blocks(xs)):
                rows_ref[gg, pl.ds(pl.multiple_of(a * 64 + mr * 8, 8), 8), :] = y
        return 0

    lax.fori_loop(0, NA, place, 0)
    for gg in range(2):
        for k in range(8):
            cols = slice(k * 128, (k + 1) * 128)
            lhs_ref[gg * 128 : gg * 128 + 128, cols] = rows_ref[gg, cols, :].T.astype(BF16)
    for part in range(2):
        rows = slice(part * 128, part * 128 + 128)
        acc_ref[rows, :NLON] = jnp.dot(lhs_ref[rows, :], table_ref[...], preferred_element_type=F32)
    row = lax.broadcasted_iota(jnp.int32, (NP, 256), 0)
    lane = lax.broadcasted_iota(jnp.int32, (NP, 256), 1)
    for z in range(NZ):
        begin = ND * z // 128 * 128
        pick = jnp.logical_and(lane == row + (ND * z - begin), row < ND)
        pick = jnp.where(pick, 1.0, 0.0).astype(BF16)
        for gg in range(2):
            x = x_ref[z, gg].astype(F32).T.astype(BF16)
            acc_ref[gg * 128 : gg * 128 + 128, begin : begin + 256] += jnp.dot(
                x, pick, preferred_element_type=F32
            )
    o_ref[...] = acc_ref[:, :NLON].astype(BF16).reshape(16, 16, NLON)


def inverse(waves, fields, table):
    return call(
        inverse_kernel,
        jax.ShapeDtypeStruct((JD, 16, NLON), BF16),
        (3,),
        [
            pl.BlockSpec((NA, 8, 16, 128), lambda g: (0, 0, g, 0)),
            pl.BlockSpec((NZ, 2, NP, 128), lambda g: (0, g, 0, 0)),
            pl.BlockSpec((2 * MODES, NLON), lambda g: (0, 0)),
        ],
        pl.BlockSpec((16, 16, NLON), lambda g: (g, 0, 0)),
        [
            pltpu.VMEM((128, 128), F32),
            pltpu.VMEM((2, 2 * MODES, 128), F32),
            pltpu.VMEM((256, 2 * MODES), BF16),
            pltpu.VMEM((256, 1536), F32),
        ],
        2 * 2 * MODES * NLON * JALL,
        10_000_000,
    )(waves, fields, table)


def wave_rows():
    row = jnp.arange(2 * MODES, dtype=jnp.int32)
    a, mr, mg = row // 64, row // 8 % 8, row % 8
    return 64 * mg + 32 * (mr // 4) + 2 * a + mr // 2 % 2, mr % 2


def waves(orders, part, points):
    phase = (orders[:, None] * points[None, :] + 360 * part[:, None]) % NLON
    return jnp.cos(2.0 * jnp.pi / NLON * phase.astype(F32))


def forward_table():
    orders, part = wave_rows()
    column = jnp.arange(NZ * NP, dtype=jnp.int32)
    n = column % NP
    table = waves(orders, part, column // NP * ND + n)
    return jnp.where(n[None, :] < ND, table, 0.0).astype(BF16)


def inverse_table():
    orders, part = wave_rows()
    table = waves(orders, part, jnp.arange(NLON, dtype=jnp.int32))
    amplitude = jnp.where(orders == 0, 1.0, 2.0).astype(F32)
    return (table * amplitude[:, None]).astype(BF16)


def legendre_inputs(lat_index):
    slot = jnp.arange(32, dtype=jnp.int32)
    orders = (32 * (slot // 2) + 2 * lat_index + slot % 2).astype(F32)
    column = jnp.arange(JALL, dtype=jnp.int32)
    local = column % JP
    theta = jnp.pi * ((column // JP * JD + local).astype(F32) + 0.5) / NLAT
    real = local < JD
    cosine = jnp.where(real, jnp.cos(theta), 0.0)
    log_sine = jnp.log(jnp.where(real, jnp.sin(theta), 1.0))
    counts = jnp.arange(1, MODES + 1, dtype=F32)
    ratios = jnp.log((2.0 * counts - 1.0) / (2.0 * counts))
    partial_log = jnp.sum(jnp.where(counts[None, :] <= orders[:, None], ratios[None, :], 0.0), axis=1)
    start_log = (
        orders[:, None] * log_sine[None, :]
        + 0.5 * jnp.log(orders + 0.5)[:, None]
        + 0.5 * partial_log[:, None]
    )
    start_log = jnp.where(real[None, :], start_log, -1e9)
    return (
        jnp.broadcast_to(orders.reshape(4, 8, 1), (4, 8, 128)),
        jnp.broadcast_to(cosine[None, :], (8, JALL)),
        start_log.reshape(4, 8, JALL),
    )


def spectrum_weights(lat_index):
    lane = jnp.arange(6 * 128, dtype=jnp.int32)
    local = lane // 16
    theta = jnp.pi * ((lat_index * JD + local).astype(F32) + 0.5) / NLAT
    weights = jnp.pi / NLAT * jnp.sin(theta) / NLON
    return jnp.where(local < JD, weights, 0.0).reshape(3, 1, 256)


def exchange(x, axis):
    return lax.all_to_all(x, axis, split_axis=0, concat_axis=0, tiled=True)


def on_device(grid, norm_gain, mlp_in, mlp_out, filter_weight):
    lat_index = lax.axis_index("lat")
    points = grid.transpose(1, 2, 0)
    mixed = mlp(points, norm_gain.reshape(1, CH), mlp_in, mlp_out)
    weight = lax.all_gather(filter_weight, "lat")
    rows = exchange(mixed, "lon")
    table = legendre(*legendre_inputs(lat_index))
    spectrum = dft(rows, forward_table(), spectrum_weights(lat_index))
    coefficients = analysis(table, exchange(spectrum, "lat"))
    filtered = channel_filter(exchange(coefficients, "lon"), weight)
    synthesized = synthesis(table, exchange(filtered, "lon"))
    updated = inverse(exchange(synthesized, "lat"), rows, inverse_table())
    return updated.transpose(1, 0, 2)


def solution(mesh):
    return jax.shard_map(
        on_device,
        mesh=mesh,
        in_specs=(P("batch", "lat", "lon"), P(), P(), P(), P(("lat", "lon"), None, None)),
        out_specs=P(("batch", "lon"), "lat", None),
        check_vma=False,
    )
```

```python
import functools

import jax
import jax.numpy as jnp
from jax import lax
from jax.experimental import pallas as pl
from jax.experimental.pallas import tpu as pltpu
from jax.sharding import PartitionSpec as P

F32 = jnp.float32
BF16 = jnp.bfloat16

CH = 256
HID = 512
JD = 45
JP = 48
ND = 90
NP = 96
NLAT = 720
NLON = 1440
MODES = 512
NA = 16
NZ = 16
JH = NA * JP // 2
LAST = JD - 1
KB = 2 * MODES
ROWS = 144
LIMIT = 56 * 1024 * 1024
MESH = pl.DeviceIdType.MESH
OTHERS = (8, 7, 9, 6, 10, 5, 11, 4, 12, 3, 13, 2, 14, 1, 15)
PLACE = (0, 1, 7, 2, 3, 4, 5, 6)


def call(kernel, out_shape, grid, in_specs, out_specs, scratch, flops, moved):
    return pl.pallas_call(
        kernel,
        out_shape=out_shape,
        grid=grid,
        in_specs=in_specs,
        out_specs=out_specs,
        scratch_shapes=scratch,
        cost_estimate=pl.CostEstimate(flops=flops, bytes_accessed=moved, transcendentals=0),
        compiler_params=pltpu.CompilerParams(
            dimension_semantics=("arbitrary",) * len(grid), vmem_limit_bytes=LIMIT
        ),
    )


def swap_blocks(xs):
    block = lax.broadcasted_iota(jnp.int32, xs[0].shape, 1) // 16
    for bit in (1, 2, 4):
        upper = (block & bit) != 0
        new = list(xs)
        for i in range(8):
            if i & bit == 0:
                low, high = xs[i], xs[i | bit]
                new[i] = jnp.where(upper, pltpu.roll(high, 16 * bit, 1), low)
                new[i | bit] = jnp.where(upper, high, pltpu.roll(low, 128 - 16 * bit, 1))
        xs = new
    return xs


def greet(axes):
    barrier = pltpu.get_barrier_semaphore()
    for axis in axes:
        me = lax.axis_index(axis)
        for d in range(1, 16):
            pl.semaphore_signal(
                barrier, inc=1, device_id={axis: lax.rem(me + d, 16)}, device_id_type=MESH
            )
    pl.semaphore_wait(barrier, 15 * len(axes))


def to_peer(axis, d, src, dst, send, recv):
    peer = lax.rem(lax.axis_index(axis) + d, 16)
    return pltpu.make_async_remote_copy(
        src_ref=src(peer),
        dst_ref=dst,
        send_sem=send,
        recv_sem=recv,
        device_id={axis: peer},
        device_id_type=MESH,
    )


def band_row(jj):
    jj = jnp.minimum(jj, LAST)
    return jnp.where(lax.axis_index("lat") >= 8, LAST - jj, jj)


def mlp_chunk(g, x_ref, gain_ref, in_ref, out_w_ref, o_ref, pad_ref, mix_ref):
    for j in range(8):
        pad_ref[j * NP : j * NP + ND, :] = x_ref[band_row(8 * g + j)].astype(F32)
    half = 2 * NP
    for part in range(4):
        rows = slice(part * half, (part + 1) * half)
        x = pad_ref[rows, :]
        mean = jnp.mean(x, axis=1, keepdims=True)
        centered = x - mean
        spread = jnp.mean(centered * centered, axis=1, keepdims=True)
        normed = (centered * lax.rsqrt(spread + 1e-05) * gain_ref[...]).astype(BF16)
        hidden = jnp.dot(normed, in_ref[...], preferred_element_type=F32)
        hidden = jax.nn.gelu(hidden).astype(BF16)
        mixed = x + jnp.dot(hidden, out_w_ref[...], preferred_element_type=F32)
        mix_ref[0, rows, :] = mixed[:, :128]
        mix_ref[1, rows, :] = mixed[:, 128:]
    lane = lax.broadcasted_iota(jnp.int32, (16, 128), 1)
    row = lax.broadcasted_iota(jnp.int32, (16, 128), 0)
    live = lane // 16 < JD - 8 * g

    def place(step, _):
        start = pl.multiple_of(step * 16, 16)
        keep = jnp.logical_and(live, row < ND - start)
        for h in range(2):
            xs = [mix_ref[h, pl.ds(pl.multiple_of(j * NP + start, 16), 16), :] for j in range(8)]
            for z, y in enumerate(swap_blocks(xs)):
                o_ref[g, h * 8 + z, pl.ds(start, 16), :] = jnp.where(keep, y, 0.0).astype(BF16)
        return 0

    lax.fori_loop(0, NP // 16, place, 0)


def wave_table(basis_ref, o_ref, halve):
    width = o_ref.shape[1]
    group_cos, group_sin = basis_ref[4, :, :width], basis_ref[5, :, :width]
    row = lax.broadcasted_iota(jnp.int32, (8, width), 0)

    def step(high, _):
        high_cos = basis_ref[2, pl.ds(high, 1), :width]
        high_sin = basis_ref[3, pl.ds(high, 1), :width]
        for low in range(8):
            low_cos = basis_ref[0, low : low + 1, :width]
            low_sin = basis_ref[1, low : low + 1, :width]
            c = high_cos * low_cos - high_sin * low_sin
            s = high_sin * low_cos + high_cos * low_sin
            real = group_cos * c - group_sin * s
            imag = -(group_sin * c + group_cos * s)
            if halve and low == 0:
                real = jnp.where(jnp.logical_and(high == 0, row == 0), 0.5 * real, real)
            offset = 8 * high + low
            start = offset // 2 % 16 * 64 + offset // 32 * 32 + low % 2 * 16
            o_ref[pl.ds(pl.multiple_of(start, 16), 16), :] = jnp.concatenate(
                [real, imag], axis=0
            ).astype(BF16)
        return 0

    lax.fori_loop(0, 8, step, 0)


def wave_basis(points, scale, order):
    count = jnp.arange(8, dtype=jnp.int32)
    multiple = jnp.stack([count, 8 * count, 64 * jnp.array(order, jnp.int32)])
    phase = multiple[:, :, None] * points[None, None, :] % NLON
    angle = 2.0 * jnp.pi / NLON * phase.astype(F32)
    factor = jnp.stack([jnp.ones_like(scale), jnp.ones_like(scale), scale])[:, None, :]
    return jnp.stack([jnp.cos(angle) * factor, jnp.sin(angle) * factor], axis=1).reshape(
        6, 8, points.shape[0]
    )


def forward_basis():
    column = jnp.arange(NZ * NP, dtype=jnp.int32)
    n = column % NP
    return wave_basis(column // NP * ND + n, jnp.where(n < ND, 1.0, 0.0), tuple(range(8)))


def inverse_basis():
    return wave_basis(jnp.arange(NLON, dtype=jnp.int32), jnp.full((NLON,), 2.0, F32), PLACE)


def dft_pair(x_ref, gp, table_ref, weight_ref, o_ref, acc_ref, swap_ref):
    both = jnp.concatenate(
        [x_ref[2 * gp + gg].reshape(NZ * NP, 128) for gg in range(2)], axis=1
    )
    for part in range(4):
        rows = slice(part * 256, (part + 1) * 256)
        acc = jnp.dot(table_ref[rows, :], both, preferred_element_type=F32)
        acc = acc * weight_ref[gp]
        acc_ref[0, rows, :] = acc[:, :128]
        acc_ref[1, rows, :] = acc[:, 128:]

    def place(a, _):
        for gg in range(2):
            xs = [
                acc_ref[gg, pl.ds(pl.multiple_of(a * 64 + mr * 8, 8), 8), :] for mr in range(8)
            ]
            for j, y in enumerate(swap_blocks(xs)):
                swap_ref[pl.ds(gg * 8 + j, 8, stride=16), :] = y
        o_ref[gp, a] = swap_ref[...].astype(BF16).reshape(8, 16, 128)
        return 0

    lax.fori_loop(0, NA, place, 0)


def legendre_group(q, i, order_ref, cos_ref, o_ref, up_ref, low_ref, scale_ref, swap_ref):
    order = order_ref[q]
    degree = lax.broadcasted_iota(jnp.int32, (8, 128), 1) + 16 * i
    degree = degree.astype(F32)
    active = degree > order
    second = degree > order + 1.0
    grow = jnp.sqrt(
        jnp.where(active, 4.0 * degree * degree - 1.0, 0.0)
        / jnp.where(active, degree * degree - order * order, 1.0)
    )
    before = degree - 1.0
    damp = grow * jnp.sqrt(
        jnp.where(second, before * before - order * order, 0.0)
        / jnp.where(second, 4.0 * before * before - 1.0, 1.0)
    )
    first = jnp.where(degree == order, 1.0, 0.0)
    up, low, scale_log = up_ref[q], low_ref[q], scale_ref[q]
    root = jnp.exp(0.5 * scale_log)
    cosine = cos_ref[...]
    for s in range(16):
        a = jnp.broadcast_to(grow[:, s : s + 1], (8, JH))
        b = jnp.broadcast_to(damp[:, s : s + 1], (8, JH))
        e = jnp.broadcast_to(first[:, s : s + 1], (8, JH))
        fresh = a * (cosine * up) - b * low + e
        low = up
        up = fresh
        value = fresh * root * root
        for k in range(3):
            swap_ref[q, k, s * 8 : s * 8 + 8, :] = value[:, k * 128 : k * 128 + 128]
    largest = jnp.maximum(jnp.abs(up), jnp.abs(low))
    largest = jnp.where(largest > 0.0, largest, 1.0)
    up_ref[q] = up / largest
    low_ref[q] = low / largest
    scale_ref[q] = scale_log + jnp.log(largest)
    start = pl.multiple_of(i * 16, 16)
    for m in range(8):
        for k in range(3):
            o_ref[8 * q + m, pl.ds(start, 16), k * 128 : k * 128 + 128] = swap_ref[
                q, k, pl.ds(m, 16, stride=8), :
            ].astype(BF16)


def legendre(order_ref, cos_ref, log_ref, o_ref, up_ref, low_ref, scale_ref, swap_ref):
    up_ref[...] = jnp.zeros_like(up_ref)
    low_ref[...] = jnp.zeros_like(low_ref)
    scale_ref[...] = log_ref[...]
    for stage in range(4):

        def step(i, _, stage=stage):
            for q in range(stage + 1):
                legendre_group(
                    q, i, order_ref, cos_ref, o_ref, up_ref, low_ref, scale_ref, swap_ref
                )
            return 0

        lax.fori_loop(8 * stage, 8 * stage + 8, step, 0)


def forward_kernel(
    x_ref,
    gain_ref,
    in_ref,
    out_w_ref,
    basis_ref,
    weight_ref,
    order_ref,
    cos_ref,
    log_ref,
    rows_ref,
    spectrum_ref,
    legendre_ref,
    pad_ref,
    mix_ref,
    out_rows,
    got_rows,
    table_ref,
    acc_ref,
    swap_ref,
    out_spectrum,
    table_l,
    up_ref,
    low_ref,
    scale_ref,
    swap_l,
    z_send,
    z_recv,
    a_send,
    a_recv,
    own,
):
    lat = lax.axis_index("lat")
    lon = lax.axis_index("lon")

    def row_copy(g, d):
        return to_peer(
            "lon",
            d,
            lambda peer: out_rows.at[g, peer],
            got_rows.at[g, lon],
            z_send.at[g, d],
            z_recv.at[g, d],
        )

    def spectrum_copy(gp, d):
        return to_peer(
            "lat",
            d,
            lambda peer: out_spectrum.at[gp, peer],
            spectrum_ref.at[gp, lat],
            a_send.at[gp, d],
            a_recv.at[gp, d],
        )

    def own_row(g):
        return pltpu.make_async_copy(out_rows.at[g, lon], got_rows.at[g, lon], own.at[0, g])

    def own_spectrum(gp):
        return pltpu.make_async_copy(
            out_spectrum.at[gp, lat], spectrum_ref.at[gp, lat], own.at[1, gp]
        )

    def keep_rows(gp):
        pair = pl.ds(2 * gp, 2)
        return pltpu.make_async_copy(got_rows.at[pair], rows_ref.at[pair], own.at[2, gp])

    def keep_table(q):
        part = (pl.ds(8 * q, 8), pl.ds(128 * q, MODES - 128 * q))
        return pltpu.make_async_copy(table_l.at[part], legendre_ref.at[part], own.at[3, q])

    greet(("lat", "lon"))

    def mlp_step(g, _):
        mlp_chunk(g, x_ref, gain_ref, in_ref, out_w_ref, out_rows, pad_ref, mix_ref)
        for d in OTHERS:
            row_copy(g, d).start()
        own_row(g).start()
        return 0

    pad_ref[...] = jnp.zeros_like(pad_ref)
    lax.fori_loop(0, 6, mlp_step, 0)
    wave_table(basis_ref, table_ref, False)
    legendre(order_ref, cos_ref, log_ref, table_l, up_ref, low_ref, scale_ref, swap_l)
    for q in range(4):
        keep_table(q).start()

    def dft_step(gp, _):
        for gg in range(2):
            own_row(2 * gp + gg).wait()
            for d in OTHERS:
                row_copy(2 * gp + gg, d).wait_recv()
        keep_rows(gp).start()
        dft_pair(got_rows, gp, table_ref, weight_ref, out_spectrum, acc_ref, swap_ref)
        for d in OTHERS:
            spectrum_copy(gp, d).start()
        own_spectrum(gp).start()
        return 0

    lax.fori_loop(0, 3, dft_step, 0)
    for q in range(4):
        keep_table(q).wait()

    def finish(gp, _):
        for gg in range(2):
            for d in OTHERS:
                row_copy(2 * gp + gg, d).wait_send()
        keep_rows(gp).wait()
        own_spectrum(gp).wait()
        for d in OTHERS:
            spectrum_copy(gp, d).wait()
        return 0

    lax.fori_loop(0, 3, finish, 0)


VM = pl.BlockSpec(memory_space=pltpu.VMEM)
ANY = pl.BlockSpec(memory_space=pl.ANY)


def forward(*operands):
    return pl.pallas_call(
        forward_kernel,
        out_shape=(
            jax.ShapeDtypeStruct((6, NZ, NP, 128), BF16),
            jax.ShapeDtypeStruct((3, NA, 8, 16, 128), BF16),
            jax.ShapeDtypeStruct((32, MODES, JH), BF16),
        ),
        in_specs=[VM] * len(operands),
        out_specs=(ANY, ANY, ANY),
        scratch_shapes=[
            pltpu.VMEM((8 * NP, CH), F32),
            pltpu.VMEM((2, 8 * NP, 128), F32),
            pltpu.VMEM((6, NZ, NP, 128), BF16),
            pltpu.VMEM((6, NZ, NP, 128), BF16),
            pltpu.VMEM((KB, NZ * NP), BF16),
            pltpu.VMEM((2, KB, 128), F32),
            pltpu.VMEM((128, 128), F32),
            pltpu.VMEM((3, NA, 8, 16, 128), BF16),
            pltpu.VMEM((32, MODES, JH), BF16),
            pltpu.VMEM((4, 8, JH), F32),
            pltpu.VMEM((4, 8, JH), F32),
            pltpu.VMEM((4, 8, JH), F32),
            pltpu.VMEM((4, 3, 128, 128), F32),
            pltpu.SemaphoreType.DMA((6, 16)),
            pltpu.SemaphoreType.DMA((6, 16)),
            pltpu.SemaphoreType.DMA((3, 16)),
            pltpu.SemaphoreType.DMA((3, 16)),
            pltpu.SemaphoreType.DMA((4, 6)),
        ],
        cost_estimate=pl.CostEstimate(
            flops=8_000_000_000, bytes_accessed=30_000_000, transcendentals=0
        ),
        compiler_params=pltpu.CompilerParams(
            collective_id=1, has_side_effects=True, vmem_limit_bytes=LIMIT
        ),
    )(*operands)


def analyse(mg, x_ref, table, all_ref):
    north, south = [], []
    for gp in range(3):
        north.append(x_ref[gp, :8, mg].reshape(128, 128).astype(F32))
        south.append(jnp.concatenate([x_ref[gp, 15 - a, mg] for a in range(8)], axis=0).astype(F32))
    north = jnp.concatenate(north, axis=0)
    south = jnp.concatenate(south, axis=0)
    both = jnp.concatenate([north + south, north - south], axis=1).astype(BF16)
    block = lax.broadcasted_iota(jnp.int32, (128, 128), 1) // 32
    odd = lax.broadcasted_iota(jnp.int32, (128, 128), 0) % 2 == 1
    for lb in range(mg // 2, 4):
        rows = slice(lb * 128, lb * 128 + 128)
        total = jnp.zeros((128, 128), F32)
        for m in range(4):
            part = jnp.dot(table(m, rows), both, preferred_element_type=F32)
            first, second = part[:, :128], part[:, 128:]
            if m % 2:
                first, second = second, first
            total = jnp.where(block == m, jnp.where(odd, second, first), total)
        all_ref[mg, rows, :] = total


def analysis_rows(z, all_ref, o_ref):
    row = lax.broadcasted_iota(jnp.int32, (16, 128), 0)
    kept = []
    for t in range(2):
        parts = [all_ref[g, pl.ds(2 * z + t, 16, stride=32), :] for g in range(8)]
        o_ref[z, t * 16 : t * 16 + 16, :] = parts[0].astype(BF16)
        for s in range(1, 4):
            both = jnp.where(row < 2 * s, pltpu.roll(parts[8 - s], 2 * s, 0), parts[s])
            o_ref[z, s * 32 + t * 16 : s * 32 + t * 16 + 16, :] = both.astype(BF16)
        kept.append(parts[4][8:])
    o_ref[z, 128:144, :] = jnp.concatenate(kept, axis=0).astype(BF16)


def analysis_kernel(table_ref, x_ref, o_ref, all_ref):
    q = pl.program_id(0)
    for mg in range(8):

        @pl.when(q == mg // 2)
        def _(mg=mg):
            analyse(mg, x_ref, lambda m, rows: table_ref[mg % 2 * 4 + m, rows, :], all_ref)

    @pl.when(q == 3)
    def _():
        def place(z, _):
            analysis_rows(z, all_ref, o_ref)
            return 0

        lax.fori_loop(0, NZ, place, 0)


def analysis(table, fields):
    return call(
        analysis_kernel,
        jax.ShapeDtypeStruct((NZ, ROWS, 128), BF16),
        (4,),
        [
            pl.BlockSpec((8, MODES, JH), lambda q: (q, 0, 0)),
            pl.BlockSpec((3, NA, 8, 16, 128), lambda q: (0, 0, 0, 0, 0)),
        ],
        pl.BlockSpec((NZ, ROWS, 128), lambda q: (0, 0, 0)),
        [pltpu.VMEM((8, MODES, 128), F32)],
        2 * 80 * 128 * JH * 256,
        18_000_000,
    )(table, fields)


def filter_row(mg, a, t):
    if mg < 4:
        return 32 * mg + 16 * t + a
    if mg == 4:
        return 128 + 8 * t + a - 8
    return 32 * (8 - mg) + 16 * t + a - 2 * mg


def filter_kernel(x_ref, w_ref, o_ref, in_ref, out_ref):
    def gather(step, _):
        start = pl.multiple_of(step * 16, 16)
        for h in range(2):
            xs = [x_ref[h * 8 + z, pl.ds(start, 16), :].astype(F32) for z in range(8)]
            for mr, y in enumerate(swap_blocks(xs)):
                in_ref[h, pl.ds(start * 8 + mr, 16, stride=8), :] = y
        return 0

    lax.fori_loop(0, ROWS // 16, gather, 0)
    for a in range(16):
        for t in range(2):
            rows = [8 * filter_row(mg, a, t) for mg in range(a // 2 + 1)]
            x = jnp.concatenate(
                [
                    jnp.concatenate([in_ref[h, r : r + 8, :] for r in rows], axis=0)
                    for h in range(2)
                ],
                axis=1,
            ).astype(BF16)
            y = jnp.dot(x, w_ref[a, t], preferred_element_type=F32)
            for i, r in enumerate(rows):
                for h in range(2):
                    out_ref[h, r : r + 8, :] = y[i * 8 : i * 8 + 8, h * 128 : h * 128 + 128]

    def scatter(step, _):
        start = pl.multiple_of(step * 16, 16)
        for h in range(2):
            xs = [out_ref[h, pl.ds(start * 8 + mr, 16, stride=8), :] for mr in range(8)]
            for z, y in enumerate(swap_blocks(xs)):
                o_ref[h * 8 + z, pl.ds(start, 16), :] = y.astype(BF16)
        return 0

    lax.fori_loop(0, ROWS // 16, scatter, 0)


def channel_filter(coefficients, weight):
    whole = pl.BlockSpec((NZ, ROWS, 128), lambda i: (0, 0, 0))
    return call(
        filter_kernel,
        jax.ShapeDtypeStruct((NZ, ROWS, 128), BF16),
        (1,),
        [whole, pl.BlockSpec((NA, 2, CH, CH), lambda i: (0, 0, 0, 0))],
        whole,
        [pltpu.VMEM((2, ROWS * 8, 128), F32), pltpu.VMEM((2, ROWS * 8, 128), F32)],
        2 * ROWS * 8 * CH * CH,
        6_000_000,
    )(coefficients, weight)


def synthesis_rows(z, x_ref, all_ref):
    row = lax.broadcasted_iota(jnp.int32, (16, 128), 0)
    last = x_ref[z, 128:144, :].astype(F32)
    for t in range(2):
        where = pl.ds(2 * z + t, 16, stride=32)
        all_ref[0, where, :] = x_ref[z, t * 16 : t * 16 + 16, :].astype(F32)
        for s in range(1, 4):
            x = x_ref[z, s * 32 + t * 16 : s * 32 + t * 16 + 16, :].astype(F32)
            all_ref[s, where, :] = jnp.where(row >= 2 * s, x, 0.0)
            all_ref[8 - s, where, :] = jnp.where(
                row >= 16 - 2 * s, pltpu.roll(x, 16 - 2 * s, 0), 0.0
            )
        all_ref[4, where, :] = jnp.concatenate(
            [jnp.zeros((8, 128), F32), last[t * 8 : t * 8 + 8]], axis=0
        )


def synthesise(mg, table, all_ref, o_ref):
    low = mg // 2 * 128
    block = lax.broadcasted_iota(jnp.int32, (MODES - low, 128), 1) // 32
    row = lax.broadcasted_iota(jnp.int32, (MODES - low, 128), 0)
    same = (block + row) % 2 == 0
    x = all_ref[mg, low:, :]
    even = jnp.where(same, x, 0.0).T.astype(BF16)
    odd = jnp.where(same, 0.0, x).T.astype(BF16)
    evens, odds = [], []
    for m in range(4):
        rows = slice(m * 32, m * 32 + 32)
        both = jnp.concatenate([even[rows], odd[rows]], axis=0)
        part = jnp.dot(both, table(m, slice(low, MODES)), preferred_element_type=F32)
        evens.append(part[:32])
        odds.append(part[32:])
    even = jnp.concatenate(evens, axis=0).T
    odd = jnp.concatenate(odds, axis=0).T
    north = (even + odd).astype(BF16)
    south = (even - odd).astype(BF16)
    place = PLACE.index(mg)
    for gp in range(3):
        for a in range(8):
            rows = slice(gp * 128 + a * 16, gp * 128 + a * 16 + 16)
            o_ref[a, place, gp] = north[rows]
            o_ref[15 - a, place, gp] = south[rows]


def synthesis_kernel(table_ref, x_ref, o_ref, all_ref):
    q = pl.program_id(0)

    @pl.when(q == 0)
    def _():
        def place(z, _):
            synthesis_rows(z, x_ref, all_ref)
            return 0

        lax.fori_loop(0, NZ, place, 0)

    for mg in range(8):

        @pl.when(q == mg // 2)
        def _(mg=mg):
            synthesise(mg, lambda m, rows: table_ref[mg % 2 * 4 + m, rows, :], all_ref, o_ref)


def synthesis(table, filtered):
    return call(
        synthesis_kernel,
        jax.ShapeDtypeStruct((NA, 8, 3, 16, 128), BF16),
        (4,),
        [
            pl.BlockSpec((8, MODES, JH), lambda q: (q, 0, 0)),
            pl.BlockSpec((NZ, ROWS, 128), lambda q: (0, 0, 0)),
        ],
        pl.BlockSpec((NA, 8, 3, 16, 128), lambda q: (0, 0, 0, 0, 0)),
        [pltpu.VMEM((8, MODES, 128), F32)],
        2 * 80 * 128 * JH * 64,
        18_000_000,
    )(table, filtered)


def inverse_pair(gp, u_ref, x_ref, table_ref, o_ref, wide_ref, rows_ref, lhs_ref, acc_ref):
    def place(a, _):
        wide_ref[...] = u_ref[a, :, gp].reshape(128, 128).astype(F32)
        for gg in range(2):
            xs = [wide_ref[pl.ds(gg * 8 + j, 8, stride=16), :] for j in range(8)]
            for mr, y in enumerate(swap_blocks(xs)):
                rows_ref[gg, pl.ds(pl.multiple_of(a * 64 + mr * 8, 8), 8), :] = y
        return 0

    lax.fori_loop(0, NA, place, 0)
    for gg in range(2):
        for k in range(8):
            cols = slice(k * 128, (k + 1) * 128)
            lhs_ref[gg * 128 : gg * 128 + 128, cols] = rows_ref[gg, cols, :].T.astype(BF16)
    for part in range(2):
        rows = slice(part * 128, part * 128 + 128)
        acc_ref[rows, :NLON] = jnp.dot(lhs_ref[rows, :], table_ref[...], preferred_element_type=F32)
    row = lax.broadcasted_iota(jnp.int32, (NP, 256), 0)
    lane = lax.broadcasted_iota(jnp.int32, (NP, 256), 1)
    for z in range(NZ):
        begin = ND * z // 128 * 128
        pick = jnp.logical_and(lane == row + (ND * z - begin), row < ND)
        pick = jnp.where(pick, 1.0, 0.0).astype(BF16)
        x = jnp.concatenate([x_ref[2 * gp + gg, z].astype(F32).T for gg in range(2)], axis=0)
        acc_ref[:, begin : begin + 256] += jnp.dot(
            x.astype(BF16), pick, preferred_element_type=F32
        )
    for j in range(16):

        @pl.when(16 * gp + j < JD)
        def _(j=j):
            o_ref[band_row(16 * gp + j)] = acc_ref[16 * j : 16 * j + 16, :NLON].astype(BF16)


def inverse_kernel(
    u_ref, x_ref, basis_ref, o_ref, table_ref, wide_ref, rows_ref, lhs_ref, acc_ref
):
    gp = pl.program_id(0)

    @pl.when(gp == 0)
    def _():
        wave_table(basis_ref, table_ref, True)

    inverse_pair(gp, u_ref, x_ref, table_ref, o_ref, wide_ref, rows_ref, lhs_ref, acc_ref)


def inverse(waves, fields, basis):
    return call(
        inverse_kernel,
        jax.ShapeDtypeStruct((JD, 16, NLON), BF16),
        (3,),
        [
            pl.BlockSpec((NA, 8, 3, 16, 128), lambda g: (0, 0, 0, 0, 0)),
            pl.BlockSpec((6, NZ, NP, 128), lambda g: (0, 0, 0, 0)),
            pl.BlockSpec((6, 8, NLON), lambda g: (0, 0, 0)),
        ],
        pl.BlockSpec((JD, 16, NLON), lambda g: (0, 0, 0)),
        [
            pltpu.VMEM((KB, NLON), BF16),
            pltpu.VMEM((128, 128), F32),
            pltpu.VMEM((2, KB, 128), F32),
            pltpu.VMEM((256, KB), BF16),
            pltpu.VMEM((256, 1536), F32),
        ],
        2 * KB * NLON * 768,
        10_000_000,
    )(waves, fields, basis)


def legendre_inputs(lat_index):
    slot = jnp.arange(32, dtype=jnp.int32)
    orders = (32 * (slot // 2) + 2 * lat_index + slot % 2).astype(F32)
    column = jnp.arange(JH, dtype=jnp.int32)
    local = column // 128 * 16 + column % 16
    theta = jnp.pi * ((column // 16 % 8 * JD + local).astype(F32) + 0.5) / NLAT
    real = local < JD
    cosine = jnp.where(real, jnp.cos(theta), 0.0)
    log_sine = jnp.log(jnp.where(real, jnp.sin(theta), 1.0))
    counts = jnp.arange(1, MODES + 1, dtype=F32)
    ratios = jnp.log((2.0 * counts - 1.0) / (2.0 * counts))
    partial_log = jnp.sum(jnp.where(counts[None, :] <= orders[:, None], ratios[None, :], 0.0), axis=1)
    start_log = (
        orders[:, None] * log_sine[None, :]
        + 0.5 * jnp.log(orders + 0.5)[:, None]
        + 0.5 * partial_log[:, None]
    )
    start_log = jnp.where(real[None, :], start_log, -1e9)
    return (
        jnp.broadcast_to(orders.reshape(4, 8, 1), (4, 8, 128)),
        jnp.broadcast_to(cosine[None, :], (8, JH)),
        start_log.reshape(4, 8, JH),
    )


def spectrum_weights(lat_index):
    local = jnp.arange(6 * 128, dtype=jnp.int32) // 16
    band = jnp.minimum(lat_index, 15 - lat_index)
    theta = jnp.pi * ((band * JD + local).astype(F32) + 0.5) / NLAT
    weights = jnp.pi / NLAT * jnp.sin(theta) / NLON
    return jnp.where(local < JD, weights, 0.0).reshape(3, 1, 256)


def exchange(x, axis):
    return lax.all_to_all(x, axis, split_axis=0, concat_axis=0, tiled=True)


def on_device(grid, norm_gain, mlp_in, mlp_out, filter_weight):
    lat_index = lax.axis_index("lat")
    weight = lax.all_gather(filter_weight, "lat")
    rows, spectrum, table = forward(
        grid.transpose(1, 2, 0),
        norm_gain.reshape(1, CH),
        mlp_in,
        mlp_out,
        forward_basis(),
        spectrum_weights(lat_index),
        *legendre_inputs(lat_index),
    )
    coefficients = analysis(table, spectrum)
    filtered = channel_filter(exchange(coefficients, "lon"), weight)
    synthesized = synthesis(table, exchange(filtered, "lon"))
    updated = inverse(exchange(synthesized, "lat"), rows, inverse_basis())
    return updated.transpose(1, 0, 2)


def solution(mesh):
    return jax.shard_map(
        on_device,
        mesh=mesh,
        in_specs=(P("batch", "lat", "lon"), P(), P(), P(), P(("lat", "lon"), None, None)),
        out_specs=P(("batch", "lon"), "lat", None),
        check_vma=False,
    )
```

```python
import functools

import jax
import jax.numpy as jnp
from jax import lax
from jax.experimental import pallas as pl
from jax.experimental.pallas import tpu as pltpu
from jax.sharding import PartitionSpec as P

F32 = jnp.float32
BF16 = jnp.bfloat16

CH = 256
HID = 512
JD = 45
JP = 48
ND = 90
NP = 96
NLAT = 720
NLON = 1440
MODES = 512
NA = 16
NZ = 16
JH = NA * JP // 2
LAST = JD - 1
KB = 2 * MODES
ROWS = 144
LIMIT = 56 * 1024 * 1024
MESH = pl.DeviceIdType.MESH
OTHERS = (8, 7, 9, 6, 10, 5, 11, 4, 12, 3, 13, 2, 14, 1, 15)
CHUNKS = ((0, 1, 4, 7), (2, 3, 5, 6))
SLOTS = ((0, 1, 4), (2, 3))
BASE = {0: 0, 1: 32, 4: 64, 2: 80, 3: 112}
SPAN = ((0, 80), (80, 64))


def swap_blocks(xs):
    block = lax.broadcasted_iota(jnp.int32, xs[0].shape, 1) // 16
    for bit in (1, 2, 4):
        upper = (block & bit) != 0
        new = list(xs)
        for i in range(8):
            if i & bit == 0:
                low, high = xs[i], xs[i | bit]
                new[i] = jnp.where(upper, pltpu.roll(high, 16 * bit, 1), low)
                new[i | bit] = jnp.where(upper, high, pltpu.roll(low, 128 - 16 * bit, 1))
        xs = new
    return xs


def greet(axes):
    barrier = pltpu.get_barrier_semaphore()
    for axis in axes:
        me = lax.axis_index(axis)
        for d in range(1, 16):
            pl.semaphore_signal(
                barrier, inc=1, device_id={axis: lax.rem(me + d, 16)}, device_id_type=MESH
            )
    pl.semaphore_wait(barrier, 15 * len(axes))


def to_peer(axis, d, src, dst, send, recv):
    peer = lax.rem(lax.axis_index(axis) + d, 16)
    return pltpu.make_async_remote_copy(
        src_ref=src(peer),
        dst_ref=dst,
        send_sem=send,
        recv_sem=recv,
        device_id={axis: peer},
        device_id_type=MESH,
    )


def band_row(jj):
    jj = jnp.minimum(jj, LAST)
    return jnp.where(lax.axis_index("lat") >= 8, LAST - jj, jj)


def mlp_chunk(g, x_ref, gain_ref, in_ref, out_w_ref, o_ref, pad_ref, mix_ref):
    for j in range(8):
        pad_ref[j * NP : j * NP + ND, :] = x_ref[band_row(8 * g + j)].astype(F32)
    half = 2 * NP
    for part in range(4):
        rows = slice(part * half, (part + 1) * half)
        x = pad_ref[rows, :]
        mean = jnp.mean(x, axis=1, keepdims=True)
        centered = x - mean
        spread = jnp.mean(centered * centered, axis=1, keepdims=True)
        normed = (centered * lax.rsqrt(spread + 1e-05) * gain_ref[...]).astype(BF16)
        hidden = jnp.dot(normed, in_ref[...], preferred_element_type=F32)
        hidden = jax.nn.gelu(hidden).astype(BF16)
        mixed = x + jnp.dot(hidden, out_w_ref[...], preferred_element_type=F32)
        mix_ref[0, rows, :] = mixed[:, :128]
        mix_ref[1, rows, :] = mixed[:, 128:]
    lane = lax.broadcasted_iota(jnp.int32, (16, 128), 1)
    row = lax.broadcasted_iota(jnp.int32, (16, 128), 0)
    live = lane // 16 < JD - 8 * g

    def place(step, _):
        start = pl.multiple_of(step * 16, 16)
        keep = jnp.logical_and(live, row < ND - start)
        for h in range(2):
            xs = [mix_ref[h, pl.ds(pl.multiple_of(j * NP + start, 16), 16), :] for j in range(8)]
            for z, y in enumerate(swap_blocks(xs)):
                o_ref[g, h * 8 + z, pl.ds(start, 16), :] = jnp.where(keep, y, 0.0).astype(BF16)
        return 0

    lax.fori_loop(0, NP // 16, place, 0)


def wave_tile(group, basis_ref, high, low):
    group_cos, group_sin = basis_ref[group], basis_ref[group + 1]
    high_cos = basis_ref[2, pl.ds(high, 1), :]
    high_sin = basis_ref[3, pl.ds(high, 1), :]
    low_cos = basis_ref[0, low : low + 1, :]
    low_sin = basis_ref[1, low : low + 1, :]
    c = high_cos * low_cos - high_sin * low_sin
    s = high_sin * low_cos + high_cos * low_sin
    return group_cos * c - group_sin * s, -(group_sin * c + group_cos * s)


def forward_waves(basis_ref, o_ref):
    def step(high, _):
        for low in range(8):
            tile = wave_tile(4, basis_ref, high, low)
            offset = 8 * high + low
            start = offset // 2 % 16 * 64 + offset // 32 * 32 + low % 2 * 16
            o_ref[pl.ds(pl.multiple_of(start, 16), 16), :] = jnp.concatenate(tile, axis=0).astype(
                BF16
            )
        return 0

    lax.fori_loop(0, 8, step, 0)


def inverse_waves(basis_ref, o_ref):
    row = lax.broadcasted_iota(jnp.int32, (8, NLON), 0)

    def step(high, _):
        for low in (0, 1, 4, 5):
            for c in range(2):
                real, imag = wave_tile(4 + 2 * c, basis_ref, high, low)
                if low == 0 and c == 0:
                    real = jnp.where(jnp.logical_and(high == 0, row == 0), 0.5 * real, real)
                w = high % 4 * 2 + low // 4
                start = c * 512 + w * 64 + high // 4 * 32 + low % 2 * 16
                o_ref[pl.ds(pl.multiple_of(start, 16), 16), :] = jnp.concatenate(
                    [real, imag], axis=0
                ).astype(BF16)
        return 0

    lax.fori_loop(0, 8, step, 0)


def wave_basis(points, scale, groups):
    count = jnp.arange(8, dtype=jnp.int32)
    multiple = jnp.stack([count, 8 * count] + [jnp.array(g, jnp.int32) for g in groups])
    phase = multiple[:, :, None] * points[None, None, :] % NLON
    angle = 2.0 * jnp.pi / NLON * phase.astype(F32)
    one = jnp.ones_like(scale)
    factor = jnp.stack([one, one] + [scale] * len(groups))[:, None, :]
    return jnp.stack([jnp.cos(angle) * factor, jnp.sin(angle) * factor], axis=1).reshape(
        -1, 8, points.shape[0]
    )


def forward_basis():
    column = jnp.arange(NZ * NP, dtype=jnp.int32)
    n = column % NP
    return wave_basis(
        column // NP * ND + n, jnp.where(n < ND, 1.0, 0.0), [[64 * mg for mg in range(8)]]
    )


def inverse_basis():
    groups = [[64 * mg + 2 * a for a in range(2) for mg in chunk] for chunk in CHUNKS]
    return wave_basis(jnp.arange(NLON, dtype=jnp.int32), jnp.full((NLON,), 2.0, F32), groups)


def dft_pair(x_ref, gp, table_ref, weight_ref, o_ref, acc_ref, swap_ref):
    both = jnp.concatenate(
        [x_ref[2 * gp + gg].reshape(NZ * NP, 128) for gg in range(2)], axis=1
    )
    for part in range(4):
        rows = slice(part * 256, (part + 1) * 256)
        acc = jnp.dot(table_ref[rows, :], both, preferred_element_type=F32)
        acc = acc * weight_ref[gp]
        acc_ref[0, rows, :] = acc[:, :128]
        acc_ref[1, rows, :] = acc[:, 128:]

    def place(a, _):
        for gg in range(2):
            xs = [
                acc_ref[gg, pl.ds(pl.multiple_of(a * 64 + mr * 8, 8), 8), :] for mr in range(8)
            ]
            for j, y in enumerate(swap_blocks(xs)):
                swap_ref[pl.ds(gg * 8 + j, 8, stride=16), :] = y
        o_ref[gp, a] = swap_ref[...].astype(BF16).reshape(8, 16, 128)
        return 0

    lax.fori_loop(0, NA, place, 0)


def legendre_group(q, i, order_ref, cos_ref, o_ref, up_ref, low_ref, scale_ref, swap_ref):
    order = order_ref[q]
    degree = lax.broadcasted_iota(jnp.int32, (8, 128), 1) + 16 * i
    degree = degree.astype(F32)
    active = degree > order
    second = degree > order + 1.0
    grow = jnp.sqrt(
        jnp.where(active, 4.0 * degree * degree - 1.0, 0.0)
        / jnp.where(active, degree * degree - order * order, 1.0)
    )
    before = degree - 1.0
    damp = grow * jnp.sqrt(
        jnp.where(second, before * before - order * order, 0.0)
        / jnp.where(second, 4.0 * before * before - 1.0, 1.0)
    )
    first = jnp.where(degree == order, 1.0, 0.0)
    up, low, scale_log = up_ref[q], low_ref[q], scale_ref[q]
    root = jnp.exp(0.5 * scale_log)
    cosine = cos_ref[...]
    for s in range(16):
        a = jnp.broadcast_to(grow[:, s : s + 1], (8, JH))
        b = jnp.broadcast_to(damp[:, s : s + 1], (8, JH))
        e = jnp.broadcast_to(first[:, s : s + 1], (8, JH))
        fresh = a * (cosine * up) - b * low + e
        low = up
        up = fresh
        value = fresh * root * root
        for k in range(3):
            swap_ref[q, k, s * 8 : s * 8 + 8, :] = value[:, k * 128 : k * 128 + 128]
    largest = jnp.maximum(jnp.abs(up), jnp.abs(low))
    largest = jnp.where(largest > 0.0, largest, 1.0)
    up_ref[q] = up / largest
    low_ref[q] = low / largest
    scale_ref[q] = scale_log + jnp.log(largest)
    start = pl.multiple_of(i * 16, 16)
    for m in range(8):
        for k in range(3):
            o_ref[8 * q + m, pl.ds(start, 16), k * 128 : k * 128 + 128] = swap_ref[
                q, k, pl.ds(m, 16, stride=8), :
            ].astype(BF16)


def legendre(order_ref, cos_ref, log_ref, o_ref, up_ref, low_ref, scale_ref, swap_ref):
    up_ref[...] = jnp.zeros_like(up_ref)
    low_ref[...] = jnp.zeros_like(low_ref)
    scale_ref[...] = log_ref[...]
    for stage in range(4):

        def step(i, _, stage=stage):
            for q in range(stage + 1):
                legendre_group(
                    q, i, order_ref, cos_ref, o_ref, up_ref, low_ref, scale_ref, swap_ref
                )
            return 0

        lax.fori_loop(8 * stage, 8 * stage + 8, step, 0)


def forward_kernel(
    x_ref,
    gain_ref,
    in_ref,
    out_w_ref,
    basis_ref,
    weight_ref,
    order_ref,
    cos_ref,
    log_ref,
    rows_ref,
    spectrum_ref,
    legendre_ref,
    pad_ref,
    mix_ref,
    out_rows,
    got_rows,
    table_ref,
    acc_ref,
    swap_ref,
    out_spectrum,
    table_l,
    up_ref,
    low_ref,
    scale_ref,
    swap_l,
    z_send,
    z_recv,
    a_send,
    a_recv,
    own,
):
    lat = lax.axis_index("lat")
    lon = lax.axis_index("lon")

    def row_copy(g, d):
        return to_peer(
            "lon",
            d,
            lambda peer: out_rows.at[g, peer],
            got_rows.at[g, lon],
            z_send.at[g, d],
            z_recv.at[g, d],
        )

    def spectrum_copy(gp, d):
        return to_peer(
            "lat",
            d,
            lambda peer: out_spectrum.at[gp, peer],
            spectrum_ref.at[gp, lat],
            a_send.at[gp, d],
            a_recv.at[gp, d],
        )

    def own_row(g):
        return pltpu.make_async_copy(out_rows.at[g, lon], got_rows.at[g, lon], own.at[0, g])

    def own_spectrum(gp):
        return pltpu.make_async_copy(
            out_spectrum.at[gp, lat], spectrum_ref.at[gp, lat], own.at[1, gp]
        )

    def keep_rows(gp):
        pair = pl.ds(2 * gp, 2)
        return pltpu.make_async_copy(got_rows.at[pair], rows_ref.at[pair], own.at[2, gp])

    def keep_table(q):
        part = (pl.ds(8 * q, 8), pl.ds(128 * q, MODES - 128 * q))
        return pltpu.make_async_copy(table_l.at[part], legendre_ref.at[part], own.at[3, q])

    greet(("lat", "lon"))

    def mlp_step(g, _):
        mlp_chunk(g, x_ref, gain_ref, in_ref, out_w_ref, out_rows, pad_ref, mix_ref)
        for d in OTHERS:
            row_copy(g, d).start()
        own_row(g).start()
        return 0

    pad_ref[...] = jnp.zeros_like(pad_ref)
    lax.fori_loop(0, 6, mlp_step, 0)
    forward_waves(basis_ref, table_ref)
    legendre(order_ref, cos_ref, log_ref, table_l, up_ref, low_ref, scale_ref, swap_l)
    for q in range(4):
        keep_table(q).start()

    def dft_step(gp, _):
        for gg in range(2):
            own_row(2 * gp + gg).wait()
            for d in OTHERS:
                row_copy(2 * gp + gg, d).wait_recv()
        keep_rows(gp).start()
        dft_pair(got_rows, gp, table_ref, weight_ref, out_spectrum, acc_ref, swap_ref)
        for d in OTHERS:
            spectrum_copy(gp, d).start()
        own_spectrum(gp).start()
        return 0

    lax.fori_loop(0, 3, dft_step, 0)
    for q in range(4):
        keep_table(q).wait()

    def finish(gp, _):
        for gg in range(2):
            for d in OTHERS:
                row_copy(2 * gp + gg, d).wait_send()
        keep_rows(gp).wait()
        own_spectrum(gp).wait()
        for d in OTHERS:
            spectrum_copy(gp, d).wait()
        return 0

    lax.fori_loop(0, 3, finish, 0)


VM = pl.BlockSpec(memory_space=pltpu.VMEM)
ANY = pl.BlockSpec(memory_space=pl.ANY)


def forward(*operands):
    return pl.pallas_call(
        forward_kernel,
        out_shape=(
            jax.ShapeDtypeStruct((6, NZ, NP, 128), BF16),
            jax.ShapeDtypeStruct((3, NA, 8, 16, 128), BF16),
            jax.ShapeDtypeStruct((32, MODES, JH), BF16),
        ),
        in_specs=[VM] * len(operands),
        out_specs=(ANY, ANY, ANY),
        scratch_shapes=[
            pltpu.VMEM((8 * NP, CH), F32),
            pltpu.VMEM((2, 8 * NP, 128), F32),
            pltpu.VMEM((6, NZ, NP, 128), BF16),
            pltpu.VMEM((6, NZ, NP, 128), BF16),
            pltpu.VMEM((KB, NZ * NP), BF16),
            pltpu.VMEM((2, KB, 128), F32),
            pltpu.VMEM((128, 128), F32),
            pltpu.VMEM((3, NA, 8, 16, 128), BF16),
            pltpu.VMEM((32, MODES, JH), BF16),
            pltpu.VMEM((4, 8, JH), F32),
            pltpu.VMEM((4, 8, JH), F32),
            pltpu.VMEM((4, 8, JH), F32),
            pltpu.VMEM((4, 3, 128, 128), F32),
            pltpu.SemaphoreType.DMA((6, 16)),
            pltpu.SemaphoreType.DMA((6, 16)),
            pltpu.SemaphoreType.DMA((3, 16)),
            pltpu.SemaphoreType.DMA((3, 16)),
            pltpu.SemaphoreType.DMA((4, 6)),
        ],
        cost_estimate=pl.CostEstimate(
            flops=8_000_000_000, bytes_accessed=30_000_000, transcendentals=0
        ),
        compiler_params=pltpu.CompilerParams(
            collective_id=1, has_side_effects=True, vmem_limit_bytes=LIMIT
        ),
    )(*operands)


def analyse(mg, x_ref, table, all_ref):
    north, south = [], []
    for gp in range(3):
        north.append(x_ref[gp, :8, mg].reshape(128, 128).astype(F32))
        south.append(jnp.concatenate([x_ref[gp, 15 - a, mg] for a in range(8)], axis=0).astype(F32))
    north = jnp.concatenate(north, axis=0)
    south = jnp.concatenate(south, axis=0)
    both = jnp.concatenate([north + south, north - south], axis=1).astype(BF16)
    block = lax.broadcasted_iota(jnp.int32, (128, 128), 1) // 32
    odd = lax.broadcasted_iota(jnp.int32, (128, 128), 0) % 2 == 1
    for lb in range(mg // 2, 4):
        rows = slice(lb * 128, lb * 128 + 128)
        total = jnp.zeros((128, 128), F32)
        for m in range(4):
            part = jnp.dot(table(m, rows), both, preferred_element_type=F32)
            first, second = part[:, :128], part[:, 128:]
            if m % 2:
                first, second = second, first
            total = jnp.where(block == m, jnp.where(odd, second, first), total)
        all_ref[mg, rows, :] = total


def analysis_rows(z, chunk, all_ref, o_ref):
    row = lax.broadcasted_iota(jnp.int32, (16, 128), 0)
    kept = []
    for t in range(2):
        where = pl.ds(2 * z + t, 16, stride=32)
        for s in SLOTS[chunk]:
            x = all_ref[s, where, :]
            if s == 4:
                kept.append(x[8:])
                continue
            if s:
                x = jnp.where(row < 2 * s, pltpu.roll(all_ref[8 - s, where, :], 2 * s, 0), x)
            start = BASE[s] + t * 16
            o_ref[z, start : start + 16, :] = x.astype(BF16)
    if kept:
        o_ref[z, 64:80, :] = jnp.concatenate(kept, axis=0).astype(BF16)


def filter_row(mg, a, t):
    if mg < 4:
        return BASE[mg] + 16 * t + a
    if mg == 4:
        return BASE[4] + 8 * t + a - 8
    return BASE[8 - mg] + 16 * t + a - 2 * mg


def filter_chunk(chunk, x_ref, w_ref, o_ref, in_ref, out_ref):
    begin, count = SPAN[chunk]

    def gather(step, _):
        start = pl.multiple_of(begin + step * 16, 16)
        for h in range(2):
            xs = [x_ref[h * 8 + z, pl.ds(start, 16), :].astype(F32) for z in range(8)]
            for mr, y in enumerate(swap_blocks(xs)):
                in_ref[h, pl.ds(start * 8 + mr, 16, stride=8), :] = y
        return 0

    lax.fori_loop(0, count // 16, gather, 0)
    for a in range(16):
        for t in range(2):
            rows = [8 * filter_row(mg, a, t) for mg in CHUNKS[chunk] if mg <= a // 2]
            if not rows:
                continue
            x = jnp.concatenate(
                [
                    jnp.concatenate([in_ref[h, r : r + 8, :] for r in rows], axis=0)
                    for h in range(2)
                ],
                axis=1,
            ).astype(BF16)
            y = jnp.dot(x, w_ref[a, t], preferred_element_type=F32)
            for i, r in enumerate(rows):
                for h in range(2):
                    out_ref[h, r : r + 8, :] = y[i * 8 : i * 8 + 8, h * 128 : h * 128 + 128]

    def scatter(step, _):
        start = pl.multiple_of(begin + step * 16, 16)
        for h in range(2):
            xs = [out_ref[h, pl.ds(start * 8 + mr, 16, stride=8), :] for mr in range(8)]
            for z, y in enumerate(swap_blocks(xs)):
                o_ref[h * 8 + z, pl.ds(start, 16), :] = y.astype(BF16)
        return 0

    lax.fori_loop(0, count // 16, scatter, 0)


def synthesis_rows(z, chunk, x_ref, all_ref):
    row = lax.broadcasted_iota(jnp.int32, (16, 128), 0)
    for s in SLOTS[chunk]:
        for t in range(2):
            where = pl.ds(2 * z + t, 16, stride=32)
            if s == 4:
                last = x_ref[z, 64:80, :].astype(F32)
                x = jnp.concatenate([jnp.zeros((8, 128), F32), last[t * 8 : t * 8 + 8]], axis=0)
                all_ref[4, where, :] = x
                continue
            start = BASE[s] + t * 16
            x = x_ref[z, start : start + 16, :].astype(F32)
            if s:
                all_ref[8 - s, where, :] = jnp.where(
                    row >= 16 - 2 * s, pltpu.roll(x, 16 - 2 * s, 0), 0.0
                )
                x = jnp.where(row >= 2 * s, x, 0.0)
            all_ref[s, where, :] = x


def synthesise(mg, table, all_ref, o_ref):
    low = mg // 2 * 128
    block = lax.broadcasted_iota(jnp.int32, (MODES - low, 128), 1) // 32
    row = lax.broadcasted_iota(jnp.int32, (MODES - low, 128), 0)
    same = (block + row) % 2 == 0
    x = all_ref[mg, low:, :]
    even = jnp.where(same, x, 0.0).T.astype(BF16)
    odd = jnp.where(same, 0.0, x).T.astype(BF16)
    evens, odds = [], []
    for m in range(4):
        rows = slice(m * 32, m * 32 + 32)
        both = jnp.concatenate([even[rows], odd[rows]], axis=0)
        part = jnp.dot(both, table(m, slice(low, MODES)), preferred_element_type=F32)
        evens.append(part[:32])
        odds.append(part[32:])
    even = jnp.concatenate(evens, axis=0).T
    odd = jnp.concatenate(odds, axis=0).T
    north = (even + odd).astype(BF16)
    south = (even - odd).astype(BF16)
    chunk = 0 if mg in CHUNKS[0] else 1
    place = CHUNKS[chunk].index(mg)
    for gp in range(3):
        for a in range(8):
            rows = slice(gp * 128 + a * 16, gp * 128 + a * 16 + 16)
            o_ref[chunk, gp, a, place] = north[rows]
            o_ref[chunk, gp, 15 - a, place] = south[rows]


def residual(gp, x_ref, acc_ref):
    row = lax.broadcasted_iota(jnp.int32, (NP, 256), 0)
    lane = lax.broadcasted_iota(jnp.int32, (NP, 256), 1)
    acc_ref[gp] = jnp.zeros(acc_ref.shape[1:], F32)
    for z in range(NZ):
        begin = ND * z // 128 * 128
        pick = jnp.logical_and(lane == row + (ND * z - begin), row < ND)
        pick = jnp.where(pick, 1.0, 0.0).astype(BF16)
        x = jnp.concatenate([x_ref[2 * gp + gg, z].astype(F32).T for gg in range(2)], axis=0)
        acc_ref[gp, :, begin : begin + 256] += jnp.dot(
            x.astype(BF16), pick, preferred_element_type=F32
        )


def inverse_part(chunk, gp, u_ref, table_ref, wide_ref, rows_ref, lhs_ref, acc_ref):
    def place(w, _):
        wide_ref[...] = u_ref[chunk, gp, pl.ds(2 * w, 2)].reshape(128, 128).astype(F32)
        for gg in range(2):
            xs = [wide_ref[pl.ds(gg * 8 + j, 8, stride=16), :] for j in range(8)]
            for mr, y in enumerate(swap_blocks(xs)):
                rows_ref[gg, pl.ds(pl.multiple_of(w * 64 + mr * 8, 8), 8), :] = y
        return 0

    lax.fori_loop(0, 8, place, 0)
    for gg in range(2):
        for k in range(4):
            cols = slice(k * 128, (k + 1) * 128)
            lhs_ref[gg * 128 : gg * 128 + 128, cols] = rows_ref[gg, cols, :].T.astype(BF16)
    waves = slice(chunk * 512, chunk * 512 + 512)
    for part in range(2):
        rows = slice(part * 128, part * 128 + 128)
        acc_ref[gp, rows, :NLON] += jnp.dot(
            lhs_ref[rows, :], table_ref[waves, :], preferred_element_type=F32
        )


def emit(gp, acc_ref, o_ref):
    for j in range(16):

        @pl.when(16 * gp + j < JD)
        def _(j=j):
            o_ref[band_row(16 * gp + j)] = acc_ref[gp, 16 * j : 16 * j + 16, :NLON].astype(BF16)


def backward_kernel(
    spectrum_any,
    legendre_any,
    weight_any,
    rows_any,
    basis_ref,
    o_ref,
    spectrum,
    table_l,
    weight,
    rows,
    all_ref,
    out_c,
    got_c,
    out_f,
    got_f,
    in_ref,
    out_ref,
    out_u,
    got_u,
    table_ref,
    wide_ref,
    rows_ref,
    lhs_ref,
    acc_ref,
    load,
    own,
    c_send,
    c_recv,
    f_send,
    f_recv,
    u_send,
    u_recv,
):
    lat = lax.axis_index("lat")
    lon = lax.axis_index("lon")

    def load_table(mg):
        low = mg // 2 * 128
        part = (pl.ds(4 * mg, 4), pl.ds(low, MODES - low))
        return pltpu.make_async_copy(legendre_any.at[part], table_l.at[part], load.at[3 + mg])

    load_spectrum = pltpu.make_async_copy(spectrum_any, spectrum, load.at[0])
    load_weight = pltpu.make_async_copy(weight_any, weight, load.at[1])
    load_rows = pltpu.make_async_copy(rows_any, rows, load.at[2])

    def row_copy(chunk, out, got, send, recv):
        part = pl.ds(*SPAN[chunk])

        def copy(d):
            return to_peer(
                "lon",
                d,
                lambda peer: out.at[peer, part],
                got.at[lon, part],
                send.at[chunk, d],
                recv.at[chunk, d],
            )

        return copy

    def own_copy(chunk, out, got, k):
        part = pl.ds(*SPAN[chunk])
        return pltpu.make_async_copy(out.at[lon, part], got.at[lon, part], own.at[k, chunk])

    def wave_copy(chunk, gp, d):
        return to_peer(
            "lat",
            d,
            lambda peer: out_u.at[chunk, gp, peer],
            got_u.at[chunk, gp, lat],
            u_send.at[chunk, gp, d],
            u_recv.at[chunk, gp, d],
        )

    def own_wave(chunk, gp):
        return pltpu.make_async_copy(
            out_u.at[chunk, gp, lat], got_u.at[chunk, gp, lat], own.at[2 + chunk, gp]
        )

    def each_z(body):
        def step(z, _):
            body(z)
            return 0

        lax.fori_loop(0, NZ, step, 0)

    def each_gp(body):
        def step(gp, _):
            body(gp)
            return 0

        lax.fori_loop(0, 3, step, 0)

    load_spectrum.start()
    for chunk in CHUNKS:
        for mg in chunk:
            load_table(mg).start()
    load_weight.start()
    load_rows.start()
    greet(("lat", "lon"))
    load_spectrum.wait()
    for c in range(2):
        for mg in CHUNKS[c]:
            load_table(mg).wait()
            analyse(mg, spectrum, lambda m, at, mg=mg: table_l[4 * mg + m, at, :], all_ref)
        each_z(lambda z, c=c: analysis_rows(z, c, all_ref, out_c))
        copy = row_copy(c, out_c, got_c, c_send, c_recv)
        for d in OTHERS:
            copy(d).start()
        own_copy(c, out_c, got_c, 0).start()
    inverse_waves(basis_ref, table_ref)
    load_weight.wait()
    load_rows.wait()
    each_gp(lambda gp: residual(gp, rows, acc_ref))
    for c in range(2):
        copy = row_copy(c, out_c, got_c, c_send, c_recv)
        own_copy(c, out_c, got_c, 0).wait()
        for d in OTHERS:
            copy(d).wait()
        filter_chunk(c, got_c, weight, out_f, in_ref, out_ref)
        copy = row_copy(c, out_f, got_f, f_send, f_recv)
        for d in OTHERS:
            copy(d).start()
        own_copy(c, out_f, got_f, 1).start()
    for c in range(2):
        copy = row_copy(c, out_f, got_f, f_send, f_recv)
        own_copy(c, out_f, got_f, 1).wait()
        for d in OTHERS:
            copy(d).wait()
        each_z(lambda z, c=c: synthesis_rows(z, c, got_f, all_ref))
        for mg in CHUNKS[c]:
            synthesise(mg, lambda m, at, mg=mg: table_l[4 * mg + m, at, :], all_ref, out_u)

        def send(gp, c=c):
            for d in OTHERS:
                wave_copy(c, gp, d).start()
            own_wave(c, gp).start()

        each_gp(send)
    for c in range(2):

        def finish(gp, c=c):
            own_wave(c, gp).wait()
            for d in OTHERS:
                wave_copy(c, gp, d).wait()
            inverse_part(c, gp, got_u, table_ref, wide_ref, rows_ref, lhs_ref, acc_ref)
            if c == 1:
                emit(gp, acc_ref, o_ref)

        each_gp(finish)


def backward(*operands):
    rows = pltpu.VMEM((NZ, ROWS, 128), BF16)
    waves = pltpu.VMEM((2, 3, NA, 4, 16, 128), BF16)
    pairs = pltpu.SemaphoreType.DMA((2, 16))
    return pl.pallas_call(
        backward_kernel,
        out_shape=jax.ShapeDtypeStruct((JD, 16, NLON), BF16),
        in_specs=[ANY] * 4 + [VM],
        out_specs=VM,
        scratch_shapes=[
            pltpu.VMEM((3, NA, 8, 16, 128), BF16),
            pltpu.VMEM((32, MODES, JH), BF16),
            pltpu.VMEM((NA, 2, CH, CH), BF16),
            pltpu.VMEM((6, NZ, NP, 128), BF16),
            pltpu.VMEM((8, MODES, 128), F32),
            rows,
            rows,
            rows,
            rows,
            pltpu.VMEM((2, ROWS * 8, 128), F32),
            pltpu.VMEM((2, ROWS * 8, 128), F32),
            waves,
            waves,
            pltpu.VMEM((KB, NLON), BF16),
            pltpu.VMEM((128, 128), F32),
            pltpu.VMEM((2, 512, 128), F32),
            pltpu.VMEM((256, 512), BF16),
            pltpu.VMEM((3, 256, 1536), F32),
            pltpu.SemaphoreType.DMA((11,)),
            pltpu.SemaphoreType.DMA((4, 3)),
            pairs,
            pairs,
            pairs,
            pairs,
            pltpu.SemaphoreType.DMA((2, 3, 16)),
            pltpu.SemaphoreType.DMA((2, 3, 16)),
        ],
        cost_estimate=pl.CostEstimate(
            flops=8_000_000_000, bytes_accessed=30_000_000, transcendentals=0
        ),
        compiler_params=pltpu.CompilerParams(
            collective_id=2, has_side_effects=True, vmem_limit_bytes=LIMIT
        ),
    )(*operands)


def legendre_inputs(lat_index):
    slot = jnp.arange(32, dtype=jnp.int32)
    orders = (32 * (slot // 2) + 2 * lat_index + slot % 2).astype(F32)
    column = jnp.arange(JH, dtype=jnp.int32)
    local = column // 128 * 16 + column % 16
    theta = jnp.pi * ((column // 16 % 8 * JD + local).astype(F32) + 0.5) / NLAT
    real = local < JD
    cosine = jnp.where(real, jnp.cos(theta), 0.0)
    log_sine = jnp.log(jnp.where(real, jnp.sin(theta), 1.0))
    counts = jnp.arange(1, MODES + 1, dtype=F32)
    ratios = jnp.log((2.0 * counts - 1.0) / (2.0 * counts))
    partial_log = jnp.sum(jnp.where(counts[None, :] <= orders[:, None], ratios[None, :], 0.0), axis=1)
    start_log = (
        orders[:, None] * log_sine[None, :]
        + 0.5 * jnp.log(orders + 0.5)[:, None]
        + 0.5 * partial_log[:, None]
    )
    start_log = jnp.where(real[None, :], start_log, -1e9)
    return (
        jnp.broadcast_to(orders.reshape(4, 8, 1), (4, 8, 128)),
        jnp.broadcast_to(cosine[None, :], (8, JH)),
        start_log.reshape(4, 8, JH),
    )


def spectrum_weights(lat_index):
    local = jnp.arange(6 * 128, dtype=jnp.int32) // 16
    band = jnp.minimum(lat_index, 15 - lat_index)
    theta = jnp.pi * ((band * JD + local).astype(F32) + 0.5) / NLAT
    weights = jnp.pi / NLAT * jnp.sin(theta) / NLON
    return jnp.where(local < JD, weights, 0.0).reshape(3, 1, 256)


def on_device(grid, norm_gain, mlp_in, mlp_out, filter_weight):
    lat_index = lax.axis_index("lat")
    weight = lax.all_gather(filter_weight, "lat")
    rows, spectrum, table = forward(
        grid.transpose(1, 2, 0),
        norm_gain.reshape(1, CH),
        mlp_in,
        mlp_out,
        forward_basis(),
        spectrum_weights(lat_index),
        *legendre_inputs(lat_index),
    )
    updated = backward(spectrum, table, weight, rows, inverse_basis())
    return updated.transpose(1, 0, 2)


def solution(mesh):
    return jax.shard_map(
        on_device,
        mesh=mesh,
        in_specs=(P("batch", "lat", "lon"), P(), P(), P(), P(("lat", "lon"), None, None)),
        out_specs=P(("batch", "lon"), "lat", None),
        check_vma=False,
    )
```

```python
import functools

import jax
import jax.numpy as jnp
from jax import lax
from jax.experimental import pallas as pl
from jax.experimental.pallas import tpu as pltpu
from jax.sharding import PartitionSpec as P

F32 = jnp.float32
BF16 = jnp.bfloat16

CH = 256
HID = 512
JD = 45
JP = 48
ND = 90
NP = 96
NLAT = 720
NLON = 1440
MODES = 512
NA = 16
NZ = 16
JH = NA * JP // 2
LAST = JD - 1
KB = 2 * MODES
ROWS = 144
LIMIT = 58 * 1024 * 1024
MESH = pl.DeviceIdType.MESH
OTHERS = (8, 7, 9, 6, 10, 5, 11, 4, 12, 3, 13, 2, 14, 1, 15)
CHUNKS = ((0, 4), (1, 7), (2, 6), (3, 5))
SLOTS = ((0, 4), (1,), (2,), (3,))
BASE = {0: 0, 4: 32, 1: 48, 2: 80, 3: 112}
SPAN = ((0, 48), (48, 32), (80, 32), (112, 32))
TAIL = 64
LEG = (0, 4096, 7168, 9216)


def swap_blocks(xs):
    block = lax.broadcasted_iota(jnp.int32, xs[0].shape, 1) // 16
    for bit in (1, 2, 4):
        upper = (block & bit) != 0
        new = list(xs)
        for i in range(8):
            if i & bit == 0:
                low, high = xs[i], xs[i | bit]
                new[i] = jnp.where(upper, pltpu.roll(high, 16 * bit, 1), low)
                new[i | bit] = jnp.where(upper, high, pltpu.roll(low, 128 - 16 * bit, 1))
        xs = new
    return xs


def announce(axes):
    barrier = pltpu.get_barrier_semaphore()
    for axis in axes:
        me = lax.axis_index(axis)
        for d in range(1, 16):
            pl.semaphore_signal(
                barrier, inc=1, device_id={axis: lax.rem(me + d, 16)}, device_id_type=MESH
            )
    return barrier


def to_peer(axis, d, src, dst, send, recv):
    peer = lax.rem(lax.axis_index(axis) + d, 16)
    return pltpu.make_async_remote_copy(
        src_ref=src(peer),
        dst_ref=dst,
        send_sem=send,
        recv_sem=recv,
        device_id={axis: peer},
        device_id_type=MESH,
    )


def band_row(jj):
    jj = jnp.minimum(jj, LAST)
    return jnp.where(lax.axis_index("lat") >= 8, LAST - jj, jj)


def mlp_chunk(g, x_ref, gain_ref, in_ref, out_w_ref, o_ref, pad_ref, mix_ref):
    for j in range(8):
        pad_ref[j * NP : j * NP + ND, :] = x_ref[band_row(8 * g + j)].astype(F32)
    half = 2 * NP
    for part in range(4):
        rows = slice(part * half, (part + 1) * half)
        x = pad_ref[rows, :]
        mean = jnp.mean(x, axis=1, keepdims=True)
        centered = x - mean
        spread = jnp.mean(centered * centered, axis=1, keepdims=True)
        normed = (centered * lax.rsqrt(spread + 1e-05) * gain_ref[...]).astype(BF16)
        hidden = jnp.dot(normed, in_ref[...], preferred_element_type=F32)
        hidden = jax.nn.gelu(hidden).astype(BF16)
        mixed = x + jnp.dot(hidden, out_w_ref[...], preferred_element_type=F32)
        mix_ref[0, rows, :] = mixed[:, :128]
        mix_ref[1, rows, :] = mixed[:, 128:]
    lane = lax.broadcasted_iota(jnp.int32, (16, 128), 1)
    row = lax.broadcasted_iota(jnp.int32, (16, 128), 0)
    live = lane // 16 < JD - 8 * g

    def place(step, _):
        start = pl.multiple_of(step * 16, 16)
        keep = jnp.logical_and(live, row < ND - start)
        for h in range(2):
            xs = [mix_ref[h, pl.ds(pl.multiple_of(j * NP + start, 16), 16), :] for j in range(8)]
            for z, y in enumerate(swap_blocks(xs)):
                o_ref[g, h * 8 + z, pl.ds(start, 16), :] = jnp.where(keep, y, 0.0).astype(BF16)
        return 0

    lax.fori_loop(0, NP // 16, place, 0)


def pack_tail(z, x_ref, o_ref):
    x = x_ref[5, z].astype(F32)
    low, high = x[:48], x[48:]
    block = lax.broadcasted_iota(jnp.int32, (48, 128), 1) // 16
    o_ref[z, :48, :] = jnp.where(block < 5, low, pltpu.roll(high, 80, 1)).astype(BF16)
    block = lax.broadcasted_iota(jnp.int32, (16, 128), 1) // 16
    rest = jnp.zeros((16, 128), F32)
    for b in (3, 4):
        for k in range(3):
            to = 3 * (b - 3) + k
            part = high[16 * k : 16 * k + 16]
            rest = jnp.where(block == to, pltpu.roll(part, (to - b) * 16 % 128, 1), rest)
    o_ref[z, 48:, :] = rest.astype(BF16)


def unpack_tail(z, x_ref, o_ref):
    x = x_ref[z].astype(F32)
    first, rest = x[:48], x[48:]
    block = lax.broadcasted_iota(jnp.int32, (48, 128), 1) // 16
    o_ref[5, z, :48, :] = jnp.where(block < 5, first, 0.0).astype(BF16)
    high = jnp.where(block < 3, pltpu.roll(first, 48, 1), 0.0)
    block = lax.broadcasted_iota(jnp.int32, (16, 128), 1) // 16
    for k in range(3):
        part = high[16 * k : 16 * k + 16]
        for b in (3, 4):
            held = 3 * (b - 3) + k
            part = jnp.where(block == b, pltpu.roll(rest, (b - held) * 16 % 128, 1), part)
        o_ref[5, z, 48 + 16 * k : 64 + 16 * k, :] = part.astype(BF16)


def wave_tile(group, basis_ref, high, low):
    group_cos, group_sin = basis_ref[group], basis_ref[group + 1]
    high_cos = basis_ref[2, pl.ds(high, 1), :]
    high_sin = basis_ref[3, pl.ds(high, 1), :]
    low_cos = basis_ref[0, low : low + 1, :]
    low_sin = basis_ref[1, low : low + 1, :]
    c = high_cos * low_cos - high_sin * low_sin
    s = high_sin * low_cos + high_cos * low_sin
    return group_cos * c - group_sin * s, -(group_sin * c + group_cos * s)


def forward_waves(basis_ref, o_ref):
    def step(high, _):
        for low in range(8):
            tile = wave_tile(4, basis_ref, high, low)
            offset = 8 * high + low
            start = offset // 2 % 16 * 64 + offset // 32 * 32 + low % 2 * 16
            o_ref[pl.ds(pl.multiple_of(start, 16), 16), :] = jnp.concatenate(tile, axis=0).astype(
                BF16
            )
        return 0

    lax.fori_loop(0, 8, step, 0)


def inverse_waves(basis_ref, o_ref):
    row = lax.broadcasted_iota(jnp.int32, (8, NLON), 0)

    def step(high, _):
        for low in range(2):
            for c in range(4):
                real, imag = wave_tile(4 + 2 * c, basis_ref, high, low)
                if low == 0 and c == 0:
                    real = jnp.where(jnp.logical_and(high == 0, row == 0), 0.5 * real, real)
                start = c * 256 + high % 4 * 64 + high // 4 * 32 + low * 16
                o_ref[pl.ds(pl.multiple_of(start, 16), 16), :] = jnp.concatenate(
                    [real, imag], axis=0
                ).astype(BF16)
        return 0

    lax.fori_loop(0, 8, step, 0)


def put_basis(k, o_ref, multiple, points, factor):
    phase = multiple.astype(F32) * points
    phase = phase - NLON * jnp.floor(phase * (1.0 / NLON))
    angle = 2.0 * jnp.pi / NLON * phase
    o_ref[k] = jnp.cos(angle) * factor
    o_ref[k + 1] = jnp.sin(angle) * factor


def forward_basis(o_ref):
    count = lax.broadcasted_iota(jnp.int32, (8, NZ * NP), 0)
    column = lax.broadcasted_iota(jnp.int32, (8, NZ * NP), 1).astype(F32)
    z = jnp.floor((column + 0.5) * (1.0 / NP))
    n = column - NP * z
    points = ND * z + n
    put_basis(0, o_ref, count, points, 1.0)
    put_basis(2, o_ref, 8 * count, points, 1.0)
    put_basis(4, o_ref, 64 * count, points, jnp.where(n < ND, 1.0, 0.0))


def inverse_basis(o_ref):
    count = lax.broadcasted_iota(jnp.int32, (8, NLON), 0)
    points = lax.broadcasted_iota(jnp.int32, (8, NLON), 1).astype(F32)
    put_basis(0, o_ref, count, points, 1.0)
    put_basis(2, o_ref, 8 * count, points, 1.0)
    for c, (first, second) in enumerate(CHUNKS):
        multiple = jnp.where(count % 2 == 0, 64 * first, 64 * second) + count // 2 * 2
        put_basis(4 + 2 * c, o_ref, multiple, points, 2.0)


def dft_half(g, gg, x_ref, table_ref, acc_ref):
    lat = lax.axis_index("lat")
    band = jnp.minimum(lat, 15 - lat)
    local = lax.broadcasted_iota(jnp.int32, (8, 128), 1) // 16 + 8 * g
    theta = jnp.pi * ((local + band * JD).astype(F32) + 0.5) / NLAT
    weights = jnp.pi / NLAT * jnp.sin(theta) / NLON
    weights = jnp.where(local < JD, weights, 0.0)[:1]
    x = x_ref[g].reshape(NZ * NP, 128)
    for part in range(4):
        rows = slice(part * 256, (part + 1) * 256)
        acc = jnp.dot(table_ref[rows, :], x, preferred_element_type=F32)
        acc_ref[gg, rows, :] = acc * weights


def dft_place(gp, a, acc_ref, swap_ref, o_ref):
    for gg in range(2):
        xs = [acc_ref[gg, pl.ds(pl.multiple_of(a * 64 + mr * 8, 8), 8), :] for mr in range(8)]
        for j, y in enumerate(swap_blocks(xs)):
            swap_ref[pl.ds(gg * 8 + j, 8, stride=16), :] = y
    o_ref[gp, a] = swap_ref[...].astype(BF16).reshape(8, 16, 128)


def legendre_orders(q, width):
    row = lax.broadcasted_iota(jnp.int32, (8, width), 0)
    order = 128 * q + row // 4 * 64 + row // 2 % 2 * 32 + row % 2
    return (order + 2 * lax.axis_index("lat")).astype(F32)


def legendre_start(cos_ref, scale_ref):
    column = lax.broadcasted_iota(jnp.int32, (8, JH), 1)
    local = column // 128 * 16 + column % 16
    theta = jnp.pi * ((column // 16 % 8 * JD + local).astype(F32) + 0.5) / NLAT
    real = local < JD
    cos_ref[...] = jnp.where(real, jnp.cos(theta), 0.0)
    log_sine = jnp.log(jnp.where(real, jnp.sin(theta), 1.0))
    counts = (lax.broadcasted_iota(jnp.int32, (8, MODES), 1) + 1).astype(F32)
    ratios = jnp.log((2.0 * counts - 1.0) / (2.0 * counts))
    for q in range(4):
        partial_log = jnp.sum(
            jnp.where(counts <= legendre_orders(q, MODES), ratios, 0.0), axis=1, keepdims=True
        )
        order = legendre_orders(q, JH)
        start_log = order * log_sine + 0.5 * jnp.log(order + 0.5) + 0.5 * partial_log
        scale_ref[q] = jnp.where(real, start_log, -1e9)


def legendre_rows(mg, m, rows):
    q = mg // 2
    base = LEG[q] + (mg % 2 * 4 + m) * (MODES - 128 * q) - 128 * q
    return slice(base + rows.start, base + rows.stop)


def legendre_group(q, i, cos_ref, o_ref, up_ref, low_ref, scale_ref, swap_ref):
    order = legendre_orders(q, 128)
    degree = lax.broadcasted_iota(jnp.int32, (8, 128), 1) + 16 * i
    degree = degree.astype(F32)
    active = degree > order
    second = degree > order + 1.0
    grow = jnp.sqrt(
        jnp.where(active, 4.0 * degree * degree - 1.0, 0.0)
        / jnp.where(active, degree * degree - order * order, 1.0)
    )
    before = degree - 1.0
    damp = grow * jnp.sqrt(
        jnp.where(second, before * before - order * order, 0.0)
        / jnp.where(second, 4.0 * before * before - 1.0, 1.0)
    )
    first = jnp.where(degree == order, 1.0, 0.0)
    up, low, scale_log = up_ref[q], low_ref[q], scale_ref[q]
    root = jnp.exp(0.5 * scale_log)
    cosine = cos_ref[...]
    for s in range(16):
        a = jnp.broadcast_to(grow[:, s : s + 1], (8, JH))
        b = jnp.broadcast_to(damp[:, s : s + 1], (8, JH))
        e = jnp.broadcast_to(first[:, s : s + 1], (8, JH))
        fresh = a * (cosine * up) - b * low + e
        low = up
        up = fresh
        value = fresh * root * root
        for k in range(3):
            swap_ref[q, k, s * 8 : s * 8 + 8, :] = value[:, k * 128 : k * 128 + 128]
    largest = jnp.maximum(jnp.abs(up), jnp.abs(low))
    largest = jnp.where(largest > 0.0, largest, 1.0)
    up_ref[q] = up / largest
    low_ref[q] = low / largest
    scale_ref[q] = scale_log + jnp.log(largest)
    for m in range(8):
        base = LEG[q] + m * (MODES - 128 * q) - 128 * q
        start = pl.multiple_of(base + i * 16, 16)
        for k in range(3):
            o_ref[pl.ds(start, 16), k * 128 : k * 128 + 128] = swap_ref[
                q, k, pl.ds(m, 16, stride=8), :
            ].astype(BF16)


def legendre(cos_ref, o_ref, up_ref, low_ref, scale_ref, swap_ref):
    up_ref[...] = jnp.zeros_like(up_ref)
    low_ref[...] = jnp.zeros_like(low_ref)
    legendre_start(cos_ref, scale_ref)
    for stage in range(4):

        def step(i, _, stage=stage):
            for q in range(stage + 1):
                legendre_group(q, i, cos_ref, o_ref, up_ref, low_ref, scale_ref, swap_ref)
            return 0

        lax.fori_loop(8 * stage, 8 * stage + 8, step, 0)


def analyse(mg, x_ref, table_ref, all_ref):
    north, south = [], []
    for gp in range(3):
        north.append(x_ref[gp, :8, mg].reshape(128, 128).astype(F32))
        south.append(jnp.concatenate([x_ref[gp, 15 - a, mg] for a in range(8)], axis=0).astype(F32))
    north = jnp.concatenate(north, axis=0)
    south = jnp.concatenate(south, axis=0)
    both = jnp.concatenate([north + south, north - south], axis=1).astype(BF16)
    block = lax.broadcasted_iota(jnp.int32, (128, 128), 1) // 32
    odd = lax.broadcasted_iota(jnp.int32, (128, 128), 0) % 2 == 1
    for lb in range(mg // 2, 4):
        rows = slice(lb * 128, lb * 128 + 128)
        total = jnp.zeros((128, 128), F32)
        for m in range(4):
            entries = table_ref[legendre_rows(mg, m, rows), :]
            part = jnp.dot(entries, both, preferred_element_type=F32)
            first, second = part[:, :128], part[:, 128:]
            if m % 2:
                first, second = second, first
            total = jnp.where(block == m, jnp.where(odd, second, first), total)
        all_ref[mg, rows, :] = total


def analysis_rows(z, chunk, all_ref, o_ref):
    row = lax.broadcasted_iota(jnp.int32, (16, 128), 0)
    kept = []
    for t in range(2):
        where = pl.ds(2 * z + t, 16, stride=32)
        for s in SLOTS[chunk]:
            x = all_ref[s, where, :]
            if s == 4:
                kept.append(x[8:])
                continue
            if s:
                x = jnp.where(row < 2 * s, pltpu.roll(all_ref[8 - s, where, :], 2 * s, 0), x)
            start = BASE[s] + t * 16
            o_ref[z, start : start + 16, :] = x.astype(BF16)
    if kept:
        o_ref[z, 32:48, :] = jnp.concatenate(kept, axis=0).astype(BF16)


def filter_row(mg, a, t):
    if mg < 4:
        return BASE[mg] + 16 * t + a
    if mg == 4:
        return BASE[4] + 8 * t + a - 8
    return BASE[8 - mg] + 16 * t + a - 2 * mg


def filter_chunk(chunk, x_ref, w_ref, o_ref, in_ref, out_ref):
    begin, count = SPAN[chunk]

    def gather(step, _):
        start = pl.multiple_of(begin + step * 16, 16)
        for h in range(2):
            xs = [x_ref[h * 8 + z, pl.ds(start, 16), :].astype(F32) for z in range(8)]
            for mr, y in enumerate(swap_blocks(xs)):
                in_ref[h, pl.ds(start * 8 + mr, 16, stride=8), :] = y
        return 0

    lax.fori_loop(0, count // 16, gather, 0)
    for a in range(16):
        for t in range(2):
            rows = [8 * filter_row(mg, a, t) for mg in CHUNKS[chunk] if mg <= a // 2]
            if not rows:
                continue
            x = jnp.concatenate(
                [
                    jnp.concatenate([in_ref[h, r : r + 8, :] for r in rows], axis=0)
                    for h in range(2)
                ],
                axis=1,
            ).astype(BF16)
            y = jnp.dot(x, w_ref[a, t], preferred_element_type=F32)
            for i, r in enumerate(rows):
                for h in range(2):
                    out_ref[h, r : r + 8, :] = y[i * 8 : i * 8 + 8, h * 128 : h * 128 + 128]

    def scatter(step, _):
        start = pl.multiple_of(begin + step * 16, 16)
        for h in range(2):
            xs = [out_ref[h, pl.ds(start * 8 + mr, 16, stride=8), :] for mr in range(8)]
            for z, y in enumerate(swap_blocks(xs)):
                o_ref[h * 8 + z, pl.ds(start, 16), :] = y.astype(BF16)
        return 0

    lax.fori_loop(0, count // 16, scatter, 0)


def synthesis_rows(z, chunk, x_ref, all_ref):
    row = lax.broadcasted_iota(jnp.int32, (16, 128), 0)
    for s in SLOTS[chunk]:
        for t in range(2):
            where = pl.ds(2 * z + t, 16, stride=32)
            if s == 4:
                last = x_ref[z, 32:48, :].astype(F32)
                x = jnp.concatenate([jnp.zeros((8, 128), F32), last[t * 8 : t * 8 + 8]], axis=0)
                all_ref[4, where, :] = x
                continue
            start = BASE[s] + t * 16
            x = x_ref[z, start : start + 16, :].astype(F32)
            if s:
                all_ref[8 - s, where, :] = jnp.where(
                    row >= 16 - 2 * s, pltpu.roll(x, 16 - 2 * s, 0), 0.0
                )
                x = jnp.where(row >= 2 * s, x, 0.0)
            all_ref[s, where, :] = x


def synthesise(chunk, place, table_ref, all_ref, o_ref):
    mg = CHUNKS[chunk][place]
    low = mg // 2 * 128
    block = lax.broadcasted_iota(jnp.int32, (MODES - low, 128), 1) // 32
    row = lax.broadcasted_iota(jnp.int32, (MODES - low, 128), 0)
    same = (block + row) % 2 == 0
    x = all_ref[mg, low:, :]
    even = jnp.where(same, x, 0.0).T.astype(BF16)
    odd = jnp.where(same, 0.0, x).T.astype(BF16)
    evens, odds = [], []
    for m in range(4):
        rows = slice(m * 32, m * 32 + 32)
        both = jnp.concatenate([even[rows], odd[rows]], axis=0)
        entries = table_ref[legendre_rows(mg, m, slice(low, MODES)), :]
        part = jnp.dot(both, entries, preferred_element_type=F32)
        evens.append(part[:32])
        odds.append(part[32:])
    even = jnp.concatenate(evens, axis=0).T
    odd = jnp.concatenate(odds, axis=0).T
    north = (even + odd).astype(BF16)
    south = (even - odd).astype(BF16)
    for gp in range(3):
        for a in range(8):
            rows = slice(gp * 128 + a * 16, gp * 128 + a * 16 + 16)
            o_ref[chunk, a, gp, place] = north[rows]
            o_ref[chunk, 15 - a, gp, place] = south[rows]


def residual(gp, x_ref, acc_ref):
    row = lax.broadcasted_iota(jnp.int32, (NP, 256), 0)
    lane = lax.broadcasted_iota(jnp.int32, (NP, 256), 1)
    acc_ref[gp] = jnp.zeros(acc_ref.shape[1:], F32)
    for z in range(NZ):
        begin = ND * z // 128 * 128
        pick = jnp.logical_and(lane == row + (ND * z - begin), row < ND)
        pick = jnp.where(pick, 1.0, 0.0).astype(BF16)
        x = jnp.concatenate([x_ref[2 * gp + gg, z].astype(F32).T for gg in range(2)], axis=0)
        acc_ref[gp, :, begin : begin + 256] += jnp.dot(
            x.astype(BF16), pick, preferred_element_type=F32
        )


def inverse_part(chunk, gp, u_ref, table_ref, wide_ref, rows_ref, lhs_ref, acc_ref):
    def place(w, _):
        wide_ref[...] = u_ref[chunk, pl.ds(4 * w, 4), gp].reshape(128, 128).astype(F32)
        for gg in range(2):
            xs = [wide_ref[pl.ds(gg * 8 + j, 8, stride=16), :] for j in range(8)]
            for mr, y in enumerate(swap_blocks(xs)):
                rows_ref[gg, pl.ds(pl.multiple_of(w * 64 + mr * 8, 8), 8), :] = y
        return 0

    lax.fori_loop(0, 4, place, 0)
    for gg in range(2):
        for k in range(2):
            cols = slice(k * 128, (k + 1) * 128)
            lhs_ref[gg * 128 : gg * 128 + 128, cols] = rows_ref[gg, cols, :].T.astype(BF16)
    waves = slice(chunk * 256, chunk * 256 + 256)
    for part in range(2):
        rows = slice(part * 128, part * 128 + 128)
        acc_ref[gp, rows, :NLON] += jnp.dot(
            lhs_ref[rows, :], table_ref[waves, :], preferred_element_type=F32
        )


def emit(gp, acc_ref, o_ref):
    for j in range(16):

        @pl.when(16 * gp + j < JD)
        def _(j=j):
            o_ref[band_row(16 * gp + j)] = acc_ref[gp, 16 * j : 16 * j + 16, :NLON].astype(BF16)


VM = pl.BlockSpec(memory_space=pltpu.VMEM)
ANY = pl.BlockSpec(memory_space=pl.ANY)
SCRATCH = {
    "points": pltpu.VMEM((JD, ND, CH), BF16),
    "pad": pltpu.VMEM((8 * NP, CH), F32),
    "mix": pltpu.VMEM((2, 8 * NP, 128), F32),
    "out_rows": pltpu.VMEM((6, NZ, NP, 128), BF16),
    "got_rows": pltpu.VMEM((6, NZ, NP, 128), BF16),
    "out_tail": pltpu.VMEM((NZ, TAIL, 128), BF16),
    "got_tail": pltpu.VMEM((NZ, TAIL, 128), BF16),
    "basis_f": pltpu.VMEM((6, 8, NZ * NP), F32),
    "basis_i": pltpu.VMEM((12, 8, NLON), F32),
    "waves_f": pltpu.VMEM((KB, NZ * NP), BF16),
    "waves_i": pltpu.VMEM((KB, NLON), BF16),
    "acc_f": pltpu.VMEM((2, KB, 128), F32),
    "swap_f": pltpu.VMEM((128, 128), F32),
    "out_spectrum": pltpu.VMEM((3, NA, 8, 16, 128), BF16),
    "got_spectrum": pltpu.VMEM((3, NA, 8, 16, 128), BF16),
    "table": pltpu.VMEM((10240, JH), BF16),
    "cosine": pltpu.VMEM((8, JH), F32),
    "up": pltpu.VMEM((4, 8, JH), F32),
    "low": pltpu.VMEM((4, 8, JH), F32),
    "scale": pltpu.VMEM((4, 8, JH), F32),
    "swap_l": pltpu.VMEM((4, 3, 128, 128), F32),
    "weight": pltpu.VMEM((NA, 2, CH, CH), BF16),
    "every": pltpu.VMEM((8, MODES, 128), F32),
    "out_c": pltpu.VMEM((NZ, ROWS, 128), BF16),
    "got_c": pltpu.VMEM((NZ, ROWS, 128), BF16),
    "out_f": pltpu.VMEM((NZ, ROWS, 128), BF16),
    "got_f": pltpu.VMEM((NZ, ROWS, 128), BF16),
    "wide_in": pltpu.VMEM((2, ROWS * 8, 128), F32),
    "wide_out": pltpu.VMEM((2, ROWS * 8, 128), F32),
    "out_u": pltpu.VMEM((4, NA, 3, 2, 16, 128), BF16),
    "got_u": pltpu.VMEM((4, NA, 3, 2, 16, 128), BF16),
    "wide_u": pltpu.VMEM((128, 128), F32),
    "rows_u": pltpu.VMEM((2, 256, 128), F32),
    "lhs_u": pltpu.VMEM((256, 256), BF16),
    "acc_u": pltpu.VMEM((3, 256, 1536), F32),
    "load": pltpu.SemaphoreType.DMA((2,)),
    "own": pltpu.SemaphoreType.DMA((5, 6)),
    "r_send": pltpu.SemaphoreType.DMA((6, 16)),
    "r_recv": pltpu.SemaphoreType.DMA((6, 16)),
    "s_send": pltpu.SemaphoreType.DMA((3, 16)),
    "s_recv": pltpu.SemaphoreType.DMA((3, 16)),
    "w_send": pltpu.SemaphoreType.DMA((16,)),
    "w_recv": pltpu.SemaphoreType.DMA((16,)),
    "c_send": pltpu.SemaphoreType.DMA((4, 16)),
    "c_recv": pltpu.SemaphoreType.DMA((4, 16)),
    "f_send": pltpu.SemaphoreType.DMA((4, 16)),
    "f_recv": pltpu.SemaphoreType.DMA((4, 16)),
    "u_send": pltpu.SemaphoreType.DMA((4, 16)),
    "u_recv": pltpu.SemaphoreType.DMA((4, 16)),
}


def each(low, high, body):
    def step(i, _):
        body(i)
        return 0

    lax.fori_loop(low, high, step, 0)


def block_kernel(points_any, gain_ref, in_ref, out_ref, weight_any, o_ref, *scratch):
    v = dict(zip(SCRATCH, scratch))
    lat = lax.axis_index("lat")
    lon = lax.axis_index("lon")
    own = v["own"]

    def rows_copy(g, d):
        return to_peer(
            "lon",
            d,
            lambda peer: v["out_rows"].at[g, peer],
            v["got_rows"].at[g, lon],
            v["r_send"].at[g, d],
            v["r_recv"].at[g, d],
        )

    def own_rows(g):
        return pltpu.make_async_copy(
            v["out_rows"].at[g, lon], v["got_rows"].at[g, lon], own.at[0, g]
        )

    def tail_copy(d):
        return to_peer(
            "lon",
            d,
            lambda peer: v["out_tail"].at[peer],
            v["got_tail"].at[lon],
            v["r_send"].at[5, d],
            v["r_recv"].at[5, d],
        )

    own_tail = pltpu.make_async_copy(v["out_tail"].at[lon], v["got_tail"].at[lon], own.at[0, 5])

    def spectrum_copy(gp, d):
        return to_peer(
            "lat",
            d,
            lambda peer: v["out_spectrum"].at[gp, peer],
            v["got_spectrum"].at[gp, lat],
            v["s_send"].at[gp, d],
            v["s_recv"].at[gp, d],
        )

    def own_spectrum(gp):
        return pltpu.make_async_copy(
            v["out_spectrum"].at[gp, lat], v["got_spectrum"].at[gp, lat], own.at[1, gp]
        )

    def weight_copy(d):
        return to_peer(
            "lat",
            d,
            lambda peer: weight_any,
            v["weight"].at[lat],
            v["w_send"].at[d],
            v["w_recv"].at[d],
        )

    own_weight = pltpu.make_async_copy(weight_any, v["weight"].at[lat], v["load"].at[1])

    def mode_copy(c, name, d):
        part = pl.ds(*SPAN[c])
        return to_peer(
            "lon",
            d,
            lambda peer: v["out_" + name].at[peer, part],
            v["got_" + name].at[lon, part],
            v[name + "_send"].at[c, d],
            v[name + "_recv"].at[c, d],
        )

    def own_modes(c, name):
        part = pl.ds(*SPAN[c])
        return pltpu.make_async_copy(
            v["out_" + name].at[lon, part],
            v["got_" + name].at[lon, part],
            own.at[2 if name == "c" else 3, c],
        )

    def u_copy(c, d):
        return to_peer(
            "lat",
            d,
            lambda peer: v["out_u"].at[c, peer],
            v["got_u"].at[c, lat],
            v["u_send"].at[c, d],
            v["u_recv"].at[c, d],
        )

    def own_u(c):
        return pltpu.make_async_copy(v["out_u"].at[c, lat], v["got_u"].at[c, lat], own.at[4, c])

    def mlp_step(g):
        mlp_chunk(
            g, v["points"], gain_ref, in_ref, out_ref, v["out_rows"], v["pad"], v["mix"]
        )

    def send_rows(g):
        for d in OTHERS:
            rows_copy(g, d).start()
        own_rows(g).start()

    def dft_step(g, gg):
        dft_half(g, gg, v["got_rows"], v["waves_f"], v["acc_f"])

    def got_rows(g):
        own_rows(g).wait()
        for d in OTHERS:
            rows_copy(g, d).wait_recv()

    def send_spectrum(gp):
        def one(d):
            peer = lax.rem(lat + d, 16)
            dft_place(gp, peer, v["acc_f"], v["swap_f"], v["out_spectrum"])
            spectrum_copy(gp, d).start()

        each(1, 16, one)
        dft_place(gp, lat, v["acc_f"], v["swap_f"], v["out_spectrum"])
        own_spectrum(gp).start()

    load_points = pltpu.make_async_copy(points_any, v["points"], v["load"].at[0])
    load_points.start()
    barrier = announce(("lat", "lon"))
    v["pad"][...] = jnp.zeros_like(v["pad"])
    load_points.wait()
    mlp_step(0)
    pl.semaphore_wait(barrier, 30)
    send_rows(0)

    def mlp_more(g):
        mlp_step(g)

        @pl.when(g < 5)
        def _():
            send_rows(g)

    each(1, 6, mlp_more)
    each(0, NZ, lambda z: pack_tail(z, v["out_rows"], v["out_tail"]))
    for d in OTHERS:
        tail_copy(d).start()
    own_tail.start()
    for d in OTHERS:
        weight_copy(d).start()
    own_weight.start()

    forward_basis(v["basis_f"])
    forward_waves(v["basis_f"], v["waves_f"])
    legendre(v["cosine"], v["table"], v["up"], v["low"], v["scale"], v["swap_l"])
    inverse_basis(v["basis_i"])
    inverse_waves(v["basis_i"], v["waves_i"])

    def pair(gp):
        for gg in range(2):
            got_rows(2 * gp + gg)
            dft_step(2 * gp + gg, gg)
        send_spectrum(gp)
        residual(gp, v["got_rows"], v["acc_u"])

    each(0, 2, pair)
    got_rows(4)
    dft_step(4, 0)
    own_tail.wait()
    for d in OTHERS:
        tail_copy(d).wait_recv()
    each(0, NZ, lambda z: unpack_tail(z, v["got_tail"], v["got_rows"]))
    dft_step(5, 1)
    send_spectrum(2)
    residual(2, v["got_rows"], v["acc_u"])

    def got_spectrum(gp):
        own_spectrum(gp).wait()
        for d in OTHERS:
            spectrum_copy(gp, d).wait()

    each(0, 3, got_spectrum)
    for c in range(4):
        for mg in CHUNKS[c]:
            analyse(mg, v["got_spectrum"], v["table"], v["every"])
        each(0, NZ, lambda z, c=c: analysis_rows(z, c, v["every"], v["out_c"]))
        for d in OTHERS:
            mode_copy(c, "c", d).start()
        own_modes(c, "c").start()
    own_weight.wait()
    for d in OTHERS:
        weight_copy(d).wait()
    for c in range(4):
        own_modes(c, "c").wait()
        for d in OTHERS:
            mode_copy(c, "c", d).wait()
        filter_chunk(c, v["got_c"], v["weight"], v["out_f"], v["wide_in"], v["wide_out"])
        for d in OTHERS:
            mode_copy(c, "f", d).start()
        own_modes(c, "f").start()

    def inverse_step(c, last):
        own_u(c).wait()
        for d in OTHERS:
            u_copy(c, d).wait()

        def one(gp):
            inverse_part(
                c, gp, v["got_u"], v["waves_i"], v["wide_u"], v["rows_u"], v["lhs_u"], v["acc_u"]
            )
            if last:
                emit(gp, v["acc_u"], o_ref)

        each(0, 3, one)

    for c in range(4):
        own_modes(c, "f").wait()
        for d in OTHERS:
            mode_copy(c, "f", d).wait()
        each(0, NZ, lambda z, c=c: synthesis_rows(z, c, v["got_f"], v["every"]))
        for place in range(2):
            synthesise(c, place, v["table"], v["every"], v["out_u"])
        for d in OTHERS:
            u_copy(c, d).start()
        own_u(c).start()
        if c >= 1:
            inverse_step(c - 1, False)

    def rows_sent(g):
        for d in OTHERS:
            rows_copy(g, d).wait_send()

    each(0, 5, rows_sent)
    for d in OTHERS:
        tail_copy(d).wait_send()
    inverse_step(3, True)


def on_device(grid, norm_gain, mlp_in, mlp_out, filter_weight):
    updated = pl.pallas_call(
        block_kernel,
        out_shape=jax.ShapeDtypeStruct((JD, 16, NLON), BF16),
        in_specs=[ANY, VM, VM, VM, ANY],
        out_specs=VM,
        scratch_shapes=list(SCRATCH.values()),
        cost_estimate=pl.CostEstimate(
            flops=20_000_000_000, bytes_accessed=10_000_000, transcendentals=0
        ),
        compiler_params=pltpu.CompilerParams(
            collective_id=1, has_side_effects=True, vmem_limit_bytes=LIMIT
        ),
    )(grid.transpose(1, 2, 0), norm_gain.reshape(1, CH), mlp_in, mlp_out, filter_weight)
    return updated.transpose(1, 0, 2)


def solution(mesh):
    return jax.shard_map(
        on_device,
        mesh=mesh,
        in_specs=(P("batch", "lat", "lon"), P(), P(), P(), P(("lat", "lon"), None, None)),
        out_specs=P(("batch", "lon"), "lat", None),
        check_vma=False,
    )
```

```python
import functools

import jax
import jax.numpy as jnp
from jax import lax
from jax.experimental import pallas as pl
from jax.experimental.pallas import tpu as pltpu
from jax.sharding import PartitionSpec as P

F32 = jnp.float32
BF16 = jnp.bfloat16

CH = 256
HID = 512
JD = 45
JP = 48
ND = 90
NP = 96
NLAT = 720
NLON = 1440
MODES = 512
NA = 16
NZ = 16
JH = NA * JP // 2
LAST = JD - 1
KB = 2 * MODES
ROWS = 144
LIMIT = 58 * 1024 * 1024
MESH = pl.DeviceIdType.MESH
OTHERS = (8, 7, 9, 6, 10, 5, 11, 4, 12, 3, 13, 2, 14, 1, 15)
CHUNKS = ((3, 5), (0, 4), (1, 7), (2, 6))
SLOTS = ((3,), (0, 4), (1,), (2,))
BASE = {3: 0, 0: 32, 4: 64, 1: 80, 2: 112}
SPAN = ((0, 32), (32, 48), (80, 32), (112, 32))
TAIL = 64
LEG = (0, 4096, 7168, 9216)


def swap_blocks(xs):
    block = lax.broadcasted_iota(jnp.int32, xs[0].shape, 1) // 16
    for bit in (1, 2, 4):
        upper = (block & bit) != 0
        new = list(xs)
        for i in range(8):
            if i & bit == 0:
                low, high = xs[i], xs[i | bit]
                new[i] = jnp.where(upper, pltpu.roll(high, 16 * bit, 1), low)
                new[i | bit] = jnp.where(upper, high, pltpu.roll(low, 128 - 16 * bit, 1))
        xs = new
    return xs


def announce(axes):
    barrier = pltpu.get_barrier_semaphore()
    for axis in axes:
        me = lax.axis_index(axis)
        for d in range(1, 16):
            pl.semaphore_signal(
                barrier, inc=1, device_id={axis: lax.rem(me + d, 16)}, device_id_type=MESH
            )
    return barrier


def to_peer(axis, d, src, dst, send, recv):
    peer = lax.rem(lax.axis_index(axis) + d, 16)
    return pltpu.make_async_remote_copy(
        src_ref=src(peer),
        dst_ref=dst,
        send_sem=send,
        recv_sem=recv,
        device_id={axis: peer},
        device_id_type=MESH,
    )


def band_row(jj):
    jj = jnp.minimum(jj, LAST)
    return jnp.where(lax.axis_index("lat") >= 8, LAST - jj, jj)


def mlp_chunk(g, x_ref, gain_ref, in_ref, out_w_ref, o_ref, pad_ref, mix_ref):
    for j in range(8):
        pad_ref[j * NP : j * NP + ND, :] = x_ref[band_row(8 * g + j)].astype(F32)
    half = 2 * NP
    for part in range(4):
        rows = slice(part * half, (part + 1) * half)
        x = pad_ref[rows, :]
        mean = jnp.mean(x, axis=1, keepdims=True)
        centered = x - mean
        spread = jnp.mean(centered * centered, axis=1, keepdims=True)
        normed = (centered * lax.rsqrt(spread + 1e-05) * gain_ref[...]).astype(BF16)
        hidden = jnp.dot(normed, in_ref[...], preferred_element_type=F32)
        hidden = jax.nn.gelu(hidden).astype(BF16)
        mixed = x + jnp.dot(hidden, out_w_ref[...], preferred_element_type=F32)
        mix_ref[0, rows, :] = mixed[:, :128]
        mix_ref[1, rows, :] = mixed[:, 128:]
    lane = lax.broadcasted_iota(jnp.int32, (16, 128), 1)
    row = lax.broadcasted_iota(jnp.int32, (16, 128), 0)
    live = lane // 16 < JD - 8 * g

    def place(step, _):
        start = pl.multiple_of(step * 16, 16)
        keep = jnp.logical_and(live, row < ND - start)
        for h in range(2):
            xs = [mix_ref[h, pl.ds(pl.multiple_of(j * NP + start, 16), 16), :] for j in range(8)]
            for z, y in enumerate(swap_blocks(xs)):
                o_ref[g, h * 8 + z, pl.ds(start, 16), :] = jnp.where(keep, y, 0.0).astype(BF16)
        return 0

    lax.fori_loop(0, NP // 16, place, 0)


def pack_tail(z, x_ref, o_ref):
    x = x_ref[5, z].astype(F32)
    low, high = x[:48], x[48:]
    block = lax.broadcasted_iota(jnp.int32, (48, 128), 1) // 16
    o_ref[z, :48, :] = jnp.where(block < 5, low, pltpu.roll(high, 80, 1)).astype(BF16)
    block = lax.broadcasted_iota(jnp.int32, (16, 128), 1) // 16
    rest = jnp.zeros((16, 128), F32)
    for b in (3, 4):
        for k in range(3):
            to = 3 * (b - 3) + k
            part = high[16 * k : 16 * k + 16]
            rest = jnp.where(block == to, pltpu.roll(part, (to - b) * 16 % 128, 1), rest)
    o_ref[z, 48:, :] = rest.astype(BF16)


def unpack_tail(z, x_ref, o_ref):
    x = x_ref[z].astype(F32)
    first, rest = x[:48], x[48:]
    block = lax.broadcasted_iota(jnp.int32, (48, 128), 1) // 16
    o_ref[5, z, :48, :] = jnp.where(block < 5, first, 0.0).astype(BF16)
    high = jnp.where(block < 3, pltpu.roll(first, 48, 1), 0.0)
    block = lax.broadcasted_iota(jnp.int32, (16, 128), 1) // 16
    for k in range(3):
        part = high[16 * k : 16 * k + 16]
        for b in (3, 4):
            held = 3 * (b - 3) + k
            part = jnp.where(block == b, pltpu.roll(rest, (b - held) * 16 % 128, 1), part)
        o_ref[5, z, 48 + 16 * k : 64 + 16 * k, :] = part.astype(BF16)


def wave_tile(group, basis_ref, high, low):
    group_cos, group_sin = basis_ref[group], basis_ref[group + 1]
    high_cos = basis_ref[2, pl.ds(high, 1), :]
    high_sin = basis_ref[3, pl.ds(high, 1), :]
    low_cos = basis_ref[0, low : low + 1, :]
    low_sin = basis_ref[1, low : low + 1, :]
    c = high_cos * low_cos - high_sin * low_sin
    s = high_sin * low_cos + high_cos * low_sin
    return group_cos * c - group_sin * s, -(group_sin * c + group_cos * s)


def forward_waves(basis_ref, o_ref):
    def step(high, _):
        for low in range(8):
            tile = wave_tile(4, basis_ref, high, low)
            offset = 8 * high + low
            start = offset // 2 % 16 * 64 + offset // 32 * 32 + low % 2 * 16
            o_ref[pl.ds(pl.multiple_of(start, 16), 16), :] = jnp.concatenate(tile, axis=0).astype(
                BF16
            )
        return 0

    lax.fori_loop(0, 8, step, 0)


def inverse_waves(basis_ref, o_ref):
    row = lax.broadcasted_iota(jnp.int32, (8, NLON), 0)

    def step(high, _):
        for low in range(2):
            for c in range(4):
                real, imag = wave_tile(4 + 2 * c, basis_ref, high, low)
                if low == 0 and c == 1:
                    real = jnp.where(jnp.logical_and(high == 0, row == 0), 0.5 * real, real)
                start = c * 256 + high % 4 * 64 + high // 4 * 32 + low * 16
                o_ref[pl.ds(pl.multiple_of(start, 16), 16), :] = jnp.concatenate(
                    [real, imag], axis=0
                ).astype(BF16)
        return 0

    lax.fori_loop(0, 8, step, 0)


def put_basis(k, o_ref, multiple, points, factor):
    phase = multiple.astype(F32) * points
    phase = phase - NLON * jnp.floor(phase * (1.0 / NLON))
    angle = 2.0 * jnp.pi / NLON * phase
    o_ref[k] = jnp.cos(angle) * factor
    o_ref[k + 1] = jnp.sin(angle) * factor


def forward_basis(o_ref):
    count = lax.broadcasted_iota(jnp.int32, (8, NZ * NP), 0)
    column = lax.broadcasted_iota(jnp.int32, (8, NZ * NP), 1).astype(F32)
    z = jnp.floor((column + 0.5) * (1.0 / NP))
    n = column - NP * z
    points = ND * z + n
    put_basis(0, o_ref, count, points, 1.0)
    put_basis(2, o_ref, 8 * count, points, 1.0)
    put_basis(4, o_ref, 64 * count, points, jnp.where(n < ND, 1.0, 0.0))


def inverse_basis(o_ref):
    count = lax.broadcasted_iota(jnp.int32, (8, NLON), 0)
    points = lax.broadcasted_iota(jnp.int32, (8, NLON), 1).astype(F32)
    put_basis(0, o_ref, count, points, 1.0)
    put_basis(2, o_ref, 8 * count, points, 1.0)
    for c, (first, second) in enumerate(CHUNKS):
        multiple = jnp.where(count % 2 == 0, 64 * first, 64 * second) + count // 2 * 2
        put_basis(4 + 2 * c, o_ref, multiple, points, 2.0)


def dft(g, x_ref, table_ref, acc_ref):
    lat = lax.axis_index("lat")
    band = jnp.minimum(lat, 15 - lat)
    local = lax.broadcasted_iota(jnp.int32, (8, 128), 1) // 16 + 8 * g
    theta = jnp.pi * ((local + band * JD).astype(F32) + 0.5) / NLAT
    weights = jnp.pi / NLAT * jnp.sin(theta) / NLON
    weights = jnp.where(local < JD, weights, 0.0)[:1]
    x = x_ref[g].reshape(NZ * NP, 128)
    for part in range(4):
        rows = slice(part * 256, (part + 1) * 256)
        acc = jnp.dot(table_ref[rows, :], x, preferred_element_type=F32)
        acc_ref[rows, :] = acc * weights


def dft_place(g, a, acc_ref, swap_ref, o_ref):
    xs = [acc_ref[pl.ds(pl.multiple_of(a * 64 + mr * 8, 8), 8), :] for mr in range(8)]
    for j, y in enumerate(swap_blocks(xs)):
        swap_ref[pl.ds(j, 8, stride=8), :] = y
    o_ref[g, a] = swap_ref[...].astype(BF16)


def legendre_orders(q, width):
    row = lax.broadcasted_iota(jnp.int32, (8, width), 0)
    order = 128 * q + row // 4 * 64 + row // 2 % 2 * 32 + row % 2
    return (order + 2 * lax.axis_index("lat")).astype(F32)


def legendre_start(cos_ref, scale_ref):
    column = lax.broadcasted_iota(jnp.int32, (8, JH), 1)
    local = column // 64 * 8 + column % 8
    theta = jnp.pi * ((column // 8 % 8 * JD + local).astype(F32) + 0.5) / NLAT
    real = local < JD
    cos_ref[...] = jnp.where(real, jnp.cos(theta), 0.0)
    log_sine = jnp.log(jnp.where(real, jnp.sin(theta), 1.0))
    counts = (lax.broadcasted_iota(jnp.int32, (8, MODES), 1) + 1).astype(F32)
    ratios = jnp.log((2.0 * counts - 1.0) / (2.0 * counts))
    for q in range(4):
        partial_log = jnp.sum(
            jnp.where(counts <= legendre_orders(q, MODES), ratios, 0.0), axis=1, keepdims=True
        )
        order = legendre_orders(q, JH)
        start_log = order * log_sine + 0.5 * jnp.log(order + 0.5) + 0.5 * partial_log
        scale_ref[q] = jnp.where(real, start_log, -1e9)


def legendre_rows(mg, m, rows):
    q = mg // 2
    base = LEG[q] + (mg % 2 * 4 + m) * (MODES - 128 * q) - 128 * q
    return slice(base + rows.start, base + rows.stop)


def legendre_group(q, i, cos_ref, o_ref, up_ref, low_ref, scale_ref, swap_ref):
    order = legendre_orders(q, 128)
    degree = lax.broadcasted_iota(jnp.int32, (8, 128), 1) + 16 * i
    degree = degree.astype(F32)
    active = degree > order
    second = degree > order + 1.0
    grow = jnp.sqrt(
        jnp.where(active, 4.0 * degree * degree - 1.0, 0.0)
        / jnp.where(active, degree * degree - order * order, 1.0)
    )
    before = degree - 1.0
    damp = grow * jnp.sqrt(
        jnp.where(second, before * before - order * order, 0.0)
        / jnp.where(second, 4.0 * before * before - 1.0, 1.0)
    )
    first = jnp.where(degree == order, 1.0, 0.0)
    up, low, scale_log = up_ref[q], low_ref[q], scale_ref[q]
    root = jnp.exp(0.5 * scale_log)
    cosine = cos_ref[...]
    for s in range(16):
        a = jnp.broadcast_to(grow[:, s : s + 1], (8, JH))
        b = jnp.broadcast_to(damp[:, s : s + 1], (8, JH))
        e = jnp.broadcast_to(first[:, s : s + 1], (8, JH))
        fresh = a * (cosine * up) - b * low + e
        low = up
        up = fresh
        value = fresh * root * root
        for k in range(3):
            swap_ref[q, k, s * 8 : s * 8 + 8, :] = value[:, k * 128 : k * 128 + 128]
    largest = jnp.maximum(jnp.abs(up), jnp.abs(low))
    largest = jnp.where(largest > 0.0, largest, 1.0)
    up_ref[q] = up / largest
    low_ref[q] = low / largest
    scale_ref[q] = scale_log + jnp.log(largest)
    for m in range(8):
        base = LEG[q] + m * (MODES - 128 * q) - 128 * q
        start = pl.multiple_of(base + i * 16, 16)
        for k in range(3):
            o_ref[pl.ds(start, 16), k * 128 : k * 128 + 128] = swap_ref[
                q, k, pl.ds(m, 16, stride=8), :
            ].astype(BF16)


def legendre(cos_ref, o_ref, up_ref, low_ref, scale_ref, swap_ref):
    up_ref[...] = jnp.zeros_like(up_ref)
    low_ref[...] = jnp.zeros_like(low_ref)
    legendre_start(cos_ref, scale_ref)
    for stage in range(4):

        def step(i, _, stage=stage):
            for q in range(stage + 1):
                legendre_group(q, i, cos_ref, o_ref, up_ref, low_ref, scale_ref, swap_ref)
            return 0

        lax.fori_loop(8 * stage, 8 * stage + 8, step, 0)


def analyse(mg, x_ref, table_ref, all_ref):
    north, south = [], []
    start = mg // 2 * 16
    part = slice(mg % 2 * 8, mg % 2 * 8 + 8)
    for g in range(6):
        x = x_ref[g, :, start : start + 16, :].astype(F32)[:, part]
        north.append(x[:8].reshape(64, 128))
        south += [x[15 - a] for a in range(8)]
    north = jnp.concatenate(north, axis=0)
    south = jnp.concatenate(south, axis=0)
    both = jnp.concatenate([north + south, north - south], axis=1).astype(BF16)
    block = lax.broadcasted_iota(jnp.int32, (128, 128), 1) // 32
    odd = lax.broadcasted_iota(jnp.int32, (128, 128), 0) % 2 == 1
    for lb in range(mg // 2, 4):
        rows = slice(lb * 128, lb * 128 + 128)
        total = jnp.zeros((128, 128), F32)
        for m in range(4):
            entries = table_ref[legendre_rows(mg, m, rows), :]
            part = jnp.dot(entries, both, preferred_element_type=F32)
            first, second = part[:, :128], part[:, 128:]
            if m % 2:
                first, second = second, first
            total = jnp.where(block == m, jnp.where(odd, second, first), total)
        all_ref[mg, rows, :] = total


def analysis_rows(z, chunk, all_ref, o_ref):
    row = lax.broadcasted_iota(jnp.int32, (16, 128), 0)
    kept = []
    for t in range(2):
        where = pl.ds(2 * z + t, 16, stride=32)
        for s in SLOTS[chunk]:
            x = all_ref[s, where, :]
            if s == 4:
                kept.append(x[8:])
                continue
            if s:
                x = jnp.where(row < 2 * s, pltpu.roll(all_ref[8 - s, where, :], 2 * s, 0), x)
            start = BASE[s] + t * 16
            o_ref[z, start : start + 16, :] = x.astype(BF16)
    if kept:
        o_ref[z, 64:80, :] = jnp.concatenate(kept, axis=0).astype(BF16)


def filter_row(mg, a, t):
    if mg < 4:
        return BASE[mg] + 16 * t + a
    if mg == 4:
        return BASE[4] + 8 * t + a - 8
    return BASE[8 - mg] + 16 * t + a - 2 * mg


def filter_chunk(chunk, x_ref, w_ref, o_ref, in_ref, out_ref):
    begin, count = SPAN[chunk]

    def gather(step, _):
        start = pl.multiple_of(begin + step * 16, 16)
        for h in range(2):
            xs = [x_ref[h * 8 + z, pl.ds(start, 16), :].astype(F32) for z in range(8)]
            for mr, y in enumerate(swap_blocks(xs)):
                in_ref[h, pl.ds(start * 8 + mr, 16, stride=8), :] = y
        return 0

    lax.fori_loop(0, count // 16, gather, 0)
    for a in range(16):
        for t in range(2):
            rows = [8 * filter_row(mg, a, t) for mg in CHUNKS[chunk] if mg <= a // 2]
            if not rows:
                continue
            x = jnp.concatenate(
                [
                    jnp.concatenate([in_ref[h, r : r + 8, :] for r in rows], axis=0)
                    for h in range(2)
                ],
                axis=1,
            ).astype(BF16)
            y = jnp.dot(x, w_ref[a, t], preferred_element_type=F32)
            for i, r in enumerate(rows):
                for h in range(2):
                    out_ref[h, r : r + 8, :] = y[i * 8 : i * 8 + 8, h * 128 : h * 128 + 128]

    def scatter(step, _):
        start = pl.multiple_of(begin + step * 16, 16)
        for h in range(2):
            xs = [out_ref[h, pl.ds(start * 8 + mr, 16, stride=8), :] for mr in range(8)]
            for z, y in enumerate(swap_blocks(xs)):
                o_ref[h * 8 + z, pl.ds(start, 16), :] = y.astype(BF16)
        return 0

    lax.fori_loop(0, count // 16, scatter, 0)


def synthesis_rows(z, chunk, x_ref, all_ref):
    row = lax.broadcasted_iota(jnp.int32, (16, 128), 0)
    for s in SLOTS[chunk]:
        for t in range(2):
            where = pl.ds(2 * z + t, 16, stride=32)
            if s == 4:
                last = x_ref[z, 64:80, :].astype(F32)
                x = jnp.concatenate([jnp.zeros((8, 128), F32), last[t * 8 : t * 8 + 8]], axis=0)
                all_ref[4, where, :] = x
                continue
            start = BASE[s] + t * 16
            x = x_ref[z, start : start + 16, :].astype(F32)
            if s:
                all_ref[8 - s, where, :] = jnp.where(
                    row >= 16 - 2 * s, pltpu.roll(x, 16 - 2 * s, 0), 0.0
                )
                x = jnp.where(row >= 2 * s, x, 0.0)
            all_ref[s, where, :] = x


def synthesise(chunk, place, table_ref, all_ref, o_ref):
    mg = CHUNKS[chunk][place]
    low = mg // 2 * 128
    block = lax.broadcasted_iota(jnp.int32, (MODES - low, 128), 1) // 32
    row = lax.broadcasted_iota(jnp.int32, (MODES - low, 128), 0)
    same = (block + row) % 2 == 0
    x = all_ref[mg, low:, :]
    even = jnp.where(same, x, 0.0).T.astype(BF16)
    odd = jnp.where(same, 0.0, x).T.astype(BF16)
    evens, odds = [], []
    for m in range(4):
        rows = slice(m * 32, m * 32 + 32)
        both = jnp.concatenate([even[rows], odd[rows]], axis=0)
        entries = table_ref[legendre_rows(mg, m, slice(low, MODES)), :]
        part = jnp.dot(both, entries, preferred_element_type=F32)
        evens.append(part[:32])
        odds.append(part[32:])
    even = jnp.concatenate(evens, axis=0).T
    odd = jnp.concatenate(odds, axis=0).T
    north = even + odd
    south = even - odd
    for gp in range(3):
        for a in range(8):
            first = gp * 128 + a * 8
            for x, to in ((north, a), (south, 15 - a)):
                o_ref[chunk, to, gp, place] = jnp.concatenate(
                    [x[first : first + 8], x[first + 64 : first + 72]], axis=0
                ).astype(BF16)


def residual(gp, x_ref, acc_ref):
    row = lax.broadcasted_iota(jnp.int32, (NP, 256), 0)
    lane = lax.broadcasted_iota(jnp.int32, (NP, 256), 1)
    acc_ref[gp] = jnp.zeros(acc_ref.shape[1:], F32)
    for z in range(NZ):
        begin = ND * z // 128 * 128
        pick = jnp.logical_and(lane == row + (ND * z - begin), row < ND)
        pick = jnp.where(pick, 1.0, 0.0).astype(BF16)
        x = jnp.concatenate([x_ref[2 * gp + gg, z].astype(F32).T for gg in range(2)], axis=0)
        acc_ref[gp, :, begin : begin + 256] += jnp.dot(
            x.astype(BF16), pick, preferred_element_type=F32
        )


def inverse_part(chunk, gp, u_ref, table_ref, wide_ref, rows_ref, lhs_ref, acc_ref):
    def place(w, _):
        wide_ref[...] = u_ref[chunk, pl.ds(4 * w, 4), gp].reshape(128, 128).astype(F32)
        for gg in range(2):
            xs = [wide_ref[pl.ds(gg * 8 + j, 8, stride=16), :] for j in range(8)]
            for mr, y in enumerate(swap_blocks(xs)):
                rows_ref[gg, pl.ds(pl.multiple_of(w * 64 + mr * 8, 8), 8), :] = y
        return 0

    lax.fori_loop(0, 4, place, 0)
    for gg in range(2):
        for k in range(2):
            cols = slice(k * 128, (k + 1) * 128)
            lhs_ref[gg * 128 : gg * 128 + 128, cols] = rows_ref[gg, cols, :].T.astype(BF16)
    waves = slice(chunk * 256, chunk * 256 + 256)
    for part in range(2):
        rows = slice(part * 128, part * 128 + 128)
        acc_ref[gp, rows, :NLON] += jnp.dot(
            lhs_ref[rows, :], table_ref[waves, :], preferred_element_type=F32
        )


def emit(gp, acc_ref, o_ref):
    for j in range(16):

        @pl.when(16 * gp + j < JD)
        def _(j=j):
            o_ref[band_row(16 * gp + j)] = acc_ref[gp, 16 * j : 16 * j + 16, :NLON].astype(BF16)


VM = pl.BlockSpec(memory_space=pltpu.VMEM)
ANY = pl.BlockSpec(memory_space=pl.ANY)
SCRATCH = {
    "points": pltpu.VMEM((JD, ND, CH), BF16),
    "pad": pltpu.VMEM((8 * NP, CH), F32),
    "mix": pltpu.VMEM((2, 8 * NP, 128), F32),
    "out_rows": pltpu.VMEM((6, NZ, NP, 128), BF16),
    "got_rows": pltpu.VMEM((6, NZ, NP, 128), BF16),
    "out_tail": pltpu.VMEM((NZ, TAIL, 128), BF16),
    "got_tail": pltpu.VMEM((NZ, TAIL, 128), BF16),
    "basis_f": pltpu.VMEM((6, 8, NZ * NP), F32),
    "basis_i": pltpu.VMEM((12, 8, NLON), F32),
    "waves_f": pltpu.VMEM((KB, NZ * NP), BF16),
    "waves_i": pltpu.VMEM((KB, NLON), BF16),
    "acc_f": pltpu.VMEM((KB, 128), F32),
    "swap_f": pltpu.VMEM((64, 128), F32),
    "out_spectrum": pltpu.VMEM((6, NA, 64, 128), BF16),
    "got_spectrum": pltpu.VMEM((6, NA, 64, 128), BF16),
    "table": pltpu.VMEM((10240, JH), BF16),
    "cosine": pltpu.VMEM((8, JH), F32),
    "up": pltpu.VMEM((4, 8, JH), F32),
    "low": pltpu.VMEM((4, 8, JH), F32),
    "scale": pltpu.VMEM((4, 8, JH), F32),
    "swap_l": pltpu.VMEM((4, 3, 128, 128), F32),
    "weight": pltpu.VMEM((NA, 2, CH, CH), BF16),
    "every": pltpu.VMEM((8, MODES, 128), F32),
    "out_c": pltpu.VMEM((NZ, ROWS, 128), BF16),
    "got_c": pltpu.VMEM((NZ, ROWS, 128), BF16),
    "out_f": pltpu.VMEM((NZ, ROWS, 128), BF16),
    "got_f": pltpu.VMEM((NZ, ROWS, 128), BF16),
    "wide_in": pltpu.VMEM((2, ROWS * 8, 128), F32),
    "wide_out": pltpu.VMEM((2, ROWS * 8, 128), F32),
    "out_u": pltpu.VMEM((4, NA, 3, 2, 16, 128), BF16),
    "got_u": pltpu.VMEM((4, NA, 3, 2, 16, 128), BF16),
    "wide_u": pltpu.VMEM((128, 128), F32),
    "rows_u": pltpu.VMEM((2, 256, 128), F32),
    "lhs_u": pltpu.VMEM((256, 256), BF16),
    "acc_u": pltpu.VMEM((3, 256, 1536), F32),
    "load": pltpu.SemaphoreType.DMA((2,)),
    "own": pltpu.SemaphoreType.DMA((6, 6)),
    "r_send": pltpu.SemaphoreType.DMA((6, 16)),
    "r_recv": pltpu.SemaphoreType.DMA((6, 16)),
    "s_send": pltpu.SemaphoreType.DMA((6, 16)),
    "s_recv": pltpu.SemaphoreType.DMA((6, 16)),
    "w_send": pltpu.SemaphoreType.DMA((16,)),
    "w_recv": pltpu.SemaphoreType.DMA((16,)),
    "c_send": pltpu.SemaphoreType.DMA((4, 16)),
    "c_recv": pltpu.SemaphoreType.DMA((4, 16)),
    "f_send": pltpu.SemaphoreType.DMA((4, 16)),
    "f_recv": pltpu.SemaphoreType.DMA((4, 16)),
    "u_send": pltpu.SemaphoreType.DMA((3, 16)),
    "u_recv": pltpu.SemaphoreType.DMA((3, 16)),
    "l_send": pltpu.SemaphoreType.DMA((3, 16)),
    "l_recv": pltpu.SemaphoreType.DMA((3, 16)),
}


def each(low, high, body):
    def step(i, _):
        body(i)
        return 0

    lax.fori_loop(low, high, step, 0)


def block_kernel(points_any, gain_ref, in_ref, out_ref, weight_any, o_ref, *scratch):
    v = dict(zip(SCRATCH, scratch))
    lat = lax.axis_index("lat")
    lon = lax.axis_index("lon")
    own = v["own"]

    def rows_copy(g, d):
        return to_peer(
            "lon",
            d,
            lambda peer: v["out_rows"].at[g, peer],
            v["got_rows"].at[g, lon],
            v["r_send"].at[g, d],
            v["r_recv"].at[g, d],
        )

    def own_rows(g):
        return pltpu.make_async_copy(
            v["out_rows"].at[g, lon], v["got_rows"].at[g, lon], own.at[0, g]
        )

    def tail_copy(d):
        return to_peer(
            "lon",
            d,
            lambda peer: v["out_tail"].at[peer],
            v["got_tail"].at[lon],
            v["r_send"].at[5, d],
            v["r_recv"].at[5, d],
        )

    own_tail = pltpu.make_async_copy(v["out_tail"].at[lon], v["got_tail"].at[lon], own.at[0, 5])

    def spectrum_copy(g, d):
        return to_peer(
            "lat",
            d,
            lambda peer: v["out_spectrum"].at[g, peer],
            v["got_spectrum"].at[g, lat],
            v["s_send"].at[g, d],
            v["s_recv"].at[g, d],
        )

    def own_spectrum(g):
        return pltpu.make_async_copy(
            v["out_spectrum"].at[g, lat], v["got_spectrum"].at[g, lat], own.at[1, g]
        )

    def weight_copy(d):
        return to_peer(
            "lat",
            d,
            lambda peer: weight_any,
            v["weight"].at[lat],
            v["w_send"].at[d],
            v["w_recv"].at[d],
        )

    own_weight = pltpu.make_async_copy(weight_any, v["weight"].at[lat], v["load"].at[1])

    def mode_copy(c, name, d):
        part = pl.ds(*SPAN[c])
        return to_peer(
            "lon",
            d,
            lambda peer: v["out_" + name].at[peer, part],
            v["got_" + name].at[lon, part],
            v[name + "_send"].at[c, d],
            v[name + "_recv"].at[c, d],
        )

    def own_modes(c, name):
        part = pl.ds(*SPAN[c])
        return pltpu.make_async_copy(
            v["out_" + name].at[lon, part],
            v["got_" + name].at[lon, part],
            own.at[2 if name == "c" else 3, c],
        )

    def u_copy(c, d):
        return to_peer(
            "lat",
            d,
            lambda peer: v["out_u"].at[c, peer],
            v["got_u"].at[c, lat],
            v["u_send"].at[c, d],
            v["u_recv"].at[c, d],
        )

    def last_copy(gp, d):
        return to_peer(
            "lat",
            d,
            lambda peer: v["out_u"].at[3, peer, gp],
            v["got_u"].at[3, lat, gp],
            v["l_send"].at[gp, d],
            v["l_recv"].at[gp, d],
        )

    def own_last(gp):
        return pltpu.make_async_copy(
            v["out_u"].at[3, lat, gp], v["got_u"].at[3, lat, gp], own.at[5, gp]
        )

    def own_u(c):
        return pltpu.make_async_copy(v["out_u"].at[c, lat], v["got_u"].at[c, lat], own.at[4, c])

    def mlp_step(g):
        mlp_chunk(
            g, v["points"], gain_ref, in_ref, out_ref, v["out_rows"], v["pad"], v["mix"]
        )

    def send_rows(g):
        for d in OTHERS:
            rows_copy(g, d).start()
        own_rows(g).start()

    def got_rows(g):
        own_rows(g).wait()
        for d in OTHERS:
            rows_copy(g, d).wait_recv()

    def transform(g):
        dft(g, v["got_rows"], v["waves_f"], v["acc_f"])

        def one(d):
            peer = lax.rem(lat + d, 16)
            dft_place(g, peer, v["acc_f"], v["swap_f"], v["out_spectrum"])
            spectrum_copy(g, d).start()

        each(1, 16, one)
        dft_place(g, lat, v["acc_f"], v["swap_f"], v["out_spectrum"])
        own_spectrum(g).start()

    load_points = pltpu.make_async_copy(points_any, v["points"], v["load"].at[0])
    load_points.start()
    barrier = announce(("lat", "lon"))
    v["pad"][...] = jnp.zeros_like(v["pad"])
    load_points.wait()
    mlp_step(0)
    pl.semaphore_wait(barrier, 30)
    send_rows(0)

    def mlp_more(g):
        mlp_step(g)

        @pl.when(g < 5)
        def _():
            send_rows(g)

    each(1, 6, mlp_more)
    each(0, NZ, lambda z: pack_tail(z, v["out_rows"], v["out_tail"]))
    for d in OTHERS:
        tail_copy(d).start()
    own_tail.start()
    for d in OTHERS:
        weight_copy(d).start()
    own_weight.start()

    forward_basis(v["basis_f"])
    forward_waves(v["basis_f"], v["waves_f"])
    legendre(v["cosine"], v["table"], v["up"], v["low"], v["scale"], v["swap_l"])
    inverse_basis(v["basis_i"])
    inverse_waves(v["basis_i"], v["waves_i"])

    def pair(gp):
        for gg in range(2):
            got_rows(2 * gp + gg)
            transform(2 * gp + gg)
        residual(gp, v["got_rows"], v["acc_u"])

    each(0, 2, pair)
    got_rows(4)
    transform(4)
    own_tail.wait()
    for d in OTHERS:
        tail_copy(d).wait_recv()
    each(0, NZ, lambda z: unpack_tail(z, v["got_tail"], v["got_rows"]))
    transform(5)
    residual(2, v["got_rows"], v["acc_u"])

    def got_spectrum(g):
        own_spectrum(g).wait()
        for d in OTHERS:
            spectrum_copy(g, d).wait()

    each(0, 6, got_spectrum)
    for c in range(4):
        for mg in CHUNKS[c]:
            analyse(mg, v["got_spectrum"], v["table"], v["every"])
        each(0, NZ, lambda z, c=c: analysis_rows(z, c, v["every"], v["out_c"]))
        for d in OTHERS:
            mode_copy(c, "c", d).start()
        own_modes(c, "c").start()
    own_weight.wait()
    for d in OTHERS:
        weight_copy(d).wait()
    for c in range(4):
        own_modes(c, "c").wait()
        for d in OTHERS:
            mode_copy(c, "c", d).wait()
        filter_chunk(c, v["got_c"], v["weight"], v["out_f"], v["wide_in"], v["wide_out"])
        for d in OTHERS:
            mode_copy(c, "f", d).start()
        own_modes(c, "f").start()

    def inverse(c, gp):
        inverse_part(
            c, gp, v["got_u"], v["waves_i"], v["wide_u"], v["rows_u"], v["lhs_u"], v["acc_u"]
        )

    def inverse_step(c):
        own_u(c).wait()
        for d in OTHERS:
            u_copy(c, d).wait()
        each(0, 3, lambda gp: inverse(c, gp))

    for c in range(4):
        own_modes(c, "f").wait()
        for d in OTHERS:
            mode_copy(c, "f", d).wait()
        each(0, NZ, lambda z, c=c: synthesis_rows(z, c, v["got_f"], v["every"]))
        for place in range(2):
            synthesise(c, place, v["table"], v["every"], v["out_u"])
        if c < 3:
            for d in OTHERS:
                u_copy(c, d).start()
            own_u(c).start()
        else:

            def send_last(gp):
                for d in OTHERS:
                    last_copy(gp, d).start()
                own_last(gp).start()

            each(0, 3, send_last)
        if c >= 1:
            inverse_step(c - 1)

    def rows_sent(g):
        for d in OTHERS:
            rows_copy(g, d).wait_send()

    each(0, 5, rows_sent)
    for d in OTHERS:
        tail_copy(d).wait_send()

    def finish(gp):
        own_last(gp).wait()
        for d in OTHERS:
            last_copy(gp, d).wait()
        inverse(3, gp)
        emit(gp, v["acc_u"], o_ref)

    each(0, 3, finish)


def on_device(grid, norm_gain, mlp_in, mlp_out, filter_weight):
    updated = pl.pallas_call(
        block_kernel,
        out_shape=jax.ShapeDtypeStruct((JD, 16, NLON), BF16),
        in_specs=[ANY, VM, VM, VM, ANY],
        out_specs=VM,
        scratch_shapes=list(SCRATCH.values()),
        cost_estimate=pl.CostEstimate(
            flops=20_000_000_000, bytes_accessed=10_000_000, transcendentals=0
        ),
        compiler_params=pltpu.CompilerParams(
            collective_id=1, has_side_effects=True, vmem_limit_bytes=LIMIT
        ),
    )(grid.transpose(1, 2, 0), norm_gain.reshape(1, CH), mlp_in, mlp_out, filter_weight)
    return updated.transpose(1, 0, 2)


def solution(mesh):
    return jax.shard_map(
        on_device,
        mesh=mesh,
        in_specs=(P("batch", "lat", "lon"), P(), P(), P(), P(("lat", "lon"), None, None)),
        out_specs=P(("batch", "lon"), "lat", None),
        check_vma=False,
    )
```

```python
import functools

import jax
import jax.numpy as jnp
from jax import lax
from jax.experimental import pallas as pl
from jax.experimental.pallas import tpu as pltpu
from jax.sharding import PartitionSpec as P

F32 = jnp.float32
BF16 = jnp.bfloat16

CH = 256
HID = 512
JD = 45
JP = 48
ND = 90
NP = 96
NLAT = 720
NLON = 1440
MODES = 512
NA = 16
NZ = 16
JH = NA * JP // 2
LAST = JD - 1
KB = 2 * MODES
ROWS = 144
LIMIT = 58 * 1024 * 1024
MESH = pl.DeviceIdType.MESH
OTHERS = (8, 7, 9, 6, 10, 5, 11, 4, 12, 3, 13, 2, 14, 1, 15)
CHUNKS = ((3, 5), (0, 4), (1, 7), (2, 6))
SLOTS = ((3,), (0, 4), (1,), (2,))
BASE = {3: 0, 0: 32, 4: 64, 1: 80, 2: 112}
SPAN = ((0, 32), (32, 48), (80, 32), (112, 32))
TAIL = 64
LEG = (0, 4096, 7168, 9216)


def swap_blocks(xs):
    block = lax.broadcasted_iota(jnp.int32, xs[0].shape, 1) // 16
    for bit in (1, 2, 4):
        upper = (block & bit) != 0
        new = list(xs)
        for i in range(8):
            if i & bit == 0:
                low, high = xs[i], xs[i | bit]
                new[i] = jnp.where(upper, pltpu.roll(high, 16 * bit, 1), low)
                new[i | bit] = jnp.where(upper, high, pltpu.roll(low, 128 - 16 * bit, 1))
        xs = new
    return xs


def announce(axes):
    barrier = pltpu.get_barrier_semaphore()
    for axis in axes:
        me = lax.axis_index(axis)
        for d in range(1, 16):
            pl.semaphore_signal(
                barrier, inc=1, device_id={axis: lax.rem(me + d, 16)}, device_id_type=MESH
            )
    return barrier


def to_peer(axis, d, src, dst, send, recv):
    peer = lax.rem(lax.axis_index(axis) + d, 16)
    return pltpu.make_async_remote_copy(
        src_ref=src(peer),
        dst_ref=dst,
        send_sem=send,
        recv_sem=recv,
        device_id={axis: peer},
        device_id_type=MESH,
    )


def band_row(jj):
    jj = jnp.minimum(jj, LAST)
    return jnp.where(lax.axis_index("lat") >= 8, LAST - jj, jj)


def mlp_chunk(g, x_ref, gain_ref, in_ref, out_w_ref, o_ref, pad_ref, mix_ref):
    for j in range(8):
        pad_ref[j * NP : j * NP + ND, :] = x_ref[band_row(8 * g + j)].astype(F32)
    half = 2 * NP
    for part in range(4):
        rows = slice(part * half, (part + 1) * half)
        x = pad_ref[rows, :]
        mean = jnp.mean(x, axis=1, keepdims=True)
        centered = x - mean
        spread = jnp.mean(centered * centered, axis=1, keepdims=True)
        normed = (centered * lax.rsqrt(spread + 1e-05) * gain_ref[...]).astype(BF16)
        hidden = jnp.dot(normed, in_ref[...], preferred_element_type=F32)
        hidden = jax.nn.gelu(hidden).astype(BF16)
        mixed = x + jnp.dot(hidden, out_w_ref[...], preferred_element_type=F32)
        mix_ref[0, rows, :] = mixed[:, :128]
        mix_ref[1, rows, :] = mixed[:, 128:]
    lane = lax.broadcasted_iota(jnp.int32, (16, 128), 1)
    row = lax.broadcasted_iota(jnp.int32, (16, 128), 0)
    live = lane // 16 < JD - 8 * g

    def place(step, _):
        start = pl.multiple_of(step * 16, 16)
        keep = jnp.logical_and(live, row < ND - start)
        for h in range(2):
            xs = [mix_ref[h, pl.ds(pl.multiple_of(j * NP + start, 16), 16), :] for j in range(8)]
            for z, y in enumerate(swap_blocks(xs)):
                o_ref[g, h * 8 + z, pl.ds(start, 16), :] = jnp.where(keep, y, 0.0).astype(BF16)
        return 0

    lax.fori_loop(0, NP // 16, place, 0)


def pack_tail(z, x_ref, o_ref):
    x = x_ref[5, z].astype(F32)
    low, high = x[:48], x[48:]
    block = lax.broadcasted_iota(jnp.int32, (48, 128), 1) // 16
    o_ref[z, :48, :] = jnp.where(block < 5, low, pltpu.roll(high, 80, 1)).astype(BF16)
    block = lax.broadcasted_iota(jnp.int32, (16, 128), 1) // 16
    rest = jnp.zeros((16, 128), F32)
    for b in (3, 4):
        for k in range(3):
            to = 3 * (b - 3) + k
            part = high[16 * k : 16 * k + 16]
            rest = jnp.where(block == to, pltpu.roll(part, (to - b) * 16 % 128, 1), rest)
    o_ref[z, 48:, :] = rest.astype(BF16)


def unpack_tail(z, x_ref, o_ref):
    x = x_ref[z].astype(F32)
    first, rest = x[:48], x[48:]
    block = lax.broadcasted_iota(jnp.int32, (48, 128), 1) // 16
    o_ref[5, z, :48, :] = jnp.where(block < 5, first, 0.0).astype(BF16)
    high = jnp.where(block < 3, pltpu.roll(first, 48, 1), 0.0)
    block = lax.broadcasted_iota(jnp.int32, (16, 128), 1) // 16
    for k in range(3):
        part = high[16 * k : 16 * k + 16]
        for b in (3, 4):
            held = 3 * (b - 3) + k
            part = jnp.where(block == b, pltpu.roll(rest, (b - held) * 16 % 128, 1), part)
        o_ref[5, z, 48 + 16 * k : 64 + 16 * k, :] = part.astype(BF16)


def wave_tile(group, basis_ref, high, low):
    group_cos, group_sin = basis_ref[group], basis_ref[group + 1]
    high_cos = basis_ref[2, pl.ds(high, 1), :]
    high_sin = basis_ref[3, pl.ds(high, 1), :]
    low_cos = basis_ref[0, low : low + 1, :]
    low_sin = basis_ref[1, low : low + 1, :]
    c = high_cos * low_cos - high_sin * low_sin
    s = high_sin * low_cos + high_cos * low_sin
    return group_cos * c - group_sin * s, -(group_sin * c + group_cos * s)


def forward_waves(basis_ref, o_ref):
    def step(high, _):
        for low in range(8):
            tile = wave_tile(4, basis_ref, high, low)
            offset = 8 * high + low
            start = offset // 2 % 16 * 64 + offset // 32 * 32 + low % 2 * 16
            o_ref[pl.ds(pl.multiple_of(start, 16), 16), :] = jnp.concatenate(tile, axis=0).astype(
                BF16
            )
        return 0

    lax.fori_loop(0, 8, step, 0)


def inverse_waves(basis_ref, o_ref):
    row = lax.broadcasted_iota(jnp.int32, (8, NLON), 0)

    def step(high, _):
        for low in range(2):
            for c in range(4):
                real, imag = wave_tile(4 + 2 * c, basis_ref, high, low)
                if low == 0 and c == 1:
                    real = jnp.where(jnp.logical_and(high == 0, row == 0), 0.5 * real, real)
                start = c * 256 + high % 4 * 64 + high // 4 * 32 + low * 16
                o_ref[pl.ds(pl.multiple_of(start, 16), 16), :] = jnp.concatenate(
                    [real, imag], axis=0
                ).astype(BF16)
        return 0

    lax.fori_loop(0, 8, step, 0)


def put_basis(k, o_ref, multiple, points, factor):
    phase = multiple.astype(F32) * points
    phase = phase - NLON * jnp.floor(phase * (1.0 / NLON))
    angle = 2.0 * jnp.pi / NLON * phase
    o_ref[k] = jnp.cos(angle) * factor
    o_ref[k + 1] = jnp.sin(angle) * factor


def forward_basis(o_ref):
    count = lax.broadcasted_iota(jnp.int32, (8, NZ * NP), 0)
    column = lax.broadcasted_iota(jnp.int32, (8, NZ * NP), 1).astype(F32)
    z = jnp.floor((column + 0.5) * (1.0 / NP))
    n = column - NP * z
    points = ND * z + n
    put_basis(0, o_ref, count, points, 1.0)
    put_basis(2, o_ref, 8 * count, points, 1.0)
    put_basis(4, o_ref, 64 * count, points, jnp.where(n < ND, 1.0, 0.0))


def inverse_basis(o_ref):
    count = lax.broadcasted_iota(jnp.int32, (8, NLON), 0)
    points = lax.broadcasted_iota(jnp.int32, (8, NLON), 1).astype(F32)
    put_basis(0, o_ref, count, points, 1.0)
    put_basis(2, o_ref, 8 * count, points, 1.0)
    for c, (first, second) in enumerate(CHUNKS):
        multiple = jnp.where(count % 2 == 0, 64 * first, 64 * second) + count // 2 * 2
        put_basis(4 + 2 * c, o_ref, multiple, points, 2.0)


def dft_part(g, part, x_ref, table_ref, acc_ref):
    lat = lax.axis_index("lat")
    band = jnp.minimum(lat, 15 - lat)
    local = lax.broadcasted_iota(jnp.int32, (8, 128), 1) // 16 + 8 * g
    theta = jnp.pi * ((local + band * JD).astype(F32) + 0.5) / NLAT
    weights = jnp.pi / NLAT * jnp.sin(theta) / NLON
    weights = jnp.where(local < JD, weights, 0.0)[:1]
    rows = pl.ds(pl.multiple_of(part * 256, 256), 256)
    x = x_ref[g].reshape(NZ * NP, 128)
    acc_ref[rows, :] = jnp.dot(table_ref[rows, :], x, preferred_element_type=F32) * weights


def dft_place(g, a, acc_ref, swap_ref, o_ref):
    xs = [acc_ref[pl.ds(pl.multiple_of(a * 64 + mr * 8, 8), 8), :] for mr in range(8)]
    for j, y in enumerate(swap_blocks(xs)):
        swap_ref[pl.ds(j, 8, stride=8), :] = y
    o_ref[g, a] = swap_ref[...].astype(BF16)


def legendre_orders(q, width):
    row = lax.broadcasted_iota(jnp.int32, (8, width), 0)
    order = 128 * q + row // 4 * 64 + row // 2 % 2 * 32 + row % 2
    return (order + 2 * lax.axis_index("lat")).astype(F32)


def legendre_start(cos_ref, scale_ref):
    column = lax.broadcasted_iota(jnp.int32, (8, JH), 1)
    local = column // 64 * 8 + column % 8
    theta = jnp.pi * ((column // 8 % 8 * JD + local).astype(F32) + 0.5) / NLAT
    real = local < JD
    cos_ref[...] = jnp.where(real, jnp.cos(theta), 0.0)
    log_sine = jnp.log(jnp.where(real, jnp.sin(theta), 1.0))
    counts = (lax.broadcasted_iota(jnp.int32, (8, MODES), 1) + 1).astype(F32)
    ratios = jnp.log((2.0 * counts - 1.0) / (2.0 * counts))
    for q in range(4):
        partial_log = jnp.sum(
            jnp.where(counts <= legendre_orders(q, MODES), ratios, 0.0), axis=1, keepdims=True
        )
        order = legendre_orders(q, JH)
        start_log = order * log_sine + 0.5 * jnp.log(order + 0.5) + 0.5 * partial_log
        scale_ref[q] = jnp.where(real, start_log, -1e9)


def legendre_rows(mg, m, rows):
    q = mg // 2
    base = LEG[q] + (mg % 2 * 4 + m) * (MODES - 128 * q) - 128 * q
    return slice(base + rows.start, base + rows.stop)


def legendre_group(q, i, cos_ref, o_ref, up_ref, low_ref, scale_ref, swap_ref):
    order = legendre_orders(q, 128)
    degree = lax.broadcasted_iota(jnp.int32, (8, 128), 1) + 16 * i
    degree = degree.astype(F32)
    active = degree > order
    second = degree > order + 1.0
    grow = jnp.sqrt(
        jnp.where(active, 4.0 * degree * degree - 1.0, 0.0)
        / jnp.where(active, degree * degree - order * order, 1.0)
    )
    before = degree - 1.0
    damp = grow * jnp.sqrt(
        jnp.where(second, before * before - order * order, 0.0)
        / jnp.where(second, 4.0 * before * before - 1.0, 1.0)
    )
    first = jnp.where(degree == order, 1.0, 0.0)
    up, low, scale_log = up_ref[q], low_ref[q], scale_ref[q]
    root = jnp.exp(0.5 * scale_log)
    cosine = cos_ref[...]
    for s in range(16):
        a = jnp.broadcast_to(grow[:, s : s + 1], (8, JH))
        b = jnp.broadcast_to(damp[:, s : s + 1], (8, JH))
        e = jnp.broadcast_to(first[:, s : s + 1], (8, JH))
        fresh = a * (cosine * up) - b * low + e
        low = up
        up = fresh
        value = fresh * root * root
        for k in range(3):
            swap_ref[q, k, s * 8 : s * 8 + 8, :] = value[:, k * 128 : k * 128 + 128]
    largest = jnp.maximum(jnp.abs(up), jnp.abs(low))
    largest = jnp.where(largest > 0.0, largest, 1.0)
    up_ref[q] = up / largest
    low_ref[q] = low / largest
    scale_ref[q] = scale_log + jnp.log(largest)
    for m in range(8):
        base = LEG[q] + m * (MODES - 128 * q) - 128 * q
        start = pl.multiple_of(base + i * 16, 16)
        for k in range(3):
            o_ref[pl.ds(start, 16), k * 128 : k * 128 + 128] = swap_ref[
                q, k, pl.ds(m, 16, stride=8), :
            ].astype(BF16)


def legendre(cos_ref, o_ref, up_ref, low_ref, scale_ref, swap_ref):
    up_ref[...] = jnp.zeros_like(up_ref)
    low_ref[...] = jnp.zeros_like(low_ref)
    legendre_start(cos_ref, scale_ref)
    for stage in range(4):

        def step(i, _, stage=stage):
            for q in range(stage + 1):
                legendre_group(q, i, cos_ref, o_ref, up_ref, low_ref, scale_ref, swap_ref)
            return 0

        lax.fori_loop(8 * stage, 8 * stage + 8, step, 0)


def analyse(mg, x_ref, table_ref, all_ref):
    north, south = [], []
    start = mg // 2 * 16
    part = slice(mg % 2 * 8, mg % 2 * 8 + 8)
    for g in range(6):
        x = x_ref[g, :, start : start + 16, :].astype(F32)[:, part]
        north.append(x[:8].reshape(64, 128))
        south += [x[15 - a] for a in range(8)]
    north = jnp.concatenate(north, axis=0)
    south = jnp.concatenate(south, axis=0)
    both = jnp.concatenate([north + south, north - south], axis=1).astype(BF16)
    block = lax.broadcasted_iota(jnp.int32, (128, 128), 1) // 32
    odd = lax.broadcasted_iota(jnp.int32, (128, 128), 0) % 2 == 1
    for lb in range(mg // 2, 4):
        rows = slice(lb * 128, lb * 128 + 128)
        total = jnp.zeros((128, 128), F32)
        for m in range(4):
            entries = table_ref[legendre_rows(mg, m, rows), :]
            part = jnp.dot(entries, both, preferred_element_type=F32)
            first, second = part[:, :128], part[:, 128:]
            if m % 2:
                first, second = second, first
            total = jnp.where(block == m, jnp.where(odd, second, first), total)
        all_ref[mg, rows, :] = total


def analysis_rows(z, chunk, all_ref, o_ref):
    row = lax.broadcasted_iota(jnp.int32, (16, 128), 0)
    kept = []
    for t in range(2):
        where = pl.ds(2 * z + t, 16, stride=32)
        for s in SLOTS[chunk]:
            x = all_ref[s, where, :]
            if s == 4:
                kept.append(x[8:])
                continue
            if s:
                x = jnp.where(row < 2 * s, pltpu.roll(all_ref[8 - s, where, :], 2 * s, 0), x)
            start = BASE[s] + t * 16
            o_ref[z, start : start + 16, :] = x.astype(BF16)
    if kept:
        o_ref[z, 64:80, :] = jnp.concatenate(kept, axis=0).astype(BF16)


def filter_row(mg, a, t):
    if mg < 4:
        return BASE[mg] + 16 * t + a
    if mg == 4:
        return BASE[4] + 8 * t + a - 8
    return BASE[8 - mg] + 16 * t + a - 2 * mg


def filter_chunk(chunk, x_ref, w_ref, o_ref, in_ref, out_ref):
    begin, count = SPAN[chunk]

    def gather(step, _):
        start = pl.multiple_of(begin + step * 16, 16)
        for h in range(2):
            xs = [x_ref[h * 8 + z, pl.ds(start, 16), :].astype(F32) for z in range(8)]
            for mr, y in enumerate(swap_blocks(xs)):
                in_ref[h, pl.ds(start * 8 + mr, 16, stride=8), :] = y
        return 0

    lax.fori_loop(0, count // 16, gather, 0)
    for a in range(16):
        for t in range(2):
            rows = [8 * filter_row(mg, a, t) for mg in CHUNKS[chunk] if mg <= a // 2]
            if not rows:
                continue
            x = jnp.concatenate(
                [
                    jnp.concatenate([in_ref[h, r : r + 8, :] for r in rows], axis=0)
                    for h in range(2)
                ],
                axis=1,
            ).astype(BF16)
            y = jnp.dot(x, w_ref[a, t], preferred_element_type=F32)
            for i, r in enumerate(rows):
                for h in range(2):
                    out_ref[h, r : r + 8, :] = y[i * 8 : i * 8 + 8, h * 128 : h * 128 + 128]

    def scatter(step, _):
        start = pl.multiple_of(begin + step * 16, 16)
        for h in range(2):
            xs = [out_ref[h, pl.ds(start * 8 + mr, 16, stride=8), :] for mr in range(8)]
            for z, y in enumerate(swap_blocks(xs)):
                o_ref[h * 8 + z, pl.ds(start, 16), :] = y.astype(BF16)
        return 0

    lax.fori_loop(0, count // 16, scatter, 0)


def synthesis_rows(z, chunk, x_ref, all_ref):
    row = lax.broadcasted_iota(jnp.int32, (16, 128), 0)
    for s in SLOTS[chunk]:
        for t in range(2):
            where = pl.ds(2 * z + t, 16, stride=32)
            if s == 4:
                last = x_ref[z, 64:80, :].astype(F32)
                x = jnp.concatenate([jnp.zeros((8, 128), F32), last[t * 8 : t * 8 + 8]], axis=0)
                all_ref[4, where, :] = x
                continue
            start = BASE[s] + t * 16
            x = x_ref[z, start : start + 16, :].astype(F32)
            if s:
                all_ref[8 - s, where, :] = jnp.where(
                    row >= 16 - 2 * s, pltpu.roll(x, 16 - 2 * s, 0), 0.0
                )
                x = jnp.where(row >= 2 * s, x, 0.0)
            all_ref[s, where, :] = x


def synthesise(chunk, place, table_ref, all_ref, o_ref):
    mg = CHUNKS[chunk][place]
    low = mg // 2 * 128
    block = lax.broadcasted_iota(jnp.int32, (MODES - low, 128), 1) // 32
    row = lax.broadcasted_iota(jnp.int32, (MODES - low, 128), 0)
    same = (block + row) % 2 == 0
    x = all_ref[mg, low:, :]
    even = jnp.where(same, x, 0.0).T.astype(BF16)
    odd = jnp.where(same, 0.0, x).T.astype(BF16)
    evens, odds = [], []
    for m in range(4):
        rows = slice(m * 32, m * 32 + 32)
        both = jnp.concatenate([even[rows], odd[rows]], axis=0)
        entries = table_ref[legendre_rows(mg, m, slice(low, MODES)), :]
        part = jnp.dot(both, entries, preferred_element_type=F32)
        evens.append(part[:32])
        odds.append(part[32:])
    even = jnp.concatenate(evens, axis=0).T
    odd = jnp.concatenate(odds, axis=0).T
    north = even + odd
    south = even - odd
    for gp in range(3):
        for a in range(8):
            first = gp * 128 + a * 8
            for x, to in ((north, a), (south, 15 - a)):
                o_ref[chunk, to, gp, place] = jnp.concatenate(
                    [x[first : first + 8], x[first + 64 : first + 72]], axis=0
                ).astype(BF16)


def residual(gp, x_ref, acc_ref):
    row = lax.broadcasted_iota(jnp.int32, (NP, 256), 0)
    lane = lax.broadcasted_iota(jnp.int32, (NP, 256), 1)
    acc_ref[gp] = jnp.zeros(acc_ref.shape[1:], F32)
    for z in range(NZ):
        begin = ND * z // 128 * 128
        pick = jnp.logical_and(lane == row + (ND * z - begin), row < ND)
        pick = jnp.where(pick, 1.0, 0.0).astype(BF16)
        x = jnp.concatenate([x_ref[2 * gp + gg, z].astype(F32).T for gg in range(2)], axis=0)
        acc_ref[gp, :, begin : begin + 256] += jnp.dot(
            x.astype(BF16), pick, preferred_element_type=F32
        )


def inverse_part(chunk, gp, u_ref, table_ref, wide_ref, rows_ref, lhs_ref, acc_ref):
    def place(w, _):
        wide_ref[...] = u_ref[chunk, pl.ds(4 * w, 4), gp].reshape(128, 128).astype(F32)
        for gg in range(2):
            xs = [wide_ref[pl.ds(gg * 8 + j, 8, stride=16), :] for j in range(8)]
            for mr, y in enumerate(swap_blocks(xs)):
                rows_ref[gg, pl.ds(pl.multiple_of(w * 64 + mr * 8, 8), 8), :] = y
        return 0

    lax.fori_loop(0, 4, place, 0)
    for gg in range(2):
        for k in range(2):
            cols = slice(k * 128, (k + 1) * 128)
            lhs_ref[gg * 128 : gg * 128 + 128, cols] = rows_ref[gg, cols, :].T.astype(BF16)
    waves = slice(chunk * 256, chunk * 256 + 256)
    for part in range(2):
        rows = slice(part * 128, part * 128 + 128)
        acc_ref[gp, rows, :NLON] += jnp.dot(
            lhs_ref[rows, :], table_ref[waves, :], preferred_element_type=F32
        )


def emit(gp, acc_ref, o_ref):
    for j in range(min(16, JD - 16 * gp)):
        o_ref[band_row(16 * gp + j)] = acc_ref[gp, 16 * j : 16 * j + 16, :NLON].astype(BF16)


VM = pl.BlockSpec(memory_space=pltpu.VMEM)
ANY = pl.BlockSpec(memory_space=pl.ANY)
SCRATCH = {
    "points": pltpu.VMEM((JD, ND, CH), BF16),
    "pad": pltpu.VMEM((8 * NP, CH), F32),
    "mix": pltpu.VMEM((2, 8 * NP, 128), F32),
    "out_rows": pltpu.VMEM((6, NZ, NP, 128), BF16),
    "got_rows": pltpu.VMEM((6, NZ, NP, 128), BF16),
    "out_tail": pltpu.VMEM((NZ, TAIL, 128), BF16),
    "got_tail": pltpu.VMEM((NZ, TAIL, 128), BF16),
    "basis_f": pltpu.VMEM((6, 8, NZ * NP), F32),
    "basis_i": pltpu.VMEM((12, 8, NLON), F32),
    "waves_f": pltpu.VMEM((KB, NZ * NP), BF16),
    "waves_i": pltpu.VMEM((KB, NLON), BF16),
    "acc_f": pltpu.VMEM((KB, 128), F32),
    "swap_f": pltpu.VMEM((64, 128), F32),
    "out_spectrum": pltpu.VMEM((6, NA, 64, 128), BF16),
    "got_spectrum": pltpu.VMEM((6, NA, 64, 128), BF16),
    "table": pltpu.VMEM((10240, JH), BF16),
    "cosine": pltpu.VMEM((8, JH), F32),
    "up": pltpu.VMEM((4, 8, JH), F32),
    "low": pltpu.VMEM((4, 8, JH), F32),
    "scale": pltpu.VMEM((4, 8, JH), F32),
    "swap_l": pltpu.VMEM((4, 3, 128, 128), F32),
    "weight": pltpu.VMEM((NA, 2, CH, CH), BF16),
    "every": pltpu.VMEM((8, MODES, 128), F32),
    "out_c": pltpu.VMEM((NZ, ROWS, 128), BF16),
    "got_c": pltpu.VMEM((NZ, ROWS, 128), BF16),
    "out_f": pltpu.VMEM((NZ, ROWS, 128), BF16),
    "got_f": pltpu.VMEM((NZ, ROWS, 128), BF16),
    "wide_in": pltpu.VMEM((2, ROWS * 8, 128), F32),
    "wide_out": pltpu.VMEM((2, ROWS * 8, 128), F32),
    "out_u": pltpu.VMEM((4, NA, 3, 2, 16, 128), BF16),
    "got_u": pltpu.VMEM((4, NA, 3, 2, 16, 128), BF16),
    "wide_u": pltpu.VMEM((128, 128), F32),
    "rows_u": pltpu.VMEM((2, 256, 128), F32),
    "lhs_u": pltpu.VMEM((256, 256), BF16),
    "acc_u": pltpu.VMEM((3, 256, 1536), F32),
    "updated": pltpu.VMEM((JD, 16, NLON), BF16),
    "load": pltpu.SemaphoreType.DMA((2,)),
    "store": pltpu.SemaphoreType.DMA((3,)),
    "own": pltpu.SemaphoreType.DMA((6, 6)),
    "r_send": pltpu.SemaphoreType.DMA((6, 16)),
    "r_recv": pltpu.SemaphoreType.DMA((6, 16)),
    "s_send": pltpu.SemaphoreType.DMA((6, 16)),
    "s_recv": pltpu.SemaphoreType.DMA((6, 16)),
    "w_send": pltpu.SemaphoreType.DMA((16,)),
    "w_recv": pltpu.SemaphoreType.DMA((16,)),
    "c_send": pltpu.SemaphoreType.DMA((4, 16)),
    "c_recv": pltpu.SemaphoreType.DMA((4, 16)),
    "f_send": pltpu.SemaphoreType.DMA((4, 16)),
    "f_recv": pltpu.SemaphoreType.DMA((4, 16)),
    "u_send": pltpu.SemaphoreType.DMA((3, 16)),
    "u_recv": pltpu.SemaphoreType.DMA((3, 16)),
    "l_send": pltpu.SemaphoreType.DMA((3, 16)),
    "l_recv": pltpu.SemaphoreType.DMA((3, 16)),
}


def each(low, high, body):
    def step(i, _):
        body(i)
        return 0

    lax.fori_loop(low, high, step, 0)


def block_kernel(points_any, gain_ref, in_ref, out_ref, weight_any, o_any, *scratch):
    v = dict(zip(SCRATCH, scratch))
    lat = lax.axis_index("lat")
    lon = lax.axis_index("lon")
    own = v["own"]

    def rows_copy(g, d):
        return to_peer(
            "lon",
            d,
            lambda peer: v["out_rows"].at[g, peer],
            v["got_rows"].at[g, lon],
            v["r_send"].at[g, d],
            v["r_recv"].at[g, d],
        )

    def own_rows(g):
        return pltpu.make_async_copy(
            v["out_rows"].at[g, lon], v["got_rows"].at[g, lon], own.at[0, g]
        )

    def tail_copy(d):
        return to_peer(
            "lon",
            d,
            lambda peer: v["out_tail"].at[peer],
            v["got_tail"].at[lon],
            v["r_send"].at[5, d],
            v["r_recv"].at[5, d],
        )

    own_tail = pltpu.make_async_copy(v["out_tail"].at[lon], v["got_tail"].at[lon], own.at[0, 5])

    def spectrum_copy(g, d):
        return to_peer(
            "lat",
            d,
            lambda peer: v["out_spectrum"].at[g, peer],
            v["got_spectrum"].at[g, lat],
            v["s_send"].at[g, d],
            v["s_recv"].at[g, d],
        )

    def own_spectrum(g):
        return pltpu.make_async_copy(
            v["out_spectrum"].at[g, lat], v["got_spectrum"].at[g, lat], own.at[1, g]
        )

    def weight_copy(d):
        return to_peer(
            "lat",
            d,
            lambda peer: weight_any,
            v["weight"].at[lat],
            v["w_send"].at[d],
            v["w_recv"].at[d],
        )

    own_weight = pltpu.make_async_copy(weight_any, v["weight"].at[lat], v["load"].at[1])

    def mode_copy(c, name, d):
        part = pl.ds(*SPAN[c])
        return to_peer(
            "lon",
            d,
            lambda peer: v["out_" + name].at[peer, part],
            v["got_" + name].at[lon, part],
            v[name + "_send"].at[c, d],
            v[name + "_recv"].at[c, d],
        )

    def own_modes(c, name):
        part = pl.ds(*SPAN[c])
        return pltpu.make_async_copy(
            v["out_" + name].at[lon, part],
            v["got_" + name].at[lon, part],
            own.at[2 if name == "c" else 3, c],
        )

    def u_copy(c, d):
        return to_peer(
            "lat",
            d,
            lambda peer: v["out_u"].at[c, peer],
            v["got_u"].at[c, lat],
            v["u_send"].at[c, d],
            v["u_recv"].at[c, d],
        )

    def last_copy(gp, d):
        return to_peer(
            "lat",
            d,
            lambda peer: v["out_u"].at[3, peer, gp],
            v["got_u"].at[3, lat, gp],
            v["l_send"].at[gp, d],
            v["l_recv"].at[gp, d],
        )

    def own_last(gp):
        return pltpu.make_async_copy(
            v["out_u"].at[3, lat, gp], v["got_u"].at[3, lat, gp], own.at[5, gp]
        )

    def own_u(c):
        return pltpu.make_async_copy(v["out_u"].at[c, lat], v["got_u"].at[c, lat], own.at[4, c])

    def mlp_step(g):
        mlp_chunk(
            g, v["points"], gain_ref, in_ref, out_ref, v["out_rows"], v["pad"], v["mix"]
        )

    def send_rows(g):
        for d in OTHERS:
            rows_copy(g, d).start()
        own_rows(g).start()

    def got_rows(g):
        own_rows(g).wait()
        for d in OTHERS:
            rows_copy(g, d).wait_recv()

    def transform(g):
        def part(k):
            quarter = lax.rem(lat // 4 + k, 4)
            dft_part(g, quarter, v["got_rows"], v["waves_f"], v["acc_f"])
            for i in range(4):
                peer = 4 * quarter + i
                dft_place(g, peer, v["acc_f"], v["swap_f"], v["out_spectrum"])

                @pl.when(peer != lat)
                def _():
                    spectrum_copy(g, lax.rem(peer - lat + 16, 16)).start()

        each(0, 4, part)
        own_spectrum(g).start()

    load_points = pltpu.make_async_copy(points_any, v["points"], v["load"].at[0])
    load_points.start()
    barrier = announce(("lat", "lon"))
    v["pad"][...] = jnp.zeros_like(v["pad"])
    load_points.wait()
    mlp_step(0)
    pl.semaphore_wait(barrier, 30)
    send_rows(0)
    for d in OTHERS:
        weight_copy(d).start()
    own_weight.start()

    def mlp_more(g):
        mlp_step(g)

        @pl.when(g < 5)
        def _():
            send_rows(g)

    each(1, 6, mlp_more)
    each(0, NZ, lambda z: pack_tail(z, v["out_rows"], v["out_tail"]))
    for d in OTHERS:
        tail_copy(d).start()
    own_tail.start()
    forward_basis(v["basis_f"])
    forward_waves(v["basis_f"], v["waves_f"])
    legendre(v["cosine"], v["table"], v["up"], v["low"], v["scale"], v["swap_l"])
    inverse_basis(v["basis_i"])
    inverse_waves(v["basis_i"], v["waves_i"])

    def pair(gp):
        for gg in range(2):
            got_rows(2 * gp + gg)
            transform(2 * gp + gg)
        residual(gp, v["got_rows"], v["acc_u"])

    each(0, 2, pair)
    got_rows(4)
    transform(4)
    own_tail.wait()
    for d in OTHERS:
        tail_copy(d).wait_recv()
    each(0, NZ, lambda z: unpack_tail(z, v["got_tail"], v["got_rows"]))
    transform(5)
    residual(2, v["got_rows"], v["acc_u"])

    def got_spectrum(g):
        own_spectrum(g).wait()
        for d in OTHERS:
            spectrum_copy(g, d).wait()

    each(0, 6, got_spectrum)
    for c in range(4):
        for mg in CHUNKS[c]:
            analyse(mg, v["got_spectrum"], v["table"], v["every"])
        each(0, NZ, lambda z, c=c: analysis_rows(z, c, v["every"], v["out_c"]))
        for d in OTHERS:
            mode_copy(c, "c", d).start()
        own_modes(c, "c").start()
    own_weight.wait()
    for d in OTHERS:
        weight_copy(d).wait()
    for c in range(4):
        own_modes(c, "c").wait()
        for d in OTHERS:
            mode_copy(c, "c", d).wait()
        filter_chunk(c, v["got_c"], v["weight"], v["out_f"], v["wide_in"], v["wide_out"])
        for d in OTHERS:
            mode_copy(c, "f", d).start()
        own_modes(c, "f").start()

    def inverse(c, gp):
        inverse_part(
            c, gp, v["got_u"], v["waves_i"], v["wide_u"], v["rows_u"], v["lhs_u"], v["acc_u"]
        )

    def inverse_step(c):
        own_u(c).wait()
        for d in OTHERS:
            u_copy(c, d).wait()
        each(0, 3, lambda gp: inverse(c, gp))

    for c in range(4):
        own_modes(c, "f").wait()
        for d in OTHERS:
            mode_copy(c, "f", d).wait()
        each(0, NZ, lambda z, c=c: synthesis_rows(z, c, v["got_f"], v["every"]))
        for place in range(2):
            synthesise(c, place, v["table"], v["every"], v["out_u"])
        if c < 3:
            for d in OTHERS:
                u_copy(c, d).start()
            own_u(c).start()
        else:

            def send_last(gp):
                for d in OTHERS:
                    last_copy(gp, d).start()
                own_last(gp).start()

            each(0, 3, send_last)
        if c >= 1:
            inverse_step(c - 1)

    def rows_sent(g):
        for d in OTHERS:
            rows_copy(g, d).wait_send()

    each(0, 5, rows_sent)
    for d in OTHERS:
        tail_copy(d).wait_send()

    stores = []
    for gp in range(3):
        own_last(gp).wait()
        for d in OTHERS:
            last_copy(gp, d).wait()
        inverse(3, gp)
        emit(gp, v["acc_u"], v["updated"])
        count = min(16, JD - 16 * gp)
        part = pl.ds(jnp.where(lat >= 8, JD - 16 * gp - count, 16 * gp), count)
        stores.append(
            pltpu.make_async_copy(v["updated"].at[part], o_any.at[part], v["store"].at[gp])
        )
        stores[gp].start()
    for store in stores:
        store.wait()


def on_device(grid, norm_gain, mlp_in, mlp_out, filter_weight):
    updated = pl.pallas_call(
        block_kernel,
        out_shape=jax.ShapeDtypeStruct((JD, 16, NLON), BF16),
        in_specs=[ANY, VM, VM, VM, ANY],
        out_specs=ANY,
        scratch_shapes=list(SCRATCH.values()),
        cost_estimate=pl.CostEstimate(
            flops=20_000_000_000, bytes_accessed=10_000_000, transcendentals=0
        ),
        compiler_params=pltpu.CompilerParams(
            collective_id=1, has_side_effects=True, vmem_limit_bytes=LIMIT
        ),
    )(grid.transpose(1, 2, 0), norm_gain.reshape(1, CH), mlp_in, mlp_out, filter_weight)
    return updated.transpose(1, 0, 2)


def solution(mesh):
    return jax.shard_map(
        on_device,
        mesh=mesh,
        in_specs=(P("batch", "lat", "lon"), P(), P(), P(), P(("lat", "lon"), None, None)),
        out_specs=P(("batch", "lon"), "lat", None),
        check_vma=False,
    )
```
